32 devices in a mesh: wide: 8 (over z, x), narrow: 4 (over y, core).
Axes of the slice: x: 2, y: 2, z: 4, core: 2. Of those that a mesh axis runs over, the one named last changes fastest.
Arguments:
- pixels: bfloat16 [8, 1568, 1536], P('wide'), may hold values from -24 to 24
- visible: int32 [16, 156], P('wide'), may hold values from 0 to 1567, as said below
- masked: int32 [16, 1412], P('wide'), may hold values from 0 to 1567
- groups: int32 [1536], replicated, may hold values from 0 to 2, as said below
- enc_qkv: float32 [3, 768, 768], P(None, None, ('narrow', 'wide')), may hold values from -0.21875 to 0.21875
- enc_qkv_mom: float32 [3, 768, 768], P(None, None, ('narrow', 'wide')), may hold values from -8.940697e-08 to 8.940697e-08
- enc_out: float32 [768, 768], P(('narrow', 'wide')), may hold values from -0.4375 to 0.4375
- enc_out_mom: float32 [768, 768], P(('narrow', 'wide')), may hold values from -8.940697e-08 to 8.940697e-08
- enc_up: float32 [768, 3072], P(None, ('narrow', 'wide')), may hold values from -0.21875 to 0.21875
- enc_up_mom: float32 [768, 3072], P(None, ('narrow', 'wide')), may hold values from -1.8626451e-08 to 1.8626451e-08
- enc_down: float32 [3072, 768], P(('narrow', 'wide')), may hold values from -0.109375 to 0.109375
- enc_down_mom: float32 [3072, 768], P(('narrow', 'wide')), may hold values from -8.940697e-08 to 8.940697e-08
- dec_qkv: float32 [384, 1152], P(None, ('wide', 'narrow')), may hold values from -0.3125 to 0.3125
- dec_qkv_mom: float32 [384, 1152], P(None, ('wide', 'narrow')), may hold values from -3.5762787e-07 to 3.5762787e-07
- dec_out: float32 [384, 384], P(('wide', 'narrow')), may hold values from -0.625 to 0.625
- dec_out_mom: float32 [384, 384], P(('wide', 'narrow')), may hold values from -3.5762787e-07 to 3.5762787e-07
- dec_up: float32 [384, 1536], P(None, ('wide', 'narrow')), may hold values from -0.3125 to 0.3125
- dec_up_mom: float32 [384, 1536], P(None, ('wide', 'narrow')), may hold values from -3.5762787e-07 to 3.5762787e-07
- dec_down: float32 [1536, 384], P(('wide', 'narrow')), may hold values from -0.15625 to 0.15625
- dec_down_mom: float32 [1536, 384], P(('wide', 'narrow')), may hold values from -3.5762787e-07 to 3.5762787e-07
- embed: float32 [1536, 768], P('wide'), may hold values from -0.15625 to 0.15625
- embed_m: float32 [1536, 768], P('wide'), may hold values from -5.820766e-10 to 5.820766e-10
- embed_v: float32 [1536, 768], P('wide'), may hold values from 3.4e-20 to 1.35e-19
- enc_to_dec: float32 [768, 384], P('wide'), may hold values from -0.21875 to 0.21875
- enc_to_dec_m: float32 [768, 384], P('wide'), may hold values from -3.7252903e-08 to 3.7252903e-08
- enc_to_dec_v: float32 [768, 384], P('wide'), may hold values from 1.8e-16 to 7.3e-16
- head: float32 [384, 1536], P(('wide', 'narrow')), may hold values from -0.078125 to 0.078125
- head_m: float32 [384, 1536], P(('wide', 'narrow')), may hold values from -3.7252903e-08 to 3.7252903e-08
- head_v: float32 [384, 1536], P(('wide', 'narrow')), may hold values from 1.8e-16 to 7.3e-16
- vectors: float32 [19200], replicated, may hold values from -1.2 to 1.6
- vectors_m: float32 [19200], replicated, may hold values from -4.172325e-07 to 4.172325e-07
- vectors_v: float32 [19200], replicated, may hold values from 1.8e-14 to 7.3e-14
Outputs:
- loss_sum: float32 [], replicated
- grad_norm: float32 [], replicated
- enc_qkv_new: float32 [3, 768, 768], P(None, None, ('narrow', 'wide'))
- enc_qkv_mom_new: float32 [3, 768, 768], P(None, None, ('narrow', 'wide'))
- enc_out_new: float32 [768, 768], P(('narrow', 'wide'))
- enc_out_mom_new: float32 [768, 768], P(('narrow', 'wide'))
- enc_up_new: float32 [768, 3072], P(None, ('narrow', 'wide'))
- enc_up_mom_new: float32 [768, 3072], P(None, ('narrow', 'wide'))
- enc_down_new: float32 [3072, 768], P(('narrow', 'wide'))
- enc_down_mom_new: float32 [3072, 768], P(('narrow', 'wide'))
- dec_qkv_new: float32 [384, 1152], P(None, ('wide', 'narrow'))
- dec_qkv_mom_new: float32 [384, 1152], P(None, ('wide', 'narrow'))
- dec_out_new: float32 [384, 384], P(('wide', 'narrow'))
- dec_out_mom_new: float32 [384, 384], P(('wide', 'narrow'))
- dec_up_new: float32 [384, 1536], P(None, ('wide', 'narrow'))
- dec_up_mom_new: float32 [384, 1536], P(None, ('wide', 'narrow'))
- dec_down_new: float32 [1536, 384], P(('wide', 'narrow'))
- dec_down_mom_new: float32 [1536, 384], P(('wide', 'narrow'))
- embed_m_new: float32 [1536, 768], P('wide')
- embed_v_new: float32 [1536, 768], P('wide')
- embed_new: float32 [1536, 768], P('wide')
- enc_to_dec_m_new: float32 [768, 384], P('wide')
- enc_to_dec_v_new: float32 [768, 384], P('wide')
- enc_to_dec_new: float32 [768, 384], P('wide')
- head_m_new: float32 [384, 1536], P(('wide', 'narrow'))
- head_v_new: float32 [384, 1536], P(('wide', 'narrow'))
- head_new: float32 [384, 1536], P(('wide', 'narrow'))
- vectors_m_new: float32 [19200], replicated
- vectors_v_new: float32 [19200], replicated
- vectors_new: float32 [19200], replicated
The draws below stay inside these ranges and needn't reach their ends.
Inputs may be any that keep to these rules, and one draw needn't show every extreme that they name: For each clip, visible and masked together hold each of 0 to 1567 exactly once. `groups`: each group holds exactly 512 of the values.
All inputs are finite; a program needn't handle non-finite values.
Results may differ from the reference program's by a relative error of at most 0.0095.
Values may be sent and summed in bfloat16 or wider, within the bound.
No kernel may reach another device: no remote copies, remote signals or barrier semaphores. Data moves between devices by JAX's collectives and lax.ppermute only.
A program may use at most 320 MiB of HBM per device.

```python
import math
import jax
import jax.numpy as jnp
from jax import lax

D = 768
HEADS = 12
HD = 64
FE = 3072
DD = 384
DHEADS = 6
FD = 1536
PIX = 1536
TUB = 1568
VIS = 156
GROUPS = 3
NS_STEPS = 5
STEP = 10
MSK = 1412
VIDEOS = 8
CLIPS = 16
NV = 19200


def clip_orders(key):
    clip_keys = jax.random.split(key, CLIPS)
    return jax.vmap(lambda one_key: jax.random.permutation(one_key, TUB))(clip_keys).astype(jnp.int32)


def draw_visible(key, part):
    return clip_orders(key)[:, :VIS]


def draw_masked(key, part):
    return clip_orders(key)[:, VIS:]


def draw_groups(key, part):
    key = jax.random.fold_in(key, 5)
    return (jax.random.permutation(key, PIX) % GROUPS).astype(jnp.int32)


def pixel_scales(low_exp):
    video_pos = jnp.arange(VIDEOS, dtype=jnp.float32) / max(VIDEOS - 1, 1)
    tube_pos = jnp.arange(TUB, dtype=jnp.float32) / max(TUB - 1, 1)
    rise = 0.6 * video_pos[:, None] + 0.4 * tube_pos[None, :]
    return (10.0 ** (low_exp + rise))[:, :, None]


def draw_pixels(key, part):
    key = jax.random.fold_in(key, 13)
    base = jnp.clip(jax.random.normal(key, (VIDEOS, TUB, PIX), jnp.float32), -6.0, 6.0)
    scales = pixel_scales(-0.5)
    return (base * scales).astype(jnp.bfloat16)


def draw_vectors(key, part):
    key = jax.random.fold_in(key, 9)
    entries = [('enc_ln1_g', D), ('enc_ln1_b', D), ('enc_q_b', D), ('enc_v_b', D), ('enc_out_b', D), ('enc_ln2_g', D), ('enc_ln2_b', D), ('enc_up_b', FE), ('enc_down_b', D), ('enc_lnf_g', D), ('enc_lnf_b', D), ('enc_emb_b', D), ('dec_in_b', DD), ('dec_mask', DD), ('dec_ln1_g', DD), ('dec_ln1_b', DD), ('dec_q_b', DD), ('dec_v_b', DD), ('dec_out_b', DD), ('dec_ln2_g', DD), ('dec_ln2_b', DD), ('dec_up_b', FD), ('dec_down_b', DD), ('dec_lnf_g', DD), ('dec_lnf_b', DD), ('dec_head_b', PIX)]
    gain_mask = jnp.concatenate([jnp.full((extent,), 1.0 if entry_name[-2:] == '_g' else 0.0, jnp.float32) for entry_name, extent in entries])
    base = jnp.clip(jax.random.normal(key, (NV,), jnp.float32), -4.0, 4.0)
    return jnp.where(gain_mask > 0.5, 1.0 + 0.15 * base, 0.3 * base)


def shard_levels(own_key, shape, cuts, least, top_value):
    level, own = 1.0, jax.random.fold_in(own_key, 6)
    for dim, parts in cuts:
        heights = jnp.exp(jax.random.uniform(jax.random.fold_in(own, dim), (parts,), jnp.float32, least / len(cuts), top_value / len(cuts)))
        level = level * jnp.repeat(heights, shape[dim] // parts).reshape([-1 if axis == dim else 1 for axis in range(len(shape))])
    return level


def bell_draw(rng, dims, width, limit, shards=(), kind=jnp.bfloat16):
    gain = shard_levels(rng, dims, shards, -0.22, 0.18) if shards else 1.0
    values = jax.random.normal(rng, dims, jnp.float32) * width * gain
    return jnp.minimum(jnp.maximum(values, -limit), limit).astype(kind)


def setup_inputs(seed: int = 0) -> dict:
    key_list = jax.random.split(jax.random.key(seed), 33)
    return {
        "pixels": draw_pixels(jax.random.fold_in(key_list[32], 71), 0),
        "visible": draw_visible(jax.random.fold_in(key_list[32], 71), 0),
        "masked": draw_masked(jax.random.fold_in(key_list[32], 71), 0),
        "groups": draw_groups(jax.random.fold_in(key_list[32], 71), 0),
        "enc_qkv": bell_draw(key_list[4], (3, D, D), D ** -0.5, 0.21875, ((2, 32),), jnp.float32),
        "enc_qkv_mom": bell_draw(key_list[5], (3, D, D), 0.000000015, 8.940696716308594e-08, ((2, 32),), jnp.float32),
        "enc_out": bell_draw(key_list[6], (D, D), (D // 4) ** -0.5, 0.4375, ((0, 32),), jnp.float32),
        "enc_out_mom": bell_draw(key_list[7], (D, D), 0.000000015, 8.940696716308594e-08, ((0, 32),), jnp.float32),
        "enc_up": bell_draw(key_list[8], (D, FE), D ** -0.5, 0.21875, ((1, 32),), jnp.float32),
        "enc_up_mom": bell_draw(key_list[9], (D, FE), 0.000000003, 1.862645149230957e-08, ((1, 32),), jnp.float32),
        "enc_down": bell_draw(key_list[10], (FE, D), FE ** -0.5, 0.109375, ((0, 32),), jnp.float32),
        "enc_down_mom": bell_draw(key_list[11], (FE, D), 0.000000015, 8.940696716308594e-08, ((0, 32),), jnp.float32),
        "dec_qkv": bell_draw(key_list[12], (DD, 3 * DD), DD ** -0.5, 0.3125, ((1, 32),), jnp.float32),
        "dec_qkv_mom": bell_draw(key_list[13], (DD, 3 * DD), 0.00000006, 3.5762786865234375e-07, ((1, 32),), jnp.float32),
        "dec_out": bell_draw(key_list[14], (DD, DD), (DD // 4) ** -0.5, 0.625, ((0, 32),), jnp.float32),
        "dec_out_mom": bell_draw(key_list[15], (DD, DD), 0.00000006, 3.5762786865234375e-07, ((0, 32),), jnp.float32),
        "dec_up": bell_draw(key_list[16], (DD, FD), DD ** -0.5, 0.3125, ((1, 32),), jnp.float32),
        "dec_up_mom": bell_draw(key_list[17], (DD, FD), 0.00000006, 3.5762786865234375e-07, ((1, 32),), jnp.float32),
        "dec_down": bell_draw(key_list[18], (FD, DD), FD ** -0.5, 0.15625, ((0, 32),), jnp.float32),
        "dec_down_mom": bell_draw(key_list[19], (FD, DD), 0.00000006, 3.5762786865234375e-07, ((0, 32),), jnp.float32),
        "embed": bell_draw(key_list[20], (PIX, D), PIX ** -0.5, 0.15625, ((0, 8),), jnp.float32),
        "embed_m": bell_draw(key_list[21], (PIX, D), 0.00000000009, 5.820766091346741e-10, ((0, 8),), jnp.float32),
        "embed_v": jnp.clip(jnp.exp(math.log(1.349999989470198e-19) - 1.37891428 * jax.random.uniform(key_list[22], (PIX, D), jnp.float32) ** shard_levels(key_list[22], (PIX, D), ((0, 8),), -0.2, 0.2)), 3.3999998921027766e-20, 1.349999989470198e-19),
        "enc_to_dec": bell_draw(key_list[23], (D, DD), D ** -0.5, 0.21875, ((0, 8),), jnp.float32),
        "enc_to_dec_m": bell_draw(key_list[24], (D, DD), 0.0000000066, 3.725290298461914e-08, ((0, 8),), jnp.float32),
        "enc_to_dec_v": jnp.clip(jnp.exp(math.log(7.299999931189498e-16) - 1.4000877 * jax.random.uniform(key_list[25], (D, DD), jnp.float32) ** shard_levels(key_list[25], (D, DD), ((0, 8),), -0.2, 0.2)), 1.7999999377080617e-16, 7.299999931189498e-16),
        "head": bell_draw(key_list[26], (DD, PIX), (16 * DD) ** -0.5, 0.078125, ((0, 32),), jnp.float32),
        "head_m": bell_draw(key_list[27], (DD, PIX), 0.0000000066, 3.725290298461914e-08, ((0, 32),), jnp.float32),
        "head_v": jnp.clip(jnp.exp(math.log(7.299999931189498e-16) - 1.4000877 * jax.random.uniform(key_list[28], (DD, PIX), jnp.float32) ** shard_levels(key_list[28], (DD, PIX), ((0, 32),), -0.2, 0.2)), 1.7999999377080617e-16, 7.299999931189498e-16),
        "vectors": draw_vectors(jax.random.fold_in(key_list[32], 71), 0),
        "vectors_m": bell_draw(key_list[30], (NV,), 0.000000066, 4.172325134277344e-07, (), jnp.float32),
        "vectors_v": jnp.clip(jnp.exp(jax.random.uniform(key_list[31], (NV,), jnp.float32, math.log(1.8000000700569598e-14), math.log(7.300000312354324e-14))), 1.8000000700569598e-14, 7.300000312354324e-14),
    }


@jax.custom_vjp
def low(v):
    return lax.optimization_barrier(v.astype(jnp.bfloat16)).astype(jnp.float32)

@jax.custom_vjp
def low_back(v):
    return v

def low_keep(v):
    return (low(v), None)

def low_pass(kept, grad):
    return (grad,)

def back_keep(v):
    return (v, None)

def back_low(kept, grad):
    return (low(grad),)
low.defvjp(low_keep, low_pass)
low_back.defvjp(back_keep, back_low)
EPS_NORM = 1e-06
TARGET_EPS = 1.0
CLIP_AT = 0.0002
MOMENTUM = 0.95
RATE_MUON = 0.15
RATE_ADAM = 0.02
RATE_VECTOR = 0.2
DECAY = 0.05
BETA_ONE = 0.9
BETA_TWO = 0.95
EPS_ADAM = 1e-12
NS_A = 3.4445
NS_B = -4.775
NS_C = 2.0315
ROOT_HALF = 0.7071067811865476
HIGH = lax.Precision.HIGHEST

def vector_layout():
    entries = [('enc_ln1_g', D), ('enc_ln1_b', D), ('enc_q_b', D), ('enc_v_b', D), ('enc_out_b', D), ('enc_ln2_g', D), ('enc_ln2_b', D), ('enc_up_b', FE), ('enc_down_b', D), ('enc_lnf_g', D), ('enc_lnf_b', D), ('enc_emb_b', D), ('dec_in_b', DD), ('dec_mask', DD), ('dec_ln1_g', DD), ('dec_ln1_b', DD), ('dec_q_b', DD), ('dec_v_b', DD), ('dec_out_b', DD), ('dec_ln2_g', DD), ('dec_ln2_b', DD), ('dec_up_b', FD), ('dec_down_b', DD), ('dec_lnf_g', DD), ('dec_lnf_b', DD), ('dec_head_b', PIX)]
    layout_map = {}
    offset = 0
    for entry_name, extent in entries:
        layout_map[entry_name] = (offset, extent)
        offset = offset + extent
    return layout_map

def sinusoid(positions, extent):
    half_extent = extent // 2
    frequency = jnp.exp(jnp.arange(half_extent, dtype=jnp.float32) * (-2.0 * math.log(10000.0) / extent))
    angles = positions.astype(jnp.float32)[:, None] * frequency[None, :]
    return jnp.concatenate([jnp.sin(angles), jnp.cos(angles)], axis=1)

def matmul_hi(left, right):
    return jnp.dot(left, right, precision=HIGH)

def layer_norm(layer_in, gain_vec, bias_vec):
    center = layer_in - lax.optimization_barrier(jnp.mean(layer_in, -1, keepdims=True))
    return center * lax.rsqrt(lax.optimization_barrier(jnp.mean(center * center, -1, keepdims=True)) + EPS_NORM) * gain_vec + bias_vec

def gelu_value(upper):
    return 0.5 * upper * (1.0 + lax.erf(upper * ROOT_HALF))

def round_both(value):
    return low(low_back(value))

def group_targets(pix_all, groups):
    onehot = (groups[:, None] == jnp.arange(GROUPS, dtype=jnp.int32)[None, :]).astype(jnp.float32)
    per_group = PIX // GROUPS
    group_mean = jnp.dot(pix_all, onehot, precision=HIGH) / per_group
    center = pix_all - jnp.dot(group_mean, onehot.T, precision=HIGH)
    deviation = jnp.dot(center * center, onehot, precision=HIGH) / per_group
    return center * jnp.dot(lax.rsqrt(deviation + TARGET_EPS), onehot.T, precision=HIGH)

def attend(queries, keys, values, head_count):
    query_h = queries.reshape(queries.shape[0], head_count, HD)
    key_h = keys.reshape(keys.shape[0], head_count, HD)
    value_h = values.reshape(values.shape[0], head_count, HD)
    scores = low_back(jnp.einsum('qhd,khd->hqk', query_h, key_h, precision=HIGH) * HD ** (-0.5))
    exp_scores = jnp.exp(scores - lax.optimization_barrier(jnp.max(scores, -1, keepdims=True)))
    probability = low(exp_scores / lax.optimization_barrier(jnp.sum(exp_scores, -1, keepdims=True)))
    mixed = jnp.einsum('hqk,khd->qhd', probability, value_h, precision=HIGH)
    return mixed.reshape(queries.shape[0], head_count * HD)

def transformer_block(stream, weights, vector_set, block_kind, head_count):
    prefix = block_kind + '_'
    w_qkv = weights[prefix + 'qkv']
    hidden1 = low(layer_norm(stream, vector_set[prefix + 'ln1_g'], vector_set[prefix + 'ln1_b']))
    queries = round_both(matmul_hi(hidden1, w_qkv[0]) + vector_set[prefix + 'q_b'])
    keys = round_both(matmul_hi(hidden1, w_qkv[1]))
    values = round_both(matmul_hi(hidden1, w_qkv[2]) + vector_set[prefix + 'v_b'])
    mixed = round_both(attend(queries, keys, values, head_count))
    middle = stream + low_back(matmul_hi(mixed, weights[prefix + 'out'])) + vector_set[prefix + 'out_b']
    hidden2 = low(layer_norm(middle, vector_set[prefix + 'ln2_g'], vector_set[prefix + 'ln2_b']))
    upper = low_back(matmul_hi(hidden2, weights[prefix + 'up']) + vector_set[prefix + 'up_b'])
    active = low(gelu_value(upper))
    return middle + low_back(matmul_hi(active, weights[prefix + 'down'])) + vector_set[prefix + 'down_b']

def clip_loss(weights, vector_set, pix_rows, target_rows, vis_index, mask_index):
    visible_pix = pix_rows[vis_index]
    stream = low_back(matmul_hi(visible_pix, weights['embed'])) + vector_set['enc_emb_b'] + sinusoid(vis_index, D)
    stream = transformer_block(stream, weights, vector_set, 'enc', HEADS)
    final = low(layer_norm(stream, vector_set['enc_lnf_g'], vector_set['enc_lnf_b']))
    latent = low_back(matmul_hi(final, weights['enc_to_dec'])) + vector_set['dec_in_b']
    tokens_in = jnp.concatenate([latent + sinusoid(vis_index, DD), vector_set['dec_mask'][None, :] + sinusoid(mask_index, DD)], 0)
    tokens_out = transformer_block(tokens_in, weights, vector_set, 'dec', DHEADS)
    head_in = low(layer_norm(tokens_out[VIS:], vector_set['dec_lnf_g'], vector_set['dec_lnf_b']))
    predicted = low_back(matmul_hi(head_in, weights['head'])) + vector_set['dec_head_b']
    error = predicted - target_rows[mask_index]
    return jnp.sum(error * error)

def total_loss(params, pix_all, targets, visible, masked):
    weights = {}
    for entry_name in ['enc_qkv', 'enc_out', 'enc_up', 'enc_down', 'dec_out', 'dec_up', 'dec_down', 'embed', 'enc_to_dec', 'head']:
        weights[entry_name] = low(params[entry_name])
    weights['dec_qkv'] = low(params['dec_qkv'].reshape(DD, 3, DD).transpose(1, 0, 2))
    vector_set = {}
    for entry_name, (offset, extent) in vector_layout().items():
        vector_set[entry_name] = params['vectors'][offset:offset + extent]

    def one_clip(clip_index):
        video_index = clip_index // 2
        return clip_loss(weights, vector_set, pix_all[video_index], targets[video_index], visible[clip_index], masked[clip_index])
    checked = jax.checkpoint(one_clip)

    def scan_step(running, clip_index):
        return (running + checked(clip_index), None)
    loss_total, _ = lax.scan(scan_step, jnp.zeros((), jnp.float32), jnp.arange(CLIPS, dtype=jnp.int32))
    return loss_total

def orthogonalize(matrix):
    tall = matrix.shape[0] > matrix.shape[1]
    work = matrix.T if tall else matrix
    work = work / (jnp.sqrt(jnp.sum(work * work)) + 1e-07)
    for _ in range(NS_STEPS):
        gram_mat = matmul_hi(work, work.T)
        work = NS_A * work + matmul_hi(NS_B * gram_mat + NS_C * matmul_hi(gram_mat, gram_mat), work)
    return work.T if tall else work

def muon_update(weight, momentum_old, gradient):
    momentum_new = MOMENTUM * momentum_old + gradient
    if weight.ndim == 3:
        extent = weight.shape[2]
        flat = jnp.concatenate([momentum_new[0], momentum_new[1], momentum_new[2]], 1)
        ortho_flat = orthogonalize(flat)
        ortho = jnp.stack([ortho_flat[:, :extent], ortho_flat[:, extent:2 * extent], ortho_flat[:, 2 * extent:]])
        largest = 3 * extent
    else:
        ortho = orthogonalize(momentum_new)
        largest = max(weight.shape[0], weight.shape[1])
    new_weight = weight * (1.0 - RATE_MUON * DECAY) - RATE_MUON * 0.2 * math.sqrt(largest) * ortho
    return (new_weight, momentum_new)

def adam_update(weight, first, second, gradient, rate, decay):
    first_new = BETA_ONE * first + (1.0 - BETA_ONE) * gradient
    second_new = BETA_TWO * second + (1.0 - BETA_TWO) * gradient * gradient
    direction = first_new / (1.0 - BETA_ONE ** STEP) / (jnp.sqrt(second_new / (1.0 - BETA_TWO ** STEP)) + EPS_ADAM)
    return (first_new, second_new, weight - rate * (direction + decay * weight))

def reference(pixels, visible, masked, groups, enc_qkv, enc_qkv_mom, enc_out, enc_out_mom, enc_up, enc_up_mom, enc_down, enc_down_mom, dec_qkv, dec_qkv_mom, dec_out, dec_out_mom, dec_up, dec_up_mom, dec_down, dec_down_mom, embed, embed_m, embed_v, enc_to_dec, enc_to_dec_m, enc_to_dec_v, head, head_m, head_v, vectors, vectors_m, vectors_v):
    params = {'enc_qkv': enc_qkv, 'enc_out': enc_out, 'enc_up': enc_up, 'enc_down': enc_down, 'dec_qkv': dec_qkv, 'dec_out': dec_out, 'dec_up': dec_up, 'dec_down': dec_down, 'embed': embed, 'enc_to_dec': enc_to_dec, 'head': head, 'vectors': vectors}
    pix_all = pixels.astype(jnp.float32)
    targets = group_targets(pix_all, groups)
    denominator = CLIPS * MSK * PIX
    loss_sum, pullback = jax.vjp(lambda chosen: total_loss(chosen, pix_all, targets, visible, masked), params)
    gradients = pullback(jnp.asarray(1.0 / denominator, jnp.float32))[0]
    squares = sum((jnp.sum(piece * piece) for piece in gradients.values()))
    grad_norm = jnp.sqrt(squares)
    factor = jnp.minimum(1.0, CLIP_AT / grad_norm)
    clipped = {key_name: factor * value for key_name, value in gradients.items()}
    results = [loss_sum, grad_norm]
    for key_name, momentum_old in [('enc_qkv', enc_qkv_mom), ('enc_out', enc_out_mom), ('enc_up', enc_up_mom), ('enc_down', enc_down_mom), ('dec_qkv', dec_qkv_mom), ('dec_out', dec_out_mom), ('dec_up', dec_up_mom), ('dec_down', dec_down_mom)]:
        new_weight, momentum_new = muon_update(params[key_name], momentum_old, clipped[key_name])
        results = results + [new_weight, momentum_new]
    for key_name, first, second, rate, decay in [('embed', embed_m, embed_v, RATE_ADAM, DECAY), ('enc_to_dec', enc_to_dec_m, enc_to_dec_v, RATE_ADAM, DECAY), ('head', head_m, head_v, RATE_ADAM, DECAY), ('vectors', vectors_m, vectors_v, RATE_VECTOR, 0.0)]:
        first_new, second_new, new_weight = adam_update(params[key_name], first, second, clipped[key_name], rate, decay)
        results = results + [first_new, second_new, new_weight]
    return tuple(results)
```

```python
import math

import jax
import jax.numpy as jnp
import numpy as np
from jax import lax
from jax.sharding import PartitionSpec as P

WD = "wide"
NR = "narrow"
D = 768
HD = 64
FE = 3072
DD = 384
FD = 1536
PIX = 1536
GROUPS = 3
NS_STEPS = 5
STEP = 10
QN = 4

EPS_NORM = 1e-06
TARGET_EPS = 1.0
CLIP_AT = 0.0002
MOMENTUM = 0.95
RATE_MUON = 0.15
RATE_ADAM = 0.02
RATE_VECTOR = 0.2
DECAY = 0.05
BETA_ONE = 0.9
BETA_TWO = 0.95
EPS_ADAM = 1e-12
NS_A = 3.4445
NS_B = -4.775
NS_C = 2.0315
ROOT_HALF = 0.7071067811865476
INV_ROOT_TWO_PI = 0.3989422804014327
HIGHEST = lax.Precision.HIGHEST
HIGH = lax.Precision.HIGH
BF = jnp.bfloat16
F32 = jnp.float32

BLOCK = "ln1_g ln1_b q_b v_b out_b ln2_g ln2_b up_b down_b"
BLOCK = ("ln1_g", "ln1_b", "q_b", "v_b", "out_b", "ln2_g", "ln2_b", "up_b", "down_b")


def vector_layout():
    entries = []
    for side, width, hidden in (("e", D, FE), ("d", DD, FD)):
        if side == "d":
            entries += [("in_b", DD), ("mask", DD)]
        entries += [(side + name, hidden if name == "up_b" else width) for name in BLOCK]
        entries += [(side + "lnf_g", width), (side + "lnf_b", width)]
        if side == "e":
            entries += [("emb_b", D)]
    entries += [("head_b", PIX)]
    table, offset = {}, 0
    for name, extent in entries:
        table[name] = (offset, extent)
        offset += extent
    return table


def wide_digits(count):
    digits, rest, step = [], count, 1
    while rest > 1:
        radix = 2 if not digits or rest % 4 else 4
        digits.append((step, radix))
        step, rest = step * radix, rest // radix
    return digits


def shift_pairs(count, digit, delta, keep=None):
    step, radix = digit
    pairs = []
    for src in range(count):
        place = src // step % radix
        if 0 <= place + delta < radix and (keep is None or keep(place)):
            pairs.append((src, src + delta * step))
    return pairs


def wide_move(value, digit, delta, keep=None):
    return lax.ppermute(value, WD, shift_pairs(lax.axis_size(WD), digit, delta, keep))


def wide_flip(value, bit):
    count = lax.axis_size(WD)
    return lax.ppermute(value, WD, [(src, src ^ bit) for src in range(count)])


def narrow_flip(value, bit):
    return lax.ppermute(value, NR, [(src, src ^ bit) for src in range(QN)])


def place_in(digit):
    return lax.axis_index(WD) // digit[0] % digit[1]


def pick_half(value, which, axis):
    return lax.dynamic_index_in_dim(value, which, axis, keepdims=False)


def both(mine, theirs, place, axis):
    first = jnp.where(place == 0, mine, theirs)
    second = jnp.where(place == 0, theirs, mine)
    return jnp.stack([first, second], axis)


def line_gather(block, digit, axis):
    radix = digit[1]
    place = place_in(digit)
    if radix == 2:
        return both(block, wide_flip(block, digit[0]), place, axis)
    right, left = [block], [block]
    for hop in range(1, radix):
        right.append(wide_move(right[-1], digit, 1, lambda p, h=hop: p >= h - 1))
        left.append(wide_move(left[-1], digit, -1, lambda p, h=hop: p <= radix - h))
    row = jnp.stack(right[:0:-1] + left, axis)
    return lax.dynamic_slice_in_dim(row, radix - 1 - place, radix, axis)


def wide_gather(block):
    digits = wide_digits(lax.axis_size(WD))
    value = block
    for axis, digit in enumerate(digits[::-1]):
        value = line_gather(value, digit, axis)
    return value.reshape((-1,) + block.shape)


def narrow_gather(block):
    place = lax.axis_index(NR)
    value = both(block, narrow_flip(block, 2), place // 2, 0)
    value = both(value, narrow_flip(value, 1), place % 2, 1)
    return value.reshape((QN,) + block.shape)


def line_scatter(value, digit, axis):
    radix = digit[1]
    place = place_in(digit)
    if radix == 2:
        sent = pick_half(value, 1 - place, axis).astype(BF)
        return pick_half(value, place, axis).astype(F32) + wide_flip(sent, digit[0]).astype(F32)
    total = pick_half(value, place, axis).astype(F32)
    for sign in (1, -1):
        carried = None
        for hop in range(radix - 1, 0, -1):
            target = jnp.clip(place + sign * hop, 0, radix - 1)
            part = pick_half(value, target, axis).astype(F32)
            if carried is not None:
                part = part + carried
            moved = wide_move(
                part.astype(BF), digit, sign, lambda p, h=hop, s=sign: 0 <= p + s * h < radix
            )
            carried = moved.astype(F32)
        total = total + carried
    return total


def slow_exchange(value, digit):
    place = place_in(digit)
    radix = digit[1]
    got = [pick_half(value, place, 0)]
    for mask in range(1, radix):
        got.append(wide_flip(pick_half(value, place ^ mask, 0), mask * digit[0]))
    stacked = jnp.stack(got, 0)
    return jnp.stack([pick_half(stacked, place ^ src, 0) for src in range(radix)], 0)


def pair_sum(value):
    return value + narrow_flip(value, 1)


def sum_all(value):
    value = pair_sum(value)
    value = value + narrow_flip(value, 2)
    bit = 1
    while bit < lax.axis_size(WD):
        value = value + wide_flip(value, bit)
        bit *= 2
    return value


def narrow_total(value):
    place = lax.axis_index(NR) % 2
    cols = value.shape[1] // 2
    low, high = value[:, :cols], value[:, cols:]
    mine = jnp.where(place == 0, low, high)
    other = jnp.where(place == 0, high, low)
    part = (mine + narrow_flip(other, 1)).astype(BF)
    part = part.astype(F32) + narrow_flip(part, 2).astype(F32)
    mate = narrow_flip(part, 1)
    return jnp.concatenate(
        [jnp.where(place == 0, part, mate), jnp.where(place == 0, mate, part)], 1
    )


def sinusoid(positions, extent):
    half_extent = extent // 2
    frequency = jnp.exp(
        jnp.arange(half_extent, dtype=F32) * (-2.0 * math.log(10000.0) / extent)
    )
    angles = positions.astype(F32)[:, None] * frequency[None, :]
    return jnp.concatenate([jnp.sin(angles), jnp.cos(angles)], axis=1)


def low(value):
    return value.astype(BF)


def mm(left, right):
    return jnp.dot(left, right, preferred_element_type=F32)


def mm_tn(left, right):
    return lax.dot_general(left, right, (((0,), (0,)), ((), ())), preferred_element_type=F32)


def mm_nt(left, right):
    return lax.dot_general(left, right, (((1,), (1,)), ((), ())), preferred_element_type=F32)


def col_sum(value):
    return jnp.sum(value, 0)


def layer_norm(value, gain, bias):
    center = value - jnp.mean(value, -1, keepdims=True)
    inv = lax.rsqrt(jnp.mean(center * center, -1, keepdims=True) + EPS_NORM)
    normed = center * inv
    return (normed * gain + bias, (normed, inv))


def norm_back(grad, saved, gain):
    normed, inv = saved
    grad_n = grad * gain
    grad_in = inv * (
        grad_n
        - jnp.mean(grad_n, -1, keepdims=True)
        - normed * jnp.mean(grad_n * normed, -1, keepdims=True)
    )
    return (grad_in, col_sum(grad * normed), col_sum(grad))


def gelu_value(upper):
    return 0.5 * upper * (1.0 + lax.erf(upper * ROOT_HALF))


def gelu_slope(upper):
    return (
        0.5 * (1.0 + lax.erf(upper * ROOT_HALF))
        + upper * jnp.exp(-0.5 * upper * upper) * INV_ROOT_TWO_PI
    )


def group_targets(pix, groups):
    rows = pix.astype(F32)
    masks = [(groups == g).astype(F32)[None, :] for g in range(GROUPS)]
    per_group = pix.shape[-1] // GROUPS

    def spread(parts):
        return sum(part * mask for part, mask in zip(parts, masks))

    means = [jnp.sum(rows * mask, -1, keepdims=True) / per_group for mask in masks]
    center = rows - spread(means)
    squares = center * center
    scale = [
        lax.rsqrt(jnp.sum(squares * mask, -1, keepdims=True) / per_group + TARGET_EPS)
        for mask in masks
    ]
    return center * spread(scale)


def heads_of(value, clips):
    rows, width = value.shape
    return value.reshape(clips, rows // clips, width // HD, HD)


def attention_forward(queries, keys, values):
    scores = (
        jnp.einsum("cqhd,ckhd->chqk", queries, keys, preferred_element_type=F32) * HD**-0.5
    )
    peak = jnp.max(scores, -1, keepdims=True)
    exp_scores = jnp.exp(scores - peak)
    total = jnp.sum(exp_scores, -1, keepdims=True)
    mixed = jnp.einsum(
        "chqk,ckhd->cqhd", low(exp_scores / total), values, preferred_element_type=F32
    )
    return (mixed, peak + jnp.log(total))


def attention_backward(queries, keys, values, log_total, grad_low):
    scores = (
        jnp.einsum("cqhd,ckhd->chqk", queries, keys, preferred_element_type=F32) * HD**-0.5
    )
    prob = jnp.exp(scores - log_total)
    grad_v = jnp.einsum("chqk,cqhd->ckhd", low(prob), grad_low, preferred_element_type=F32)
    grad_p = jnp.einsum("cqhd,ckhd->chqk", grad_low, values, preferred_element_type=F32)
    grad_s = low(prob * (grad_p - jnp.sum(prob * grad_p, -1, keepdims=True)))
    grad_q = (
        jnp.einsum("chqk,ckhd->cqhd", grad_s, keys, preferred_element_type=F32) * HD**-0.5
    )
    grad_k = (
        jnp.einsum("chqk,cqhd->ckhd", grad_s, queries, preferred_element_type=F32) * HD**-0.5
    )
    return (grad_q, grad_k, grad_v)


def gram_of(rows):
    return lax.dot_general(
        rows, rows, (((0,), (0,)), ((), ())), precision=HIGH, preferred_element_type=F32
    )


def pack_symmetric(gram):
    block = gram.shape[0] // 3
    return jnp.concatenate(
        [
            gram[i * block : (i + 1) * block, j * block : (j + 1) * block]
            for i in range(3)
            for j in range(i, 3)
        ],
        0,
    )


def unpack_symmetric(packed):
    block = packed.shape[1]
    tiles = {}
    at = 0
    for i in range(3):
        for j in range(i, 3):
            tile = packed[at : at + block]
            at += block
            tiles[i, j] = tile
            if i != j:
                tiles[j, i] = tile.T
    return jnp.concatenate(
        [jnp.concatenate([tiles[i, j] for j in range(3)], 1) for i in range(3)], 0
    )


def group_total(value):
    place = lax.axis_index(NR) % 2
    parts = value.reshape((2, value.shape[0] // 2) + value.shape[1:])
    mine = pick_half(parts, place, 0) + narrow_flip(pick_half(parts, 1 - place, 0), 1)
    rows = mine.shape[0] // 2
    one, two = mine[:rows], mine[rows:]
    digits = wide_digits(lax.axis_size(WD))
    bits = []
    bit = 1
    while bit < digits[-1][0]:
        bits.append(bit)
        bit *= 2
    for bit in bits:
        one = one + wide_flip(one, bit)
    one = one + narrow_flip(one, 2)
    two = two + narrow_flip(two, 2)
    for bit in bits:
        two = two + wide_flip(two, bit)
    mine = jnp.concatenate([one, two], 0)
    return both(mine, narrow_flip(mine, 1), place, 0).reshape(value.shape)


def hdot(left, right):
    return jnp.dot(left, right, precision=HIGH, preferred_element_type=F32)


def iterate(gram):
    eye = jnp.eye(gram.shape[0], dtype=F32)
    product = None
    for step in range(NS_STEPS):
        poly = NS_A * eye + NS_B * gram + NS_C * hdot(gram, gram)
        product = poly if product is None else hdot(poly, product)
        if step < NS_STEPS - 1:
            gram = hdot(hdot(poly, gram), poly)
    return product


def adam_update(weight, first, second, gradient, rate, decay):
    first_new = BETA_ONE * first + (1.0 - BETA_ONE) * gradient
    second_new = BETA_TWO * second + (1.0 - BETA_TWO) * gradient * gradient
    direction = (
        first_new
        / (1.0 - BETA_ONE**STEP)
        / (jnp.sqrt(second_new / (1.0 - BETA_TWO**STEP)) + EPS_ADAM)
    )
    return (first_new, second_new, weight - rate * (direction + decay * weight))


def pad_rows(value, rows, axis):
    if value.shape[axis] == rows:
        return value
    widths = [(0, 0)] * value.ndim
    widths[axis] = (0, rows - value.shape[axis])
    return jnp.pad(value, widths)


def per_device(
    pixels,
    visible,
    masked,
    groups,
    enc_qkv,
    enc_qkv_mom,
    enc_out,
    enc_out_mom,
    enc_up,
    enc_up_mom,
    enc_down,
    enc_down_mom,
    dec_qkv,
    dec_qkv_mom,
    dec_out,
    dec_out_mom,
    dec_up,
    dec_up_mom,
    dec_down,
    dec_down_mom,
    embed,
    embed_m,
    embed_v,
    enc_to_dec,
    enc_to_dec_m,
    enc_to_dec_v,
    head,
    head_m,
    head_v,
    vectors,
    vectors_m,
    vectors_v,
):
    wide = lax.axis_size(WD)
    me = lax.axis_index(NR)
    half, clip = me % 2, me // 2
    slow = wide_digits(wide)[-1]
    fast = slow[0]
    plane = place_in(slow)
    clips, vis = visible.shape
    tubs = pixels.shape[1]
    own = tubs // 2
    rows = clips * vis

    n_up = enc_up.shape[1]
    n_q = enc_qkv.shape[2]
    n_out = enc_out.shape[0]
    n_emb = embed.shape[0] // QN
    n_link = enc_to_dec.shape[0] * DD // D // QN
    m_up = dec_up.shape[1]
    m_qkv = dec_qkv.shape[1]
    m_out = dec_out.shape[0]
    m_head = head.shape[0] * (PIX // DD)

    up_rows, down_rows = enc_up.T, enc_down
    qkv_rows = jnp.swapaxes(enc_qkv, 1, 2).reshape(3 * n_q, D)
    dqkv_rows, dup_rows = dec_qkv.T, dec_up.T
    head_rows = head.reshape(m_head, DD)
    emb_rows = lax.dynamic_slice_in_dim(embed, me * n_emb, n_emb, 0)
    link_rows = lax.dynamic_slice_in_dim(enc_to_dec.reshape(-1, D), me * n_link, n_link, 0)
    pack_a = low(jnp.concatenate([emb_rows, link_rows], 0))
    pack_b = low(jnp.concatenate([qkv_rows, enc_out], 0))
    pack_c = low(jnp.concatenate([up_rows, down_rows], 0))
    pack_d = low(jnp.concatenate([dup_rows, dqkv_rows, dec_out, dec_down, head_rows], 0))
    full_a = narrow_gather(wide_gather(pack_a))
    embed_w = jnp.swapaxes(full_a[:, :, :n_emb], 0, 1).reshape(PIX, D)
    link_w = jnp.swapaxes(full_a[:, :, n_emb:], 0, 1).reshape(D, DD)
    full_b = wide_gather(pack_b)
    w_qkv = [full_b[:, k * n_q : (k + 1) * n_q].reshape(wide * n_q, D) for k in range(3)]
    w_out = full_b[:, 3 * n_q :].reshape(wide * n_out, D)
    full_c = wide_gather(pack_c)
    w_up = full_c[:, :n_up].reshape(wide * n_up, D)
    w_down = full_c[:, n_up:].reshape(wide * n_up, D)
    full_d = jnp.swapaxes(narrow_gather(wide_gather(pack_d)), 0, 1)
    at, taken = 0, []
    for extent in (m_up, m_qkv, m_out, m_up, m_head):
        taken.append(full_d[:, :, at : at + extent].reshape(wide * QN * extent, DD))
        at += extent
    d_up, d_qkv, d_out, d_down, d_head = taken
    d_head = d_head.reshape(DD, PIX)

    table = vector_layout()

    def vec_of(name):
        offset, extent = table[name]
        return vectors[offset : offset + extent]

    def share_of(name):
        offset, extent = table[name]
        share = extent // QN
        return lax.dynamic_slice_in_dim(vectors, offset + me * share, share)

    grads = {}

    vis_rows = visible.reshape(rows)
    tube_ids = jnp.arange(tubs, dtype=jnp.int32)
    vis_pix = mm(low(vis_rows[:, None] == tube_ids[None, :]), pixels[0]).astype(BF)
    stream = mm(vis_pix, embed_w) + vec_of("emb_b") + sinusoid(vis_rows, D)
    hid1, saved1 = layer_norm(stream, vec_of("eln1_g"), vec_of("eln1_b"))
    hid1 = low(hid1)
    eq = low(mm_nt(hid1, w_qkv[0]) + share_of("eq_b"))
    ek = low(mm_nt(hid1, w_qkv[1]))
    ev = low(mm_nt(hid1, w_qkv[2]) + share_of("ev_b"))
    mixed, elog = attention_forward(heads_of(eq, clips), heads_of(ek, clips), heads_of(ev, clips))
    eattn = low(mixed.reshape(eq.shape))
    middle = stream + narrow_total(mm(eattn, w_out)) + vec_of("eout_b")
    hid2, saved2 = layer_norm(middle, vec_of("eln2_g"), vec_of("eln2_b"))
    hid2 = low(hid2)
    upper = mm_nt(hid2, w_up) + share_of("eup_b")
    active = low(gelu_value(upper))
    enc_result = middle + narrow_total(mm(active, w_down)) + vec_of("edown_b")
    final, fsaved = layer_norm(enc_result, vec_of("elnf_g"), vec_of("elnf_b"))
    final = low(final)

    clip_final = lax.dynamic_slice_in_dim(final, clip * vis, vis, 0)
    latent = mm(clip_final, link_w) + vec_of("in_b")
    clip_vis = pick_half(visible, clip, 0)
    own_pos = half * own + jnp.arange(own, dtype=jnp.int32)
    pick = (own_pos[:, None] == clip_vis[None, :]).astype(F32)
    shown = jnp.sum(pick, -1, keepdims=True)
    hidden_row = 1.0 - shown
    dstream = (
        jnp.dot(pick, latent, precision=HIGHEST)
        + hidden_row * vec_of("mask")
        + sinusoid(own_pos, DD)
    )
    dh1, dsaved1 = layer_norm(dstream, vec_of("dln1_g"), vec_of("dln1_b"))
    dh1 = low(dh1)
    joined = mm_nt(dh1, d_qkv)
    dq = low(joined[:, :DD] + vec_of("dq_b"))
    dkv = low(
        jnp.concatenate([joined[:, DD : 2 * DD], joined[:, 2 * DD :] + vec_of("dv_b")], 1)
    )
    all_kv = both(dkv, narrow_flip(dkv, 1), half, 0).reshape(tubs, 2 * DD)
    dk, dv = all_kv[:, :DD], all_kv[:, DD:]
    mixed, dlog = attention_forward(heads_of(dq, 1), heads_of(dk, 1), heads_of(dv, 1))
    dattn = low(mixed.reshape(dq.shape))
    dmiddle = dstream + mm(dattn, d_out) + vec_of("dout_b")
    dh2, dsaved2 = layer_norm(dmiddle, vec_of("dln2_g"), vec_of("dln2_b"))
    dh2 = low(dh2)
    dupper = mm_nt(dh2, d_up) + vec_of("dup_b")
    dactive = low(gelu_value(dupper))
    dresult = dmiddle + mm(dactive, d_down) + vec_of("ddown_b")
    hf, hsaved = layer_norm(dresult, vec_of("dlnf_g"), vec_of("dlnf_b"))
    hf = low(hf)
    predicted = mm(hf, d_head) + vec_of("head_b")
    own_pix = lax.dynamic_slice_in_dim(pixels[0], half * own, own, 0)
    error = (predicted - group_targets(own_pix, groups)) * hidden_row
    loss_part = jnp.sum(error * error)
    pred_grad = error * (2.0 / (clips * wide * (tubs - vis) * PIX))

    pred_low = low(pred_grad)
    g_head = mm_tn(hf, pred_low)
    grads["head_b"] = col_sum(pred_grad)
    dgrad, grads["dlnf_g"], grads["dlnf_b"] = norm_back(
        mm_nt(pred_low, d_head), hsaved, vec_of("dlnf_g")
    )
    down_low = low(dgrad)
    g_ddown = mm_tn(dactive, down_low)
    grads["ddown_b"] = col_sum(dgrad)
    upper_low = low(mm_nt(down_low, d_down) * gelu_slope(dupper))
    g_dup = mm_tn(upper_low, dh2)
    grads["dup_b"] = col_sum(upper_low.astype(F32))
    mid_grad, grads["dln2_g"], grads["dln2_b"] = norm_back(
        mm(upper_low, d_up), dsaved2, vec_of("dln2_g")
    )
    mid_grad = mid_grad + dgrad
    out_low = low(mid_grad)
    g_dout = mm_tn(dattn, out_low)
    grads["dout_b"] = col_sum(mid_grad)
    attn_grad = low(mm_nt(out_low, d_out))
    gq, gk, gv = attention_backward(
        heads_of(dq, 1), heads_of(dk, 1), heads_of(dv, 1), dlog, heads_of(attn_grad, 1)
    )
    gkv = jnp.concatenate([gk.reshape(2, own, DD), gv.reshape(2, own, DD)], 2)
    gkv = pick_half(gkv, half, 0) + narrow_flip(low(pick_half(gkv, 1 - half, 0)), 1).astype(F32)
    joined_low = jnp.concatenate([low(gq.reshape(own, DD)), low(gkv)], 1)
    sums = col_sum(joined_low.astype(F32))
    grads["dq_b"], grads["dv_b"] = sums[:DD], sums[2 * DD :]
    g_dqkv = mm_tn(joined_low, dh1)
    sgrad, grads["dln1_g"], grads["dln1_b"] = norm_back(
        mm(joined_low, d_qkv), dsaved1, vec_of("dln1_g")
    )
    din_grad = sgrad + mid_grad
    grads["mask"] = jnp.sum(hidden_row * din_grad, 0)
    latent_part = lax.dot_general(
        pick, din_grad, (((0,), (0,)), ((), ())), precision=HIGHEST, preferred_element_type=F32
    )

    def dec_parts(value, extent):
        return low(value).reshape(4, fast, QN, extent, DD)

    cut = m_head - m_qkv if False else m_up - m_qkv
    p_head = dec_parts(g_head.reshape(-1, DD), m_head)
    dec_pack = jnp.stack(
        [
            dec_parts(g_dup, m_up),
            jnp.concatenate([dec_parts(g_dqkv, m_qkv), p_head[:, :, :, :cut]], 3),
            jnp.concatenate([dec_parts(g_dout, m_out), p_head[:, :, :, cut:]], 3),
            dec_parts(g_ddown, m_up),
        ],
        0,
    )
    dec_pack = dec_pack.reshape(4, 4, fast, 2, 2, m_up, DD).transpose(4, 0, 2, 3, 1, 5, 6)
    dec_sum = pick_half(dec_pack, half, 0).astype(F32) + narrow_flip(
        pick_half(dec_pack, 1 - half, 0), 1
    ).astype(F32)

    def fast_scatter(value, axis):
        digits = wide_digits(wide)[:-1]
        shape = value.shape
        value = value.reshape(
            shape[:axis] + tuple(radix for _, radix in digits[::-1]) + shape[axis + 1 :]
        )
        for count, digit in enumerate(digits):
            value = line_scatter(value, digit, axis + len(digits) - 1 - count)
        return value

    dec_sum = line_scatter(fast_scatter(dec_sum, 1), slow, 0)
    dec_sum = pick_half(dec_sum, clip, 0) + narrow_flip(
        low(pick_half(dec_sum, 1 - clip, 0)), 2
    ).astype(F32)

    latent_pair = pair_sum(latent_part)
    latent_grad = both(low(latent_pair), narrow_flip(low(latent_pair), 2), clip, 0)
    latent_low = latent_grad.reshape(rows, DD)
    g_link = mm_tn(final, latent_low)
    grads["in_b"] = col_sum(latent_low.astype(F32))
    egrad, grads["elnf_g"], grads["elnf_b"] = norm_back(
        mm_nt(latent_low, link_w), fsaved, vec_of("elnf_g")
    )
    down_low = low(egrad)
    g_down = mm_tn(active, down_low)
    grads["edown_b"] = col_sum(egrad)
    upper_low = low(mm_nt(down_low, w_down) * gelu_slope(upper))
    g_up = mm_tn(upper_low, hid2)
    grads["eup_b"] = col_sum(upper_low.astype(F32))

    def enc_parts(value, extent):
        return low(value).reshape(4, fast, extent, D).transpose(1, 0, 2, 3)

    sum_up = fast_scatter(enc_parts(g_up, n_up), 0)
    sum_down = fast_scatter(enc_parts(g_down, n_up), 0)
    mid_grad, grads["eln2_g"], grads["eln2_b"] = norm_back(
        narrow_total(mm(upper_low, w_up)), saved2, vec_of("eln2_g")
    )
    mid_grad = mid_grad + egrad
    out_low = low(mid_grad)
    g_out = mm_tn(eattn, out_low)
    grads["eout_b"] = col_sum(mid_grad)
    attn_grad = low(mm_nt(out_low, w_out))
    gq, gk, gv = attention_backward(
        heads_of(eq, clips), heads_of(ek, clips), heads_of(ev, clips), elog, heads_of(attn_grad, clips)
    )
    lows = [low(g.reshape(eq.shape)) for g in (gq, gk, gv)]
    grads["eq_b"] = col_sum(lows[0].astype(F32))
    grads["ev_b"] = col_sum(lows[2].astype(F32))
    g_qkv = [mm_tn(g, hid1) for g in lows]
    hid1_grad = narrow_total(sum(mm(g, w) for g, w in zip(lows, w_qkv)))
    sgrad, grads["eln1_g"], grads["eln1_b"] = norm_back(hid1_grad, saved1, vec_of("eln1_g"))
    stream_grad = sgrad + mid_grad
    g_embed = mm_tn(vis_pix, low(stream_grad))
    grads["emb_b"] = col_sum(stream_grad)
    g_embed = pick_half(g_embed.reshape(wide, QN, n_emb, D), me, 1)
    g_link = pick_half(g_link.reshape(wide, QN, n_link, D), me, 1)
    part_qkv = jnp.concatenate([enc_parts(g, n_q) for g in g_qkv], 2)
    part_rest = jnp.concatenate(
        [enc_parts(g_out, n_out), enc_parts(g_embed, n_emb), enc_parts(g_link, n_link)], 2
    )
    sum_qkv = fast_scatter(pad_rows(part_qkv, n_up, 2), 0)
    sum_rest = fast_scatter(pad_rows(part_rest, n_up, 2), 0)
    enc_sum = line_scatter(jnp.stack([sum_up, sum_qkv, sum_rest, sum_down], 0), slow, 0)

    leading = jnp.where(me == 0, 1.0, 0.0)

    def spread(share):
        full = jnp.zeros((share.shape[0] * QN,), F32)
        return lax.dynamic_update_slice_in_dim(full, share, me * share.shape[0], 0)

    pieces = []
    for name in table:
        if name in ("eq_b", "ev_b", "eup_b"):
            pieces.append(spread(grads[name]))
        elif name[0] == "e" or name == "in_b":
            pieces.append(leading * grads[name])
        else:
            pieces.append(grads[name])
    vec_total = sum_all(jnp.concatenate(pieces + [loss_part[None]]).reshape(1, -1))[0]
    loss_sum = vec_total[-1]
    vec_total = vec_total[:-1]
    squares = jnp.sum(dec_sum * dec_sum) + jnp.sum(enc_sum * enc_sum)
    square_total = sum_all(jnp.broadcast_to(squares, (8, 128)))[0, 0]
    grad_norm = jnp.sqrt(square_total + jnp.sum(vec_total * vec_total))
    factor = jnp.minimum(1.0, CLIP_AT / grad_norm)

    def plane_rows(parts):
        return jnp.stack([pad_rows(low(part), parts[0].shape[0], 0) for part in parts], 0)

    qkv_mom_rows = jnp.swapaxes(enc_qkv_mom, 1, 2).reshape(3 * n_q, D)
    enc_moms = [enc_up_mom.T, qkv_mom_rows, enc_out_mom, enc_down_mom]
    dec_moms = [dec_up_mom.T, dec_qkv_mom.T, dec_out_mom, dec_down_mom]
    enc_mom = slow_exchange(plane_rows(enc_moms), slow)
    dec_mom = slow_exchange(plane_rows(dec_moms), slow)

    def valid(total, counts):
        count = jnp.asarray(counts, jnp.int32)[plane]
        return (jnp.arange(total, dtype=jnp.int32) < count).astype(F32)[None, :, None]

    enc_slab = MOMENTUM * enc_mom.astype(F32) + factor * enc_sum * valid(
        n_up, [n_up, 3 * n_q, n_out, n_up]
    )
    dec_slab = MOMENTUM * dec_mom.astype(F32) + factor * dec_sum * valid(
        m_up, [m_up, m_qkv, m_out, m_up]
    )
    enc_slab = enc_slab.reshape(-1, D)
    dec_slab = dec_slab.reshape(-1, DD)
    enc_packed = pack_symmetric(gram_of(enc_slab))
    dec_packed = pack_symmetric(gram_of(dec_slab))
    width = enc_packed.shape[1]
    packed = group_total(jnp.concatenate([enc_packed, dec_packed.reshape(-1, width)], 0))
    cut_at = enc_packed.shape[0]
    ortho = []
    for slab, gram in (
        (enc_slab, unpack_symmetric(packed[:cut_at])),
        (dec_slab, unpack_symmetric(packed[cut_at:].reshape(dec_packed.shape))),
    ):
        scale = 1.0 / (jnp.sqrt(jnp.trace(gram)) + 1e-07)
        ortho.append(hdot(slab * scale, iterate(gram * (scale * scale))))
    enc_ortho = slow_exchange(low(ortho[0]).reshape(4, n_up, D), slow).astype(F32)
    dec_ortho = slow_exchange(low(ortho[1]).reshape(4, m_up, DD), slow).astype(F32)
    enc_grad = slow_exchange(low(enc_sum), slow).astype(F32) * factor
    dec_grad = slow_exchange(low(dec_sum), slow).astype(F32) * factor

    def turned(value):
        return value.T

    def same(value):
        return value

    def unqkv(value):
        return jnp.swapaxes(value.reshape(3, n_q, D), 1, 2)

    results = [loss_sum, grad_norm]
    for weight, mom, grad, part, side, largest in [
        (enc_qkv, enc_qkv_mom, enc_grad[1, : 3 * n_q], enc_ortho[1, : 3 * n_q], unqkv, 3 * D),
        (enc_out, enc_out_mom, enc_grad[2, :n_out], enc_ortho[2, :n_out], same, D),
        (enc_up, enc_up_mom, enc_grad[0], enc_ortho[0], turned, FE),
        (enc_down, enc_down_mom, enc_grad[3], enc_ortho[3], same, FE),
        (dec_qkv, dec_qkv_mom, dec_grad[1, :m_qkv], dec_ortho[1, :m_qkv], turned, 3 * DD),
        (dec_out, dec_out_mom, dec_grad[2, :m_out], dec_ortho[2, :m_out], same, DD),
        (dec_up, dec_up_mom, dec_grad[0], dec_ortho[0], turned, FD),
        (dec_down, dec_down_mom, dec_grad[3], dec_ortho[3], same, FD),
    ]:
        new_weight = weight * (1.0 - RATE_MUON * DECAY) - RATE_MUON * 0.2 * math.sqrt(
            largest
        ) * side(part)
        results += [new_weight, MOMENTUM * mom + side(grad)]
    rest = enc_grad[2, n_out : n_out + n_emb + n_link]
    rest = narrow_gather(rest)
    embed_grad = rest[:, :n_emb].reshape(embed.shape)
    link_grad = rest[:, n_emb:].reshape(enc_to_dec.shape)
    head_grad = jnp.concatenate([dec_grad[1, m_qkv:], dec_grad[2, m_out:]], 0).reshape(head.shape)
    for weight, first, second, grad, rate, decay in [
        (embed, embed_m, embed_v, embed_grad, RATE_ADAM, DECAY),
        (enc_to_dec, enc_to_dec_m, enc_to_dec_v, link_grad, RATE_ADAM, DECAY),
        (head, head_m, head_v, head_grad, RATE_ADAM, DECAY),
        (vectors, vectors_m, vectors_v, factor * vec_total, RATE_VECTOR, 0.0),
    ]:
        first_new, second_new, new_weight = adam_update(weight, first, second, grad, rate, decay)
        results += [first_new, second_new, new_weight]
    return tuple(results)


def solution(mesh):
    enc, dec = (NR, WD), (WD, NR)
    muon = [P(None, None, enc), P(enc, None), P(None, enc), P(enc, None)]
    muon += [P(None, dec), P(dec, None), P(None, dec), P(dec, None)]
    pairs = [spec for spec in muon for _ in range(2)]
    adam = [P(WD, None)] * 6 + [P(dec, None)] * 3 + [P()] * 3
    in_specs = [P(WD, None, None), P(WD, None), P(WD, None), P()] + pairs + adam
    out_specs = [P(), P()] + pairs + adam
    return jax.shard_map(
        per_device,
        mesh=mesh,
        in_specs=tuple(in_specs),
        out_specs=tuple(out_specs),
        check_vma=False,
    )
```

```python
import functools
import math

import jax
import jax.numpy as jnp
from jax import lax
from jax.experimental import pallas as pl
from jax.experimental.pallas import tpu as pltpu
from jax.sharding import PartitionSpec as P

WD = "wide"
NR = "narrow"
D = 768
HD = 64
FE = 3072
DD = 384
FD = 1536
PIX = 1536
GROUPS = 3
NS_STEPS = 5
STEP = 10
QN = 4

EPS_NORM = 1e-06
TARGET_EPS = 1.0
CLIP_AT = 0.0002
MOMENTUM = 0.95
RATE_MUON = 0.15
RATE_ADAM = 0.02
RATE_VECTOR = 0.2
DECAY = 0.05
BETA_ONE = 0.9
BETA_TWO = 0.95
EPS_ADAM = 1e-12
NS_A = 3.4445
NS_B = -4.775
NS_C = 2.0315
ROOT_HALF = 0.7071067811865476
INV_ROOT_TWO_PI = 0.3989422804014327
BF = jnp.bfloat16
F32 = jnp.float32
LOG2E = 1.4426950408889634
PAIR = 2 * HD
BLOCKS = 3
PAIRS = [(i, j) for i in range(BLOCKS) for j in range(i, BLOCKS)]
VMEM_LIMIT = 56 * 2**20
COST = pl.CostEstimate(flops=1000, bytes_accessed=1000, transcendentals=0)

BLOCK = ("ln1_g", "ln1_b", "q_b", "v_b", "out_b", "ln2_g", "ln2_b", "up_b", "down_b")


def vector_layout():
    entries = []
    for side, width, hidden in (("e", D, FE), ("d", DD, FD)):
        if side == "d":
            entries += [("in_b", DD), ("mask", DD)]
        entries += [(side + name, hidden if name == "up_b" else width) for name in BLOCK]
        entries += [(side + "lnf_g", width), (side + "lnf_b", width)]
        if side == "e":
            entries += [("emb_b", D)]
    entries += [("head_b", PIX)]
    table, offset = {}, 0
    for name, extent in entries:
        table[name] = (offset, extent)
        offset += extent
    return table


def wide_digits(count):
    digits, rest, step = [], count, 1
    while rest > 1:
        radix = 2 if not digits or rest % 4 else 4
        digits.append((step, radix))
        step, rest = step * radix, rest // radix
    return digits


def shift_pairs(count, digit, delta, keep=None):
    step, radix = digit
    pairs = []
    for src in range(count):
        place = src // step % radix
        if 0 <= place + delta < radix and (keep is None or keep(place)):
            pairs.append((src, src + delta * step))
    return pairs


def wide_move(value, digit, delta, keep=None):
    return lax.ppermute(value, WD, shift_pairs(lax.axis_size(WD), digit, delta, keep))


def wide_flip(value, bit):
    count = lax.axis_size(WD)
    return lax.ppermute(value, WD, [(src, src ^ bit) for src in range(count)])


def narrow_flip(value, bit):
    return lax.ppermute(value, NR, [(src, src ^ bit) for src in range(QN)])


def place_in(digit):
    return lax.axis_index(WD) // digit[0] % digit[1]


def pick_half(value, which, axis):
    return lax.dynamic_index_in_dim(value, which, axis, keepdims=False)


def both(mine, theirs, place, axis):
    first = jnp.where(place == 0, mine, theirs)
    second = jnp.where(place == 0, theirs, mine)
    return jnp.stack([first, second], axis)


def in_order(got, place):
    odd, high = place % 2 == 1, place // 2 == 1
    got = [jnp.where(odd, got[k ^ 1], got[k]) for k in range(4)]
    return [jnp.where(high, got[k ^ 2], got[k]) for k in range(4)]


def after(value, *earlier):
    return lax.optimization_barrier((value,) + earlier)[0]


def slow_pieces(block):
    step, radix = wide_digits(lax.axis_size(WD))[-1]
    return {mask * step: wide_flip(block, mask * step) if mask else block for mask in range(radix)}


def all_pieces(pieces):
    pieces = dict(pieces)
    for step, radix in wide_digits(lax.axis_size(WD))[-2::-1]:
        others = [held for held in pieces if held]
        joined = jnp.stack([pieces[held] for held in others], 0)
        for mask in range(1, radix):
            pieces[mask * step] = wide_flip(pieces[0], mask * step)
            moved = wide_flip(joined, mask * step)
            for k, held in enumerate(others):
                pieces[held ^ mask * step] = moved[k]
    return pieces


def assemble(pieces):
    count = lax.axis_size(WD)
    shape = pieces[0].shape
    for digit in wide_digits(count):
        step, radix = digit
        place = place_in(digit)
        joined = {}
        for held in pieces:
            if held // step % radix == 0:
                group = [pieces[held ^ mask * step] for mask in range(radix)]
                if radix == 2:
                    joined[held] = both(group[0], group[1], place, 0)
                else:
                    joined[held] = jnp.stack(in_order(group, place), 0)
        pieces = joined
    return pieces[0].reshape((count,) + shape)


def tied(pieces, *earlier):
    return dict(zip(pieces, lax.optimization_barrier((tuple(pieces.values()),) + earlier)[0]))


def narrow_pair(value, bit, axis=0):
    return both(value, narrow_flip(value, bit), lax.axis_index(NR) // bit % 2, axis)


def narrow_gather(block):
    return narrow_pair(narrow_pair(block, 2), 1, 1).reshape((QN,) + block.shape)


def line_scatter(value, digit, axis):
    place = place_in(digit)
    total = pick_half(value, place, axis).astype(F32)
    for mask in range(1, digit[1]):
        sent = pick_half(value, place ^ mask, axis).astype(BF)
        total = total + wide_flip(sent, mask * digit[0]).astype(F32)
    return total


def slow_exchange(value, digit):
    place = place_in(digit)
    got = [pick_half(value, place, 0)]
    for mask in range(1, digit[1]):
        got.append(wide_flip(pick_half(value, place ^ mask, 0), mask * digit[0]))
    return jnp.stack(in_order(got, place), 0)


def ends_total(one, two, digit, targets):
    place = place_in(digit)
    total = jnp.where(place == targets[0], one, two)
    one, two = low(one), low(two)
    count = lax.axis_size(WD)
    for mask in range(1, 4):
        pairs = [
            (src, src ^ mask * digit[0])
            for src in range(count)
            if (src // digit[0] % digit[1]) ^ mask in targets
        ]
        sent = jnp.where(place ^ mask == targets[0], one, two)
        total = total + lax.ppermute(sent, WD, pairs).astype(F32)
    return total


def joined(big, small):
    rows = small.shape[1] // 2
    return jnp.concatenate([big, jnp.concatenate([small[:, :rows], small[:, rows:]], 2)], 1)


def parted(value, rows):
    small = value[:, rows:]
    width = small.shape[2] // 2
    return value[:, :rows], jnp.concatenate([small[..., :width], small[..., width:]], 1)


def joined_exchange(big, small, digit):
    return parted(slow_exchange(joined(big, small), digit), big.shape[1])


def pair_sum(value):
    return value + narrow_flip(value, 1)


def sum_all(value):
    value = pair_sum(value)
    value = value + narrow_flip(value, 2)
    bit = 1
    while bit < lax.axis_size(WD):
        value = value + wide_flip(value, bit)
        bit *= 2
    return value


def sum_tiny(value):
    me = lax.axis_index(NR)
    parts = in_order([value] + [narrow_flip(value, mask) for mask in range(1, QN)], me)
    value = (parts[0] + parts[1]) + (parts[2] + parts[3])
    for digit in wide_digits(lax.axis_size(WD)):
        if digit[1] == 2:
            value = value + wide_flip(value, digit[0])
        else:
            flips = [wide_flip(value, mask * digit[0]) for mask in range(1, 4)]
            parts = in_order([value] + flips, place_in(digit))
            value = (parts[0] + parts[1]) + (parts[2] + parts[3])
    return value


def narrow_parts(part):
    part = low(part.astype(F32) + narrow_flip(part, 1).astype(F32))
    return [part, narrow_flip(part, 2)]


def sinusoid(positions, extent):
    half_extent = extent // 2
    frequency = jnp.exp(
        jnp.arange(half_extent, dtype=F32) * (-2.0 * math.log(10000.0) / extent)
    )
    angles = positions.astype(F32)[:, None] * frequency[None, :]
    return jnp.concatenate([jnp.sin(angles), jnp.cos(angles)], axis=1)


def low(value):
    return value.astype(BF)


def mm(left, right):
    return jnp.dot(left, right, preferred_element_type=F32)


def mm_tn(left, right):
    return lax.dot_general(left, right, (((0,), (0,)), ((), ())), preferred_element_type=F32)


def mm_nt(left, right):
    return lax.dot_general(left, right, (((1,), (1,)), ((), ())), preferred_element_type=F32)


def col_sum(value):
    return jnp.sum(value, 0, keepdims=True)


def layer_norm(value, gain, bias):
    center = value - jnp.mean(value, -1, keepdims=True)
    inv = lax.rsqrt(jnp.mean(center * center, -1, keepdims=True) + EPS_NORM)
    normed = center * inv
    return (normed * gain + bias, (normed, inv))


def norm_back(grad, saved, gain):
    normed, inv = saved
    grad_n = grad * gain
    grad_in = inv * (
        grad_n
        - jnp.mean(grad_n, -1, keepdims=True)
        - normed * jnp.mean(grad_n * normed, -1, keepdims=True)
    )
    return (grad_in, col_sum(grad * normed), col_sum(grad))


def gelu_value(upper):
    return 0.5 * upper * (1.0 + lax.erf(upper * ROOT_HALF))


def gelu_slope(upper):
    return (
        0.5 * (1.0 + lax.erf(upper * ROOT_HALF))
        + upper * jnp.exp(-0.5 * upper * upper) * INV_ROOT_TWO_PI
    )


def group_targets(pix, groups):
    rows = pix.astype(F32)
    masks = [(groups == g).astype(F32)[None, :] for g in range(GROUPS)]
    per_group = pix.shape[-1] // GROUPS

    def spread(parts):
        return sum(part * mask for part, mask in zip(parts, masks))

    means = [jnp.sum(rows * mask, -1, keepdims=True) / per_group for mask in masks]
    center = rows - spread(means)
    squares = center * center
    scale = [
        lax.rsqrt(jnp.sum(squares * mask, -1, keepdims=True) / per_group + TARGET_EPS)
        for mask in masks
    ]
    return center * spread(scale)


def dot_nn(left, right):
    return jnp.dot(left, right, preferred_element_type=F32)


def dot_tn(left, right):
    return mm_tn(left, right)


def dot_nt(left, right):
    return mm_nt(left, right)


def lane_masked(value):
    lane = lax.broadcasted_iota(jnp.int32, value.shape, 1)
    zero = jnp.zeros_like(value)
    return [jnp.where(lane < HD, value, zero), jnp.where(lane < HD, zero, value)]

def attn_fwd_kernel(tile, q_ref, kv_ref, o_ref, of_ref, lse_ref, s_ref):
    queries = q_ref.shape[0]; keys = kv_ref.shape[1]
    qs = lane_masked(q_ref[...])
    scale = HD ** -0.5 * LOG2E
    def first(t, peaks):
        at = pl.ds(pl.multiple_of(t * tile, tile), tile)
        k_t = kv_ref[0, at, :]
        out = []
        for h in range(2):
            s = dot_nt(k_t, qs[h])
            s_ref[h, at, :] = s
            out.append(jnp.maximum(peaks[h], jnp.max(s, 0, keepdims=True)))
        return tuple(out)
    start = jnp.full((1, queries), -jnp.inf, F32)
    peaks = lax.fori_loop(0, keys // tile, first, (start, start))
    peaks = [p * scale for p in peaks]
    def second(t, carry):
        at = pl.ds(pl.multiple_of(t * tile, tile), tile)
        v_t = kv_ref[1, at, :]
        out = []
        for h in range(2):
            total, mixed = carry[h]
            p = jnp.exp2(s_ref[h, at, :] * scale - peaks[h])
            out.append((total + jnp.sum(p, 0, keepdims=True), mixed + dot_tn(v_t, p.astype(BF))))
        return tuple(out)
    zero = (jnp.zeros((1, queries), F32), jnp.zeros((PAIR, queries), F32))
    done = lax.fori_loop(0, keys // tile, second, (zero, zero))
    row = lax.broadcasted_iota(jnp.int32, (PAIR, queries), 0)
    mixed = jnp.where(row < HD, done[0][1] / done[0][0], done[1][1] / done[1][0]).T
    of_ref[...] = mixed
    o_ref[...] = mixed.astype(BF)
    for h in range(2):
        lse_ref[0, h : h + 1, :] = peaks[h] + jnp.log2(done[h][0])

def attention_fwd(q, kv, tile):
    queries, width = q.shape; keys = kv.shape[1]
    pairs = width // PAIR
    return pl.pallas_call(
        functools.partial(attn_fwd_kernel, tile),
        grid=(pairs,),
        in_specs=[pl.BlockSpec((queries, PAIR), lambda i: (0, i)), pl.BlockSpec((2, keys, PAIR), lambda i: (0, 0, i))],
        out_specs=[pl.BlockSpec((queries, PAIR), lambda i: (0, i)), pl.BlockSpec((queries, PAIR), lambda i: (0, i)), pl.BlockSpec((1, 2, queries), lambda i: (i, 0, 0))],
        out_shape=[jax.ShapeDtypeStruct((queries, width), BF), jax.ShapeDtypeStruct((queries, width), F32), jax.ShapeDtypeStruct((pairs, 2, queries), F32)],
        scratch_shapes=[pltpu.VMEM((2, keys, queries), F32)],
        compiler_params=pltpu.CompilerParams(vmem_limit_bytes=VMEM_LIMIT),
        cost_estimate=COST,
    )(q, kv)

def attn_bwd_kernel(tile, q_ref, kv_ref, g_ref, of_ref, lse_ref, dq_ref, dkv_ref, dqt_ref):
    queries = q_ref.shape[0]; keys = kv_ref.shape[1]
    scale = HD ** -0.5
    qs = lane_masked(q_ref[...]); gs = lane_masked(g_ref[...])
    prod = g_ref[...].astype(F32) * of_ref[...]
    which = lax.broadcasted_iota(jnp.int32, (8, PAIR), 0); lane = lax.broadcasted_iota(jnp.int32, (8, PAIR), 1)
    picks = jnp.where(lane // HD == which, 1.0, 0.0)
    deltas = lax.dot_general(picks, prod, (((1,), (1,)), ((), ())), precision=lax.Precision.HIGHEST, preferred_element_type=F32)
    dqt_ref[...] = jnp.zeros_like(dqt_ref)
    def step(t, carry):
        at = pl.ds(pl.multiple_of(t * tile, tile), tile)
        k_t = kv_ref[0, at, :]; v_t = kv_ref[1, at, :]
        dk = jnp.zeros((tile, PAIR), F32); dv = jnp.zeros((tile, PAIR), F32)
        for h in range(2):
            p = jnp.exp2(dot_nt(k_t, qs[h]) * (scale * LOG2E) - lse_ref[0, h : h + 1, :])
            dp = dot_nt(v_t, gs[h])
            ds = (p * (dp - deltas[h : h + 1, :])).astype(BF)
            dv = dv + dot_nn(p.astype(BF), gs[h])
            dk = dk + dot_nn(ds, qs[h])
            dqt_ref[h] += dot_tn(k_t, ds)
        dkv_ref[0, at, :] = (dk * scale).astype(BF)
        dkv_ref[1, at, :] = dv.astype(BF)
        return carry
    lax.fori_loop(0, keys // tile, step, 0)
    row = lax.broadcasted_iota(jnp.int32, (PAIR, queries), 0)
    dq_ref[...] = (jnp.where(row < HD, dqt_ref[0], dqt_ref[1]).T * scale).astype(BF)

def attention_bwd(q, kv, grad, mixed, lse, tile):
    queries, width = q.shape; keys = kv.shape[1]
    pairs = width // PAIR
    qspec = pl.BlockSpec((queries, PAIR), lambda i: (0, i)); kspec = pl.BlockSpec((2, keys, PAIR), lambda i: (0, 0, i))
    return pl.pallas_call(
        functools.partial(attn_bwd_kernel, tile),
        grid=(pairs,),
        in_specs=[qspec, kspec, qspec, qspec, pl.BlockSpec((1, 2, queries), lambda i: (i, 0, 0))],
        out_specs=[qspec, kspec],
        out_shape=[jax.ShapeDtypeStruct((queries, width), BF), jax.ShapeDtypeStruct((2, keys, width), BF)],
        scratch_shapes=[pltpu.VMEM((2, PAIR, queries), F32)],
        compiler_params=pltpu.CompilerParams(vmem_limit_bytes=VMEM_LIMIT),
        cost_estimate=COST,
    )(q, kv, grad, mixed, lse)


def split(value):
    high = value.astype(BF)
    return high, (value - high.astype(F32)).astype(BF)

def tile_rows(size, other, index):
    if not other:
        return slice(index * size, (index + 1) * size), slice(0, size)
    half = len(PAIRS) // 2
    at = len(PAIRS) * other + index % half * size
    return slice(at, at + size), slice(index // half * size, (index // half + 1) * size)


def slab_rows(grad, mom, factor, period, count):
    row = lax.rem(lax.broadcasted_iota(jnp.int32, (grad.shape[0], 1), 0), period)
    scale = jnp.where(row < count, factor, 0.0)
    return MOMENTUM * mom.astype(F32) + scale * grad


def gram_kernel(
    periods, counts_ref, factor_ref, big_grad, big_mom, small_grad, small_mom, keep_ref, send_ref, out_ref
):
    for k, (grad, mom) in enumerate(((big_grad, big_mom), (small_grad, small_mom))):
        rows = slab_rows(grad[...], mom[...], factor_ref[0], periods[k], counts_ref[k])
        size = rows.shape[1] // BLOCKS
        high, rest = split(rows)
        for index, (i, j) in enumerate(PAIRS):
            a, b = slice(i * size, (i + 1) * size), slice(j * size, (j + 1) * size)
            tile = dot_tn(high[:, a], high[:, b]) + (
                dot_tn(high[:, a], rest[:, b]) + dot_tn(rest[:, a], high[:, b])
            )
            at, cols = tile_rows(size, k * big_grad.shape[1] // BLOCKS, index)
            out_ref[at, cols] = tile
    cols = keep_ref.shape[1]
    first = counts_ref[2] == 0
    left, right = out_ref[:, :cols], out_ref[:, cols:]
    keep_ref[...] = jnp.where(first, left, right)
    send_ref[...] = jnp.where(first, right, left)


def packed_gram(periods, counts, factor, slabs):
    n, m = slabs[0].shape[1], slabs[2].shape[1]
    rows = len(PAIRS) * (n // BLOCKS) + len(PAIRS) // 2 * (m // BLOCKS)
    cols = n // BLOCKS
    return pl.pallas_call(
        functools.partial(gram_kernel, periods),
        in_specs=[pl.BlockSpec(memory_space=pltpu.SMEM)] * 2
        + [pl.BlockSpec(memory_space=pltpu.VMEM)] * 4,
        out_shape=[jax.ShapeDtypeStruct((rows, cols // 2), F32)] * 2,
        scratch_shapes=[pltpu.VMEM((rows, cols), F32)],
        compiler_params=pltpu.CompilerParams(vmem_limit_bytes=VMEM_LIMIT),
        cost_estimate=COST,
    )(counts, factor, *slabs)


class Square:
    def __init__(self, refs, blocks):
        self.full, self.gram, self.poly, self.prod, self.temp = refs
        self.blocks = blocks

def put(ref, rows, cols, value):
    high, rest = split(value)
    ref[0, rows, cols] = high
    ref[1, rows, cols] = rest

def product(left, right, blocks, store):
    n = left.shape[1]
    size = n // blocks
    for j in range(blocks):
        rows, cols = slice(0, (j + 1) * size), slice(j * size, (j + 1) * size)
        tile = dot_nn(left[0, rows, :], right[0, :, cols]) + (
            dot_nn(left[0, rows, :], right[1, :, cols]) + dot_nn(left[1, rows, :], right[0, :, cols])
        )
        for i in range(j + 1):
            a = slice(i * size, (i + 1) * size)
            block = tile[a]
            store(a, cols, block)
            if i != j:
                store(cols, a, block.T)

def make_poly(sq):
    n = sq.full.shape[0]
    def store(rows, cols, block):
        value = NS_C * block + NS_B * sq.full[rows, cols]
        if rows == cols:
            r = lax.broadcasted_iota(jnp.int32, block.shape, 0); c = lax.broadcasted_iota(jnp.int32, block.shape, 1)
            value = value + jnp.where(r == c, NS_A, 0.0)
        put(sq.poly, rows, cols, value)
    product(sq.gram, sq.gram, sq.blocks, store)

def next_gram(sq):
    product(sq.poly, sq.gram, sq.blocks, lambda r, c, b: put(sq.temp, r, c, b))
    def store(r, c, b):
        sq.full[r, c] = b
        put(sq.gram, r, c, b)
    product(sq.temp, sq.poly, sq.blocks, store)

def next_product(sq):
    product(sq.poly, sq.prod, sq.blocks, lambda r, c, b: put(sq.temp, r, c, b))
    sq.prod[...] = sq.temp[...]

def ortho_kernel(
    periods, counts_ref, factor_ref, mine_ref, other_ref, big_grad, big_mom, small_grad, small_mom,
    big_out, small_out, packed_ref, *refs,
):
    squares = [Square(refs[:5], BLOCKS), Square(refs[5:], 1)]
    cols = mine_ref.shape[1]
    first = counts_ref[2] == 0
    packed_ref[:, :cols] = jnp.where(first, mine_ref[...], other_ref[...])
    packed_ref[:, cols:] = jnp.where(first, other_ref[...], mine_ref[...])
    scales = []
    for sq, other in zip(squares, (0, big_grad.shape[1] // BLOCKS)):
        size = sq.full.shape[0] // BLOCKS
        r = lax.broadcasted_iota(jnp.int32, (size, size), 0)
        c = lax.broadcasted_iota(jnp.int32, (size, size), 1)
        diag = jnp.zeros((size, size), F32)
        for index, (i, j) in enumerate(PAIRS):
            if i == j:
                diag = diag + jnp.where(r == c, packed_ref[tile_rows(size, other, index)], 0.0)
        trace = jnp.sum(jnp.sum(diag, 0, keepdims=True), 1, keepdims=True)
        scale = 1.0 / (jnp.sqrt(trace) + 1e-07)
        scales.append(scale)
        for index, (i, j) in enumerate(PAIRS):
            tile = packed_ref[tile_rows(size, other, index)] * (scale * scale)
            a, b = slice(i * size, (i + 1) * size), slice(j * size, (j + 1) * size)
            sq.full[a, b] = tile
            put(sq.gram, a, b, tile)
            if i != j:
                sq.full[b, a] = tile.T
                put(sq.gram, b, a, tile.T)
    for sq in squares:
        make_poly(sq)
    for sq in squares:
        sq.prod[...] = sq.poly[...]
        next_gram(sq)
    def step(_, carry):
        for sq in squares: make_poly(sq)
        for sq in squares: next_product(sq)
        for sq in squares: next_gram(sq)
        return carry
    lax.fori_loop(1, NS_STEPS - 1, step, 0)
    for sq in squares: make_poly(sq)
    for sq in squares: next_product(sq)
    slabs = ((big_grad, big_mom, big_out), (small_grad, small_mom, small_out))
    for k, (sq, scale, (grad, mom, out)) in enumerate(zip(squares, scales, slabs)):
        rows = slab_rows(grad[...], mom[...], factor_ref[0], periods[k], counts_ref[k])
        high, rest = split(rows * scale)
        out[...] = (
            dot_nn(high, sq.prod[0]) + (dot_nn(high, sq.prod[1]) + dot_nn(rest, sq.prod[0]))
        ).astype(BF)


def orthogonal(periods, counts, factor, mine, other, slabs):
    def scratch(n):
        return [pltpu.VMEM((n, n), F32)] + [pltpu.VMEM((2, n, n), BF)] * 4

    big, small = slabs[0], slabs[2]
    return pl.pallas_call(
        functools.partial(ortho_kernel, periods),
        in_specs=[pl.BlockSpec(memory_space=pltpu.SMEM)] * 2
        + [pl.BlockSpec(memory_space=pltpu.VMEM)] * 6,
        out_shape=[jax.ShapeDtypeStruct(big.shape, BF), jax.ShapeDtypeStruct(small.shape, BF)],
        scratch_shapes=[pltpu.VMEM((mine.shape[0], 2 * mine.shape[1]), F32)]
        + scratch(big.shape[1])
        + scratch(small.shape[1]),
        compiler_params=pltpu.CompilerParams(vmem_limit_bytes=VMEM_LIMIT),
        cost_estimate=COST,
    )(counts, factor, mine, other, *slabs)


def call(kernel, outs, args, flops, smem=0):
    return pl.pallas_call(
        kernel,
        in_specs=[pl.BlockSpec(memory_space=pltpu.SMEM)] * smem
        + [pl.BlockSpec(memory_space=pltpu.VMEM)] * (len(args) - smem),
        out_specs=[pl.BlockSpec(memory_space=pltpu.VMEM)] * len(outs),
        out_shape=[jax.ShapeDtypeStruct(shape, kind) for shape, kind in outs],
        compiler_params=pltpu.CompilerParams(vmem_limit_bytes=VMEM_LIMIT),
        cost_estimate=COST,
    )(*args)


def vec_at(vec_ref, name):
    offset, extent = vector_layout()[name]
    return vec_ref[:, offset : offset + extent]


def head_masks(value):
    lane = lax.broadcasted_iota(jnp.int32, value.shape, 1) // HD
    return [jnp.where(lane == h, value, jnp.zeros_like(value)) for h in range(value.shape[1] // HD)]


def small_probs(queries, keys, vis):
    scores = dot_nt(queries, keys) * HD**-0.5
    column = lax.broadcasted_iota(jnp.int32, scores.shape, 1)
    scores = jnp.where(column < vis, scores, -jnp.inf)
    exp_scores = jnp.exp(scores - jnp.max(scores, -1, keepdims=True))
    return exp_scores / jnp.sum(exp_scores, -1, keepdims=True)


def enc_attention_kernel(
    vis, clips, start_ref, pos_ref, vec_ref, w_ref, qb_ref, vb_ref, wout_ref,
    stream_ref, hid_ref, qkv_ref, attn_ref, part_ref,
):
    stream = start_ref[...] + vec_at(vec_ref, "emb_b") + pos_ref[...]
    stream_ref[...] = stream
    hid = low(layer_norm(stream, vec_at(vec_ref, "eln1_g"), vec_at(vec_ref, "eln1_b"))[0])
    hid_ref[...] = hid
    qkv_ref[0] = low(dot_nt(hid, w_ref[0]) + qb_ref[...])
    qkv_ref[1] = low(dot_nt(hid, w_ref[1]))
    qkv_ref[2] = low(dot_nt(hid, w_ref[2]) + vb_ref[...])
    rows = stream.shape[0] // clips
    for clip in range(clips):
        at = slice(clip * rows, (clip + 1) * rows)
        keys = qkv_ref[1, at, :]
        mixed = 0.0
        for queries, values in zip(head_masks(qkv_ref[0, at, :]), head_masks(qkv_ref[2, at, :])):
            mixed = mixed + dot_nn(low(small_probs(queries, keys, vis)), values)
        attn_ref[at, :] = low(mixed)
    part_ref[...] = low(dot_nn(attn_ref[...], wout_ref[...]))


def enc_units_kernel(
    stream_ref, total_ref, more_ref, vec_ref, wup_ref, upb_ref, wdown_ref,
    middle_ref, hid_ref, upper_ref, active_ref, part_ref,
):
    middle = stream_ref[...] + (total_ref[...].astype(F32) + more_ref[...].astype(F32)) + vec_at(vec_ref, "eout_b")
    middle_ref[...] = middle
    hid = low(layer_norm(middle, vec_at(vec_ref, "eln2_g"), vec_at(vec_ref, "eln2_b"))[0])
    hid_ref[...] = hid
    upper = dot_nt(hid, wup_ref[...]) + upb_ref[...]
    upper_ref[...] = upper
    active = low(gelu_value(upper))
    active_ref[...] = active
    part_ref[...] = low(dot_nn(active, wdown_ref[...]))


def pick_matrix(own, padded, first, shown_ref):
    row = lax.broadcasted_iota(jnp.int32, (own, padded), 0) + first
    return (row == shown_ref[...]).astype(F32)


def bridge_kernel(
    own, where_ref, middle_ref, total_ref, more_ref, vec_ref, link_ref, w_ref, shown_ref, pos_ref,
    result_ref, dstream_ref, hid_ref, q_ref, kv_ref,
):
    result_ref[...] = middle_ref[...] + (total_ref[...].astype(F32) + more_ref[...].astype(F32)) + vec_at(vec_ref, "edown_b")
    padded = shown_ref.shape[1]
    mine = result_ref[pl.ds(pl.multiple_of(where_ref[0] * padded, padded), padded), :]
    final = low(layer_norm(mine, vec_at(vec_ref, "elnf_g"), vec_at(vec_ref, "elnf_b"))[0])
    latent = dot_nn(final, link_ref[...]) + vec_at(vec_ref, "in_b")
    parts = []
    for _ in range(3):
        parts.append(low(latent))
        latent = latent - parts[-1].astype(F32)
    tile = pos_ref.shape[0] // 7

    def step(t, carry):
        first = pl.multiple_of(t * tile, tile)
        at = pl.ds(first, tile)
        pick = pick_matrix(tile, padded, where_ref[1] * own + first, shown_ref)
        chosen = low(pick)
        value = (dot_nn(chosen, parts[0]) + dot_nn(chosen, parts[1])) + dot_nn(chosen, parts[2])
        hidden = 1.0 - jnp.sum(pick, -1, keepdims=True)
        value = value + hidden * vec_at(vec_ref, "mask") + pos_ref[at, :]
        dstream_ref[at, :] = value
        hid_ref[at, :] = low(
            layer_norm(value, vec_at(vec_ref, "dln1_g"), vec_at(vec_ref, "dln1_b"))[0]
        )
        return carry

    lax.fori_loop(0, 7, step, 0)
    hid = hid_ref[...]
    width = hid.shape[1]
    q_ref[...] = low(dot_nt(hid, w_ref[:width, :]) + vec_at(vec_ref, "dq_b"))
    kv_ref[0] = low(dot_nt(hid, w_ref[width : 2 * width, :]))
    kv_ref[1] = low(dot_nt(hid, w_ref[2 * width :, :]) + vec_at(vec_ref, "dv_b"))


def bridge_back_kernel(
    own, where_ref, gq_ref, gkv_ref, got_ref, hid_ref, w_ref, dstream_ref, mid_ref, vec_ref, shown_ref,
    gw_ref, latent_ref, sums_ref, hgrad_ref,
):
    width = gq_ref.shape[1]
    gk = low(gkv_ref[0].astype(F32) + got_ref[0].astype(F32))
    gv = low(gkv_ref[1].astype(F32) + got_ref[1].astype(F32))
    hid = hid_ref[...]
    hgrad = 0.0
    for k, grad in enumerate((gq_ref[...], gk, gv)):
        at = slice(k * width, (k + 1) * width)
        gw_ref[at, :] = low(dot_tn(grad, hid))
        hgrad = hgrad + dot_nn(grad, w_ref[at, :])
    sums_ref[...] = jnp.zeros_like(sums_ref)
    hgrad_ref[...] = hgrad
    sums_ref[0:1, :] = col_sum(gq_ref[...].astype(F32))
    sums_ref[1:2, :] = col_sum(gv.astype(F32))
    latent_ref[...] = jnp.zeros_like(latent_ref)
    padded = shown_ref.shape[1]
    tile = own // 7
    gain = vec_at(vec_ref, "dln1_g")

    def step(t, carry):
        first = pl.multiple_of(t * tile, tile)
        at = pl.ds(first, tile)
        saved = layer_norm(dstream_ref[at, :], gain, gain)[1]
        sgrad, gain_grad, bias_grad = norm_back(hgrad_ref[at, :], saved, gain)
        din = sgrad + mid_ref[at, :]
        pick = pick_matrix(tile, padded, where_ref[1] * own + first, shown_ref)
        hidden = 1.0 - jnp.sum(pick, -1, keepdims=True)
        sums_ref[2:3, :] += gain_grad
        sums_ref[3:4, :] += bias_grad
        sums_ref[4:5, :] += col_sum(hidden * din)
        chosen = low(pick)
        high = low(din)
        rest = low(din - high.astype(F32))
        latent_ref[...] += dot_tn(chosen, high) + dot_tn(chosen, rest)
        return carry

    lax.fori_loop(0, 7, step, 0)


def enc_units_back_kernel(
    latent_ref, result_ref, vec_ref, link_ref, wdown_ref, wup_ref, upper_ref, active_ref, hid_ref,
    glink_ref, grad_ref, gdown_ref, gup_ref, part_ref, sums_ref,
):
    sums_ref[...] = jnp.zeros_like(sums_ref)
    latent = latent_ref[...]
    gain = vec_at(vec_ref, "elnf_g")
    final, saved = layer_norm(result_ref[...], gain, vec_at(vec_ref, "elnf_b"))
    glink_ref[...] = low(dot_tn(low(final), latent))
    grad, gain_grad, bias_grad = norm_back(dot_nt(latent, link_ref[...]), saved, gain)
    grad_ref[...] = grad
    sums_ref[0:1, : latent.shape[1]] = col_sum(latent.astype(F32))
    sums_ref[1:2, :] = gain_grad
    sums_ref[2:3, :] = bias_grad
    sums_ref[3:4, :] = col_sum(grad)
    down = low(grad)
    gdown_ref[...] = low(dot_tn(active_ref[...], down))
    upper = low(dot_nt(down, wdown_ref[...]) * gelu_slope(upper_ref[...]))
    sums_ref[4:5, :] = col_sum(upper.astype(F32))
    part_ref[...] = low(dot_nn(upper, wup_ref[...]))
    gup_ref[...] = low(dot_tn(upper, hid_ref[...]))


def enc_attention_back_kernel(
    vis, clips, total_ref, more_ref, grad_ref, middle_ref, vec_ref, attn_ref, wout_ref, qkv_ref, w_ref, hid_ref,
    mid_ref, gout_ref, gqkv_ref, part_ref, sums_ref, dqkv_ref,
):
    sums_ref[...] = jnp.zeros_like(sums_ref)
    gain = vec_at(vec_ref, "eln2_g")
    saved = layer_norm(middle_ref[...], gain, gain)[1]
    mid, gain_grad, bias_grad = norm_back((total_ref[...].astype(F32) + more_ref[...].astype(F32)), saved, gain)
    mid = mid + grad_ref[...]
    mid_ref[...] = mid
    sums_ref[0:1, :] = gain_grad
    sums_ref[1:2, :] = bias_grad
    sums_ref[2:3, :] = col_sum(mid)
    out = low(mid)
    gout_ref[...] = low(dot_tn(attn_ref[...], out))
    attn_grad = low(dot_nt(out, wout_ref[...]))
    rows = mid.shape[0] // clips
    for clip in range(clips):
        at = slice(clip * rows, (clip + 1) * rows)
        queries, keys, values = (head_masks(qkv_ref[k, at, :]) for k in range(3))
        all_keys, all_values = qkv_ref[1, at, :], qkv_ref[2, at, :]
        grads = head_masks(attn_grad[at, :])
        dq = dk = dv = 0.0
        for query, key, grad in zip(queries, keys, grads):
            prob = small_probs(query, all_keys, vis)
            dprob = dot_nt(grad, all_values)
            product = prob * dprob
            dscore = low(product - prob * jnp.sum(product, -1, keepdims=True))
            dv = dv + dot_tn(low(prob), grad)
            dq = dq + dot_nn(dscore, key)
            dk = dk + dot_tn(dscore, query)
        dqkv_ref[0, at, :] = low(dq * HD**-0.5)
        dqkv_ref[1, at, :] = low(dk * HD**-0.5)
        dqkv_ref[2, at, :] = low(dv)
    width = attn_ref.shape[1]
    sums_ref[3:4, :width] = col_sum(dqkv_ref[0].astype(F32))
    sums_ref[4:5, :width] = col_sum(dqkv_ref[2].astype(F32))
    part = 0.0
    for k in range(3):
        part = part + dot_nn(dqkv_ref[k], w_ref[k])
        gqkv_ref[k] = low(dot_tn(dqkv_ref[k], hid_ref[...]))
    part_ref[...] = low(part)


def enc_start_back_kernel(total_ref, more_ref, mid_ref, stream_ref, vec_ref, pix_ref, gembed_ref, sums_ref):
    sums_ref[...] = jnp.zeros_like(sums_ref)
    gain = vec_at(vec_ref, "eln1_g")
    saved = layer_norm(stream_ref[...], gain, gain)[1]
    grad, gain_grad, bias_grad = norm_back((total_ref[...].astype(F32) + more_ref[...].astype(F32)), saved, gain)
    grad = grad + mid_ref[...]
    sums_ref[0:1, :] = gain_grad
    sums_ref[1:2, :] = bias_grad
    sums_ref[2:3, :] = col_sum(grad)
    gembed_ref[...] = low(dot_tn(pix_ref[...], low(grad)))


def group_total(keep, send):
    mine = keep + narrow_flip(send, 1)
    rows = mine.shape[0] // 2
    one, two = mine[:rows], mine[rows:]
    bits = []
    bit = 1
    while bit < wide_digits(lax.axis_size(WD))[-1][0]:
        bits.append(bit)
        bit *= 2
    for bit in bits:
        one = one + wide_flip(one, bit)
    two = two + narrow_flip(two, 2)
    one = one + narrow_flip(one, 2)
    for bit in bits:
        two = two + wide_flip(two, bit)
    mine = jnp.concatenate([one, two], 0)
    return mine, narrow_flip(mine, 1)


def adam_update(weight, first, second, gradient, rate, decay):
    first_new = BETA_ONE * first + (1.0 - BETA_ONE) * gradient
    second_new = BETA_TWO * second + (1.0 - BETA_TWO) * gradient * gradient
    direction = (
        first_new
        / (1.0 - BETA_ONE**STEP)
        / (jnp.sqrt(second_new / (1.0 - BETA_TWO**STEP)) + EPS_ADAM)
    )
    return (first_new, second_new, weight - rate * (direction + decay * weight))


def pad_rows(value, rows, axis):
    if value.shape[axis] == rows:
        return value
    widths = [(0, 0)] * value.ndim
    widths[axis] = (0, rows - value.shape[axis])
    return jnp.pad(value, widths)


def per_device(
    pixels,
    visible,
    masked,
    groups,
    enc_qkv,
    enc_qkv_mom,
    enc_out,
    enc_out_mom,
    enc_up,
    enc_up_mom,
    enc_down,
    enc_down_mom,
    dec_qkv,
    dec_qkv_mom,
    dec_out,
    dec_out_mom,
    dec_up,
    dec_up_mom,
    dec_down,
    dec_down_mom,
    embed,
    embed_m,
    embed_v,
    enc_to_dec,
    enc_to_dec_m,
    enc_to_dec_v,
    head,
    head_m,
    head_v,
    vectors,
    vectors_m,
    vectors_v,
):
    wide = lax.axis_size(WD)
    me = lax.axis_index(NR)
    half, clip = me % 2, me // 2
    slow = wide_digits(wide)[-1]
    fast = slow[0]
    plane = place_in(slow)
    clips, vis = visible.shape
    tubs = pixels.shape[1]
    own = tubs // 2

    n_up = enc_up.shape[1]
    n_q = enc_qkv.shape[2]
    n_out = enc_out.shape[0]
    n_emb = embed.shape[0] // QN
    n_link = enc_to_dec.shape[0] * DD // D // QN
    m_up = dec_up.shape[1]
    m_qkv = dec_qkv.shape[1]
    m_out = dec_out.shape[0]
    m_head = head.shape[0] * (PIX // DD)

    up_rows, down_rows = enc_up.T, enc_down
    qkv_rows = jnp.swapaxes(enc_qkv, 1, 2).reshape(3 * n_q, D)
    dqkv_rows, dup_rows = dec_qkv.T, dec_up.T
    head_rows = head.reshape(m_head, DD)
    emb_cols = lax.dynamic_slice_in_dim(embed, me * (D // QN), D // QN, 1)
    m_link = enc_to_dec.shape[0] // QN
    link_rows = lax.dynamic_slice_in_dim(enc_to_dec, me * m_link, m_link, 0)
    pack_b = jnp.concatenate([low(emb_cols).reshape(n_emb, D), low(qkv_rows), low(enc_out)], 0)
    pack_c = low(jnp.concatenate([up_rows, down_rows], 0))
    pack_d = low(
        jnp.concatenate([dup_rows, dqkv_rows, dec_out, dec_down, head_rows, link_rows], 0)
    )
    pack_d = narrow_pair(pack_d, 2)
    line_b = slow_pieces(pack_b)
    pieces_b = all_pieces(line_b)
    came = tuple(line_b.values())
    pack_c, pack_d, vis_now, _ = lax.optimization_barrier((pack_c, pack_d, visible, came))
    line_c = slow_pieces(pack_c)
    full_b = assemble(pieces_b)
    pieces_c = all_pieces(tied(line_c, full_b))
    full_c = assemble(pieces_c)
    line_d = slow_pieces(after(pack_d, tuple(pieces_c.values())))
    embed_w = full_b[:, :n_emb].reshape(PIX, D // QN)
    w_qkv = full_b[:, n_emb : n_emb + 3 * n_q].reshape(wide, 3, n_q, D)
    w_qkv = jnp.swapaxes(w_qkv, 0, 1).reshape(3, wide * n_q, D)
    w_out = full_b[:, n_emb + 3 * n_q :].reshape(wide * n_out, D)
    w_up = full_c[:, :n_up].reshape(wide * n_up, D)
    w_down = full_c[:, n_up:].reshape(wide * n_up, D)
    table = vector_layout()

    def vec_of(name):
        offset, extent = table[name]
        return vectors[offset : offset + extent]

    def share_of(name):
        offset, extent = table[name]
        share = extent // QN
        return lax.dynamic_slice_in_dim(vectors, offset + me * share, share)[None, :]

    grads = {}

    padded = -(-vis // 16) * 16
    rows = clips * padded
    shown = jnp.pad(visible, ((0, 0), (0, padded - vis)), constant_values=-1)
    vis_rows = shown.reshape(rows)
    tube_ids = jnp.arange(tubs, dtype=jnp.int32)
    vis_pix = mm(low(vis_rows[:, None] == tube_ids[None, :]), pixels[0]).astype(BF)
    vec_row = vectors[None, :]
    now_rows = jnp.pad(vis_now, ((0, 0), (0, padded - vis)), constant_values=-1).reshape(rows)
    vis_table = sinusoid(now_rows, D)
    start = mm(vis_pix, embed_w)
    start = both(start, narrow_flip(start, 2), clip, 1)
    start = both(start, narrow_flip(start, 1), half, 2).reshape(rows, D)
    units = D // QN * 4
    stream, hid1, eqkv, eattn, part = call(
        functools.partial(enc_attention_kernel, vis, clips),
        [((rows, D), F32), ((rows, D), BF), ((3, rows, D // QN), BF), ((rows, D // QN), BF), ((rows, D), BF)],
        [start, vis_table, vec_row, w_qkv, share_of("eq_b"), share_of("ev_b"), w_out],
        2 * rows * D * D,
    )
    own_pix = after(lax.dynamic_slice_in_dim(pixels[0], half * own, own, 0), part)
    targets = group_targets(own_pix, groups)
    own_pos = after(half * own + jnp.arange(own, dtype=jnp.int32), part)
    own_table = sinusoid(own_pos, DD)
    parts = narrow_parts(part)
    pieces_d = all_pieces(tied(line_d, parts[1]))
    middle, hid2, upper, active, part = call(
        enc_units_kernel,
        [((rows, D), F32), ((rows, D), BF), ((rows, units), F32), ((rows, units), BF), ((rows, D), BF)],
        [stream, *parts, vec_row, w_up, share_of("eup_b"), w_down],
        4 * rows * D * units,
    )

    parts = narrow_parts(part)
    full_d = narrow_pair(assemble(tied(pieces_d, parts[0])), 1, 2)
    at, taken = 0, []
    for extent in (m_up, m_qkv, m_out, m_up, m_head, m_link):
        taken.append(full_d[:, :, :, at : at + extent].reshape(wide * QN * extent, DD))
        at += extent
    d_up, d_qkv, d_out, d_down, d_head, link_w = taken
    d_head = d_head.reshape(DD, PIX)

    where = jnp.stack([clip, half])
    clip_shown = lax.dynamic_slice_in_dim(shown, clip, 1, 0)
    enc_result, dstream, dh1, dq, dkv = call(
        functools.partial(bridge_kernel, own),
        [((rows, D), F32), ((own, DD), F32), ((own, DD), BF), ((own, DD), BF), ((2, own, DD), BF)],
        [where, middle, *parts, vec_row, link_w, d_qkv, clip_shown, own_table],
        6 * own * DD * DD,
        1,
    )
    pick = own_pos[:, None] == clip_shown
    hidden_row = 1.0 - jnp.sum(pick.astype(F32), -1, keepdims=True)
    all_kv = both(dkv, narrow_flip(dkv, 1), half, 1).reshape(2, tubs, DD)
    def plane_rows(parts):
        return jnp.stack([pad_rows(low(part), parts[0].shape[0], 0) for part in parts], 0)

    late = lax.optimization_barrier(
        (
            (enc_up_mom, enc_qkv_mom, enc_out_mom, enc_down_mom),
            (dec_up_mom, dec_qkv_mom, dec_out_mom, dec_down_mom),
            all_kv,
        )
    )
    (up_mom, qkv_mom, out_mom, down_mom), (dup_mom, dqkv_mom, dout_mom, ddown_mom), all_kv = late
    qkv_mom = jnp.swapaxes(qkv_mom, 1, 2).reshape(3 * n_q, D)
    enc_mom, dec_mom = joined_exchange(
        plane_rows([up_mom.T, qkv_mom, out_mom, down_mom]),
        plane_rows([dup_mom.T, dqkv_mom.T, dout_mom, ddown_mom]),
        slow,
    )

    tile = next(t for t in (224, 112, 16) if tubs % t == 0)
    dattn, mixed, dlog = attention_fwd(dq, all_kv, tile)
    dattn, enc_mom, dec_mom = lax.optimization_barrier((dattn, enc_mom, dec_mom))

    dmiddle = dstream + mm(dattn, d_out) + vec_of("dout_b")
    dh2, dsaved2 = layer_norm(dmiddle, vec_of("dln2_g"), vec_of("dln2_b"))
    dh2 = low(dh2)
    dupper = mm_nt(dh2, d_up) + vec_of("dup_b")
    dactive = low(gelu_value(dupper))
    dresult = dmiddle + mm(dactive, d_down) + vec_of("ddown_b")
    hf, hsaved = layer_norm(dresult, vec_of("dlnf_g"), vec_of("dlnf_b"))
    hf = low(hf)
    predicted = mm(hf, d_head) + vec_of("head_b")
    error = (predicted - targets) * hidden_row
    loss_part = jnp.sum(error * error)
    pred_grad = error * (2.0 / (clips * wide * (tubs - vis) * PIX))

    pred_low = low(pred_grad)
    g_head = mm_tn(hf, pred_low)
    grads["head_b"] = col_sum(pred_grad)
    dgrad, grads["dlnf_g"], grads["dlnf_b"] = norm_back(
        mm_nt(pred_low, d_head), hsaved, vec_of("dlnf_g")
    )
    down_low = low(dgrad)
    g_ddown = mm_tn(dactive, down_low)
    grads["ddown_b"] = col_sum(dgrad)
    upper_low = low(mm_nt(down_low, d_down) * gelu_slope(dupper))
    g_dup = mm_tn(upper_low, dh2)
    grads["dup_b"] = col_sum(upper_low.astype(F32))
    mid_grad, grads["dln2_g"], grads["dln2_b"] = norm_back(
        mm(upper_low, d_up), dsaved2, vec_of("dln2_g")
    )
    mid_grad = mid_grad + dgrad
    out_low = low(mid_grad)
    g_dout = mm_tn(dattn, out_low)
    grads["dout_b"] = col_sum(mid_grad)
    attn_grad = low(mm_nt(out_low, d_out))
    def dec_parts(value, extent):
        return low(value).reshape(4, fast, 2, 2, extent, DD)

    def fast_scatter(value, axis):
        digits = wide_digits(wide)[:-1]
        shape = value.shape
        value = value.reshape(
            shape[:axis] + tuple(radix for _, radix in digits[::-1]) + shape[axis + 1 :]
        )
        for count, digit in enumerate(digits):
            value = line_scatter(value, digit, axis + len(digits) - 1 - count)
        return value

    def half_sum(value, place, axis, bit):
        sent = low(pick_half(value, 1 - place, axis))
        return pick_half(value, place, axis).astype(F32) + narrow_flip(sent, bit).astype(F32)

    cut = m_up - m_qkv
    p_head = dec_parts(g_head.reshape(-1, DD), m_head)
    early = jnp.stack(
        [
            dec_parts(g_dup, m_up),
            jnp.concatenate([dec_parts(g_dout, m_out), p_head[:, :, :, :, cut:]], 4),
            dec_parts(g_ddown, m_up),
        ],
        0,
    )
    early = half_sum(early, half, 4, 1)
    attn_grad, early = lax.optimization_barrier((attn_grad, early))
    early = half_sum(early, clip, 3, 2)
    gq, gkv = attention_bwd(dq, all_kv, attn_grad, mixed, dlog, tile)
    gkv, early = lax.optimization_barrier((gkv, early))
    gkv = gkv.reshape(2, 2, own, DD)
    got = narrow_flip(pick_half(gkv, 1 - half, 1), 1)
    g_dqkv, latent_part, sums, _ = call(
        functools.partial(bridge_back_kernel, own),
        [((3 * DD, DD), BF), ((padded, DD), F32), ((8, DD), F32), ((own, DD), F32)],
        [where, gq, pick_half(gkv, half, 1), got, dh1, d_qkv, dstream, mid_grad, vec_row, clip_shown],
        12 * own * DD * DD,
        1,
    )
    for row, name in enumerate(("dq_b", "dv_b", "dln1_g", "dln1_b", "mask")):
        grads[name] = sums[row]

    late = jnp.concatenate([dec_parts(g_dqkv, m_qkv), p_head[:, :, :, :, :cut]], 4)[None]
    early = fast_scatter(after(early, latent_part), 2)

    latent_pair = low(pair_sum(latent_part))
    latent_low = both(latent_pair, narrow_flip(latent_pair, 2), clip, 0).reshape(rows, DD)
    g_link, egrad, g_down, g_up, part, sums = call(
        enc_units_back_kernel,
        [((D, DD), BF), ((rows, D), F32), ((units, D), BF), ((units, D), BF), ((rows, D), BF), ((8, D), F32)],
        [latent_low, enc_result, vec_row, link_w, w_down, w_up, upper, active, hid2],
        8 * rows * D * units,
    )
    grads["in_b"] = sums[0, :DD]
    for row, name in enumerate(("elnf_g", "elnf_b", "edown_b", "eup_b")):
        grads[name] = sums[row + 1]

    def enc_parts(value, extent):
        return low(value).reshape(4, fast, extent, D).transpose(1, 0, 2, 3)

    parts = narrow_parts(part)
    g_up, g_down, late, _ = lax.optimization_barrier((g_up, g_down, late, parts[0]))
    late = half_sum(late, half, 4, 1)
    late = half_sum(after(late, parts[1]), clip, 3, 2)
    sum_up = fast_scatter(enc_parts(g_up, n_up), 0)
    sum_down = fast_scatter(enc_parts(g_down, n_up), 0)
    mid_grad, g_out, g_qkv, part, sums, _ = call(
        functools.partial(enc_attention_back_kernel, vis, clips),
        [((rows, D), F32), ((D // QN, D), BF), ((3, D // QN, D), BF), ((rows, D), BF), ((8, D), F32), ((3, rows, D // QN), BF)],
        [*parts, egrad, middle, vec_row, eattn, w_out, eqkv, w_qkv, hid1],
        4 * rows * D * D,
    )
    for row, name in enumerate(("eln2_g", "eln2_b", "eout_b")):
        grads[name] = sums[row]
    grads["eq_b"], grads["ev_b"] = sums[3, : D // QN], sums[4, : D // QN]
    parts = narrow_parts(part)
    sum_up, sum_down, _ = lax.optimization_barrier((sum_up, sum_down, parts[1]))
    ends_sum = ends_total(joined(sum_up, early[0]), joined(sum_down, early[2]), slow, (0, 3))
    g_embed, sums = call(
        enc_start_back_kernel,
        [((PIX, D), BF), ((8, D), F32)],
        [*parts, mid_grad, stream, vec_row, vis_pix],
        2 * rows * D * PIX,
    )
    for row, name in enumerate(("eln1_g", "eln1_b", "emb_b")):
        grads[name] = sums[row]
    g_embed = pick_half(g_embed.reshape(wide, QN, n_emb, D), me, 1)
    g_link = pick_half(g_link.reshape(wide, QN, n_link, D), me, 1)
    part_qkv = jnp.concatenate([enc_parts(g, n_q) for g in g_qkv], 2)
    part_rest = jnp.concatenate(
        [enc_parts(g_out, n_out), enc_parts(g_embed, n_emb), enc_parts(g_link, n_link)], 2
    )
    longer = max(part_qkv.shape[2], part_rest.shape[2])
    sum_qkv = fast_scatter(pad_rows(part_qkv, longer, 2), 0)
    sum_rest = fast_scatter(pad_rows(part_rest, longer, 2), 0)
    late = fast_scatter(late, 2)
    sum_rest, ends_sum = lax.optimization_barrier((sum_rest, ends_sum))
    middle_sum = ends_total(joined(sum_qkv, late[0]), joined(sum_rest, early[1]), slow, (1, 2))
    enc_ends, dec_ends = parted(ends_sum, n_up)
    enc_middle, dec_middle = parted(middle_sum, longer)
    middle = (plane == 1) | (plane == 2)
    enc_sum = jnp.where(middle, pad_rows(enc_middle, n_up, 1), enc_ends)
    dec_sum = jnp.where(middle, dec_middle, dec_ends)

    leading = jnp.where(me == 0, 1.0, 0.0)

    def spread(share):
        full = jnp.zeros((share.shape[0] * QN,), F32)
        return lax.dynamic_update_slice_in_dim(full, share, me * share.shape[0], 0)

    pieces = []
    for name in table:
        piece = grads[name].reshape(-1)
        if name in ("eq_b", "ev_b", "eup_b"):
            piece = spread(piece)
        elif name[0] == "e" or name == "in_b":
            piece = leading * piece
        pieces.append(piece)
    vec_total = sum_all(jnp.concatenate(pieces + [loss_part[None]]).reshape(1, -1))[0]
    loss_sum = vec_total[-1]
    vec_total = vec_total[:-1]
    squares = jnp.sum(dec_sum * dec_sum) + jnp.sum(enc_sum * enc_sum)
    square_total = sum_tiny(jnp.broadcast_to(squares, (8, 128)))[0, 0]
    grad_norm = jnp.sqrt(square_total + jnp.sum(vec_total * vec_total))
    factor = jnp.minimum(1.0, CLIP_AT / grad_norm)

    counts = jnp.asarray(
        [[n_up, m_up], [3 * n_q, m_qkv], [n_out, m_out], [n_up, m_up]], jnp.int32
    )[plane]
    counts = jnp.concatenate([counts, half[None]])
    slabs = [
        enc_sum.reshape(4 * n_up, D),
        enc_mom.reshape(4 * n_up, D),
        dec_sum.reshape(4 * m_up, DD),
        dec_mom.reshape(4 * m_up, DD),
    ]
    periods = (n_up, m_up)
    mine, other = group_total(*packed_gram(periods, counts, factor[None], slabs))
    enc_back, dec_back, _ = lax.optimization_barrier((enc_sum, dec_sum, grad_norm))
    enc_grad, dec_grad = joined_exchange(low(enc_back), low(dec_back), slow)
    enc_grad, dec_grad = enc_grad.astype(F32) * factor, dec_grad.astype(F32) * factor

    def turned(value):
        return value.T

    def same(value):
        return value

    def unqkv(value):
        return jnp.swapaxes(value.reshape(3, n_q, D), 1, 2)

    rest = enc_grad[2, n_out : n_out + n_emb + n_link]
    rest = narrow_gather(rest)
    embed_grad = rest[:, :n_emb].reshape(embed.shape)
    link_grad = rest[:, n_emb:].reshape(enc_to_dec.shape)
    head_grad = jnp.concatenate([dec_grad[1, m_qkv:], dec_grad[2, m_out:]], 0).reshape(head.shape)
    adam = []
    for weight, first, second, grad, rate, decay in [
        (embed, embed_m, embed_v, embed_grad, RATE_ADAM, DECAY),
        (enc_to_dec, enc_to_dec_m, enc_to_dec_v, link_grad, RATE_ADAM, DECAY),
        (head, head_m, head_v, head_grad, RATE_ADAM, DECAY),
        (vectors, vectors_m, vectors_v, factor * vec_total, RATE_VECTOR, 0.0),
    ]:
        adam += adam_update(weight, first, second, grad, rate, decay)
    entries = [
        (enc_qkv, enc_qkv_mom, enc_grad[1, : 3 * n_q], unqkv, 3 * D),
        (enc_out, enc_out_mom, enc_grad[2, :n_out], same, D),
        (enc_up, enc_up_mom, enc_grad[0], turned, FE),
        (enc_down, enc_down_mom, enc_grad[3], same, FE),
        (dec_qkv, dec_qkv_mom, dec_grad[1, :m_qkv], turned, 3 * DD),
        (dec_out, dec_out_mom, dec_grad[2, :m_out], same, DD),
        (dec_up, dec_up_mom, dec_grad[0], turned, FD),
        (dec_down, dec_down_mom, dec_grad[3], same, FD),
    ]
    moms = [MOMENTUM * mom + side(grad) for _, mom, grad, side, _ in entries]
    mine, moms, adam = lax.optimization_barrier((mine, moms, adam))
    enc_ortho, dec_ortho = orthogonal(periods, counts, factor[None], mine, other, slabs)
    enc_ortho, dec_ortho = joined_exchange(
        enc_ortho.reshape(4, n_up, D), dec_ortho.reshape(4, m_up, DD), slow
    )
    enc_ortho, dec_ortho = enc_ortho.astype(F32), dec_ortho.astype(F32)
    results = [loss_sum, grad_norm]
    orthos = [
        enc_ortho[1, : 3 * n_q],
        enc_ortho[2, :n_out],
        enc_ortho[0],
        enc_ortho[3],
        dec_ortho[1, :m_qkv],
        dec_ortho[2, :m_out],
        dec_ortho[0],
        dec_ortho[3],
    ]
    for (weight, _, _, side, largest), mom, part in zip(entries, moms, orthos):
        step = RATE_MUON * 0.2 * math.sqrt(largest)
        results += [weight * (1.0 - RATE_MUON * DECAY) - step * side(part), mom]
    results += adam
    return tuple(results)


def solution(mesh):
    enc, dec = (NR, WD), (WD, NR)
    muon = [P(None, None, enc), P(enc, None), P(None, enc), P(enc, None)]
    muon += [P(None, dec), P(dec, None), P(None, dec), P(dec, None)]
    pairs = [spec for spec in muon for _ in range(2)]
    adam = [P(WD, None)] * 6 + [P(dec, None)] * 3 + [P()] * 3
    in_specs = [P(WD, None, None), P(WD, None), P(WD, None), P()] + pairs + adam
    out_specs = [P(), P()] + pairs + adam
    return jax.shard_map(
        per_device,
        mesh=mesh,
        in_specs=tuple(in_specs),
        out_specs=tuple(out_specs),
        check_vma=False,
    )
```

```python
import functools
import math

import jax
import jax.numpy as jnp
from jax import lax
from jax.experimental import pallas as pl
from jax.experimental.pallas import tpu as pltpu
from jax.sharding import PartitionSpec as P

WD = "wide"
NR = "narrow"
D = 768
HD = 64
FE = 3072
DD = 384
FD = 1536
PIX = 1536
GROUPS = 3
NS_STEPS = 5
STEP = 10
QN = 4

EPS_NORM = 1e-06
TARGET_EPS = 1.0
CLIP_AT = 0.0002
MOMENTUM = 0.95
RATE_MUON = 0.15
RATE_ADAM = 0.02
RATE_VECTOR = 0.2
DECAY = 0.05
BETA_ONE = 0.9
BETA_TWO = 0.95
EPS_ADAM = 1e-12
NS_A = 3.4445
NS_B = -4.775
NS_C = 2.0315
ROOT_HALF = 0.7071067811865476
INV_ROOT_TWO_PI = 0.3989422804014327
BF = jnp.bfloat16
F32 = jnp.float32
LOG2E = 1.4426950408889634
PAIR = 2 * HD
BLOCKS = 3
PAIRS = [(i, j) for i in range(BLOCKS) for j in range(i, BLOCKS)]
VMEM_LIMIT = 56 * 2**20
COST = pl.CostEstimate(flops=2000000000, bytes_accessed=1000, transcendentals=0)

BLOCK = ("ln1_g", "ln1_b", "q_b", "v_b", "out_b", "ln2_g", "ln2_b", "up_b", "down_b")


def vector_layout():
    entries = []
    for side, width, hidden in (("e", D, FE), ("d", DD, FD)):
        if side == "d":
            entries += [("in_b", DD), ("mask", DD)]
        entries += [(side + name, hidden if name == "up_b" else width) for name in BLOCK]
        entries += [(side + "lnf_g", width), (side + "lnf_b", width)]
        if side == "e":
            entries += [("emb_b", D)]
    entries += [("head_b", PIX)]
    table, offset = {}, 0
    for name, extent in entries:
        table[name] = (offset, extent)
        offset += extent
    return table


def wide_digits(count):
    digits, rest, step = [], count, 1
    while rest > 1:
        radix = 2 if not digits or rest % 4 else 4
        digits.append((step, radix))
        step, rest = step * radix, rest // radix
    return digits


def shift_pairs(count, digit, delta, keep=None):
    step, radix = digit
    pairs = []
    for src in range(count):
        place = src // step % radix
        if 0 <= place + delta < radix and (keep is None or keep(place)):
            pairs.append((src, src + delta * step))
    return pairs


def wide_move(value, digit, delta, keep=None):
    return lax.ppermute(value, WD, shift_pairs(lax.axis_size(WD), digit, delta, keep))


def wide_flip(value, bit):
    count = lax.axis_size(WD)
    return lax.ppermute(value, WD, [(src, src ^ bit) for src in range(count)])


def narrow_flip(value, bit):
    return lax.ppermute(value, NR, [(src, src ^ bit) for src in range(QN)])


def place_in(digit):
    return lax.axis_index(WD) // digit[0] % digit[1]


def pick_half(value, which, axis):
    return lax.dynamic_index_in_dim(value, which, axis, keepdims=False)


def both(mine, theirs, place, axis):
    first = jnp.where(place == 0, mine, theirs)
    second = jnp.where(place == 0, theirs, mine)
    return jnp.stack([first, second], axis)


def in_order(got, place):
    odd, high = place % 2 == 1, place // 2 == 1
    got = [jnp.where(odd, got[k ^ 1], got[k]) for k in range(4)]
    return [jnp.where(high, got[k ^ 2], got[k]) for k in range(4)]


def after(value, *earlier):
    return lax.optimization_barrier((value,) + earlier)[0]


def slow_pieces(block):
    step, radix = wide_digits(lax.axis_size(WD))[-1]
    return {mask * step: wide_flip(block, mask * step) if mask else block for mask in range(radix)}


def all_pieces(pieces):
    pieces = dict(pieces)
    for step, radix in wide_digits(lax.axis_size(WD))[-2::-1]:
        others = [held for held in pieces if held]
        joined = jnp.stack([pieces[held] for held in others], 0)
        for mask in range(1, radix):
            pieces[mask * step] = wide_flip(pieces[0], mask * step)
            moved = wide_flip(joined, mask * step)
            for k, held in enumerate(others):
                pieces[held ^ mask * step] = moved[k]
    return pieces


def assemble(pieces):
    count = lax.axis_size(WD)
    shape = pieces[0].shape
    for digit in wide_digits(count):
        step, radix = digit
        place = place_in(digit)
        joined = {}
        for held in pieces:
            if held // step % radix == 0:
                group = [pieces[held ^ mask * step] for mask in range(radix)]
                if radix == 2:
                    joined[held] = both(group[0], group[1], place, 0)
                else:
                    joined[held] = jnp.stack(in_order(group, place), 0)
        pieces = joined
    return pieces[0].reshape((count,) + shape)


def tied(pieces, *earlier):
    return dict(zip(pieces, lax.optimization_barrier((tuple(pieces.values()),) + earlier)[0]))


def narrow_pair(value, bit, axis=0):
    return both(value, narrow_flip(value, bit), lax.axis_index(NR) // bit % 2, axis)


def narrow_gather(block):
    return narrow_pair(narrow_pair(block, 2), 1, 1).reshape((QN,) + block.shape)


def line_scatter(value, digit, axis):
    place = place_in(digit)
    total = pick_half(value, place, axis).astype(F32)
    for mask in range(1, digit[1]):
        sent = pick_half(value, place ^ mask, axis).astype(BF)
        total = total + wide_flip(sent, mask * digit[0]).astype(F32)
    return total


def slow_exchange(value, digit):
    place = place_in(digit)
    got = [pick_half(value, place, 0)]
    for mask in range(1, digit[1]):
        got.append(wide_flip(pick_half(value, place ^ mask, 0), mask * digit[0]))
    return jnp.stack(in_order(got, place), 0)


def ends_total(one, two, digit, targets):
    place = place_in(digit)
    total = jnp.where(place == targets[0], one, two)
    one, two = low(one), low(two)
    count = lax.axis_size(WD)
    for mask in range(1, 4):
        pairs = [
            (src, src ^ mask * digit[0])
            for src in range(count)
            if (src // digit[0] % digit[1]) ^ mask in targets
        ]
        sent = jnp.where(place ^ mask == targets[0], one, two)
        total = total + lax.ppermute(sent, WD, pairs).astype(F32)
    return total


def joined(big, small):
    rows = small.shape[1] // 2
    return jnp.concatenate([big, jnp.concatenate([small[:, :rows], small[:, rows:]], 2)], 1)


def parted(value, rows):
    small = value[:, rows:]
    width = small.shape[2] // 2
    return value[:, :rows], jnp.concatenate([small[..., :width], small[..., width:]], 1)


def joined_exchange(big, small, digit):
    return parted(slow_exchange(joined(big, small), digit), big.shape[1])


def pair_sum(value):
    return value + narrow_flip(value, 1)


def sum_all(value):
    value = pair_sum(value)
    value = value + narrow_flip(value, 2)
    bit = 1
    while bit < lax.axis_size(WD):
        value = value + wide_flip(value, bit)
        bit *= 2
    return value


def sum_tiny(value):
    me = lax.axis_index(NR)
    parts = in_order([value] + [narrow_flip(value, mask) for mask in range(1, QN)], me)
    value = (parts[0] + parts[1]) + (parts[2] + parts[3])
    for digit in wide_digits(lax.axis_size(WD)):
        if digit[1] == 2:
            value = value + wide_flip(value, digit[0])
        else:
            flips = [wide_flip(value, mask * digit[0]) for mask in range(1, 4)]
            parts = in_order([value] + flips, place_in(digit))
            value = (parts[0] + parts[1]) + (parts[2] + parts[3])
    return value


def narrow_parts(part):
    part = low(part.astype(F32) + narrow_flip(part, 1).astype(F32))
    return [part, narrow_flip(part, 2)]


def sinusoid(positions, extent):
    half_extent = extent // 2
    frequency = jnp.exp(
        jnp.arange(half_extent, dtype=F32) * (-2.0 * math.log(10000.0) / extent)
    )
    angles = positions.astype(F32)[:, None] * frequency[None, :]
    return jnp.concatenate([jnp.sin(angles), jnp.cos(angles)], axis=1)


def low(value):
    return value.astype(BF)


def mm(left, right):
    return jnp.dot(left, right, preferred_element_type=F32)


def mm_tn(left, right):
    return lax.dot_general(left, right, (((0,), (0,)), ((), ())), preferred_element_type=F32)


def mm_nt(left, right):
    return lax.dot_general(left, right, (((1,), (1,)), ((), ())), preferred_element_type=F32)


def col_sum(value):
    return jnp.sum(value, 0, keepdims=True)


def layer_norm(value, gain, bias):
    center = value - jnp.mean(value, -1, keepdims=True)
    inv = lax.rsqrt(jnp.mean(center * center, -1, keepdims=True) + EPS_NORM)
    normed = center * inv
    return (normed * gain + bias, (normed, inv))


def norm_back(grad, saved, gain):
    normed, inv = saved
    grad_n = grad * gain
    grad_in = inv * (
        grad_n
        - jnp.mean(grad_n, -1, keepdims=True)
        - normed * jnp.mean(grad_n * normed, -1, keepdims=True)
    )
    return (grad_in, col_sum(grad * normed), col_sum(grad))


def gelu_value(upper):
    return 0.5 * upper * (1.0 + lax.erf(upper * ROOT_HALF))


def gelu_slope(upper):
    return (
        0.5 * (1.0 + lax.erf(upper * ROOT_HALF))
        + upper * jnp.exp(-0.5 * upper * upper) * INV_ROOT_TWO_PI
    )


def group_targets(pix, groups):
    rows = pix.astype(F32)
    masks = [(groups == g).astype(F32)[None, :] for g in range(GROUPS)]
    per_group = pix.shape[-1] // GROUPS

    def spread(parts):
        return sum(part * mask for part, mask in zip(parts, masks))

    means = [jnp.sum(rows * mask, -1, keepdims=True) / per_group for mask in masks]
    center = rows - spread(means)
    squares = center * center
    scale = [
        lax.rsqrt(jnp.sum(squares * mask, -1, keepdims=True) / per_group + TARGET_EPS)
        for mask in masks
    ]
    return center * spread(scale)


def dot_nn(left, right):
    return jnp.dot(left, right, preferred_element_type=F32)


def dot_tn(left, right):
    return mm_tn(left, right)


def dot_nt(left, right):
    return mm_nt(left, right)


def lane_masked(value):
    lane = lax.broadcasted_iota(jnp.int32, value.shape, 1)
    zero = jnp.zeros_like(value)
    return [jnp.where(lane < HD, value, zero), jnp.where(lane < HD, zero, value)]

def attn_fwd_kernel(tile, q_ref, kv_ref, o_ref, of_ref, lse_ref, s_ref):
    queries = q_ref.shape[0]; keys = kv_ref.shape[1]
    qs = lane_masked(q_ref[...])
    scale = HD ** -0.5 * LOG2E
    def first(t, peaks):
        at = pl.ds(pl.multiple_of(t * tile, tile), tile)
        k_t = kv_ref[0, at, :]
        out = []
        for h in range(2):
            s = dot_nt(k_t, qs[h])
            s_ref[h, at, :] = s
            out.append(jnp.maximum(peaks[h], jnp.max(s, 0, keepdims=True)))
        return tuple(out)
    start = jnp.full((1, queries), -jnp.inf, F32)
    peaks = lax.fori_loop(0, keys // tile, first, (start, start))
    peaks = [p * scale for p in peaks]
    def second(t, carry):
        at = pl.ds(pl.multiple_of(t * tile, tile), tile)
        v_t = kv_ref[1, at, :]
        out = []
        for h in range(2):
            total, mixed = carry[h]
            p = jnp.exp2(s_ref[h, at, :] * scale - peaks[h])
            out.append((total + jnp.sum(p, 0, keepdims=True), mixed + dot_tn(v_t, p.astype(BF))))
        return tuple(out)
    zero = (jnp.zeros((1, queries), F32), jnp.zeros((PAIR, queries), F32))
    done = lax.fori_loop(0, keys // tile, second, (zero, zero))
    row = lax.broadcasted_iota(jnp.int32, (PAIR, queries), 0)
    mixed = jnp.where(row < HD, done[0][1] / done[0][0], done[1][1] / done[1][0]).T
    of_ref[...] = mixed
    o_ref[...] = mixed.astype(BF)
    for h in range(2):
        lse_ref[0, h : h + 1, :] = peaks[h] + jnp.log2(done[h][0])

def attention_fwd(q, kv, tile):
    queries, width = q.shape; keys = kv.shape[1]
    pairs = width // PAIR
    return pl.pallas_call(
        functools.partial(attn_fwd_kernel, tile),
        grid=(pairs,),
        in_specs=[pl.BlockSpec((queries, PAIR), lambda i: (0, i)), pl.BlockSpec((2, keys, PAIR), lambda i: (0, 0, i))],
        out_specs=[pl.BlockSpec((queries, PAIR), lambda i: (0, i)), pl.BlockSpec((queries, PAIR), lambda i: (0, i)), pl.BlockSpec((1, 2, queries), lambda i: (i, 0, 0))],
        out_shape=[jax.ShapeDtypeStruct((queries, width), BF), jax.ShapeDtypeStruct((queries, width), F32), jax.ShapeDtypeStruct((pairs, 2, queries), F32)],
        scratch_shapes=[pltpu.VMEM((2, keys, queries), F32)],
        compiler_params=pltpu.CompilerParams(vmem_limit_bytes=VMEM_LIMIT),
        cost_estimate=COST,
    )(q, kv)

def attn_bwd_kernel(tile, q_ref, kv_ref, g_ref, of_ref, lse_ref, dq_ref, dkv_ref, dqt_ref):
    queries = q_ref.shape[0]; keys = kv_ref.shape[1]
    scale = HD ** -0.5
    qs = lane_masked(q_ref[...]); gs = lane_masked(g_ref[...])
    prod = g_ref[...].astype(F32) * of_ref[...]
    which = lax.broadcasted_iota(jnp.int32, (8, PAIR), 0); lane = lax.broadcasted_iota(jnp.int32, (8, PAIR), 1)
    picks = jnp.where(lane // HD == which, 1.0, 0.0)
    deltas = lax.dot_general(picks, prod, (((1,), (1,)), ((), ())), precision=lax.Precision.HIGHEST, preferred_element_type=F32)
    dqt_ref[...] = jnp.zeros_like(dqt_ref)
    def step(t, carry):
        at = pl.ds(pl.multiple_of(t * tile, tile), tile)
        k_t = kv_ref[0, at, :]; v_t = kv_ref[1, at, :]
        dk = jnp.zeros((tile, PAIR), F32); dv = jnp.zeros((tile, PAIR), F32)
        for h in range(2):
            p = jnp.exp2(dot_nt(k_t, qs[h]) * (scale * LOG2E) - lse_ref[0, h : h + 1, :])
            dp = dot_nt(v_t, gs[h])
            ds = (p * (dp - deltas[h : h + 1, :])).astype(BF)
            dv = dv + dot_nn(p.astype(BF), gs[h])
            dk = dk + dot_nn(ds, qs[h])
            dqt_ref[h] += dot_tn(k_t, ds)
        dkv_ref[0, at, :] = (dk * scale).astype(BF)
        dkv_ref[1, at, :] = dv.astype(BF)
        return carry
    lax.fori_loop(0, keys // tile, step, 0)
    row = lax.broadcasted_iota(jnp.int32, (PAIR, queries), 0)
    dq_ref[...] = (jnp.where(row < HD, dqt_ref[0], dqt_ref[1]).T * scale).astype(BF)

def attention_bwd(q, kv, grad, mixed, lse, tile):
    queries, width = q.shape; keys = kv.shape[1]
    pairs = width // PAIR
    qspec = pl.BlockSpec((queries, PAIR), lambda i: (0, i)); kspec = pl.BlockSpec((2, keys, PAIR), lambda i: (0, 0, i))
    return pl.pallas_call(
        functools.partial(attn_bwd_kernel, tile),
        grid=(pairs,),
        in_specs=[qspec, kspec, qspec, qspec, pl.BlockSpec((1, 2, queries), lambda i: (i, 0, 0))],
        out_specs=[qspec, kspec],
        out_shape=[jax.ShapeDtypeStruct((queries, width), BF), jax.ShapeDtypeStruct((2, keys, width), BF)],
        scratch_shapes=[pltpu.VMEM((2, PAIR, queries), F32)],
        compiler_params=pltpu.CompilerParams(vmem_limit_bytes=VMEM_LIMIT),
        cost_estimate=COST,
    )(q, kv, grad, mixed, lse)


def split(value):
    high = value.astype(BF)
    return high, (value - high.astype(F32)).astype(BF)

def tile_rows(size, other, index):
    if not other:
        return slice(index * size, (index + 1) * size), slice(0, size)
    half = len(PAIRS) // 2
    at = len(PAIRS) * other + index % half * size
    return slice(at, at + size), slice(index // half * size, (index // half + 1) * size)


def slab_rows(grad, mom, factor, period, count):
    row = lax.rem(lax.broadcasted_iota(jnp.int32, (grad.shape[0], 1), 0), period)
    scale = jnp.where(row < count, factor, 0.0)
    return MOMENTUM * mom.astype(F32) + scale * grad


def gram_kernel(
    periods, counts_ref, factor_ref, big_grad, big_mom, small_grad, small_mom, keep_ref, send_ref, out_ref
):
    for k, (grad, mom) in enumerate(((big_grad, big_mom), (small_grad, small_mom))):
        rows = slab_rows(grad[...], mom[...], factor_ref[0], periods[k], counts_ref[k])
        size = rows.shape[1] // BLOCKS
        high, rest = split(rows)
        for index, (i, j) in enumerate(PAIRS):
            a, b = slice(i * size, (i + 1) * size), slice(j * size, (j + 1) * size)
            tile = dot_tn(high[:, a], high[:, b]) + (
                dot_tn(high[:, a], rest[:, b]) + dot_tn(rest[:, a], high[:, b])
            )
            at, cols = tile_rows(size, k * big_grad.shape[1] // BLOCKS, index)
            out_ref[at, cols] = tile
    cols = keep_ref.shape[1]
    first = counts_ref[2] == 0
    left, right = out_ref[:, :cols], out_ref[:, cols:]
    keep_ref[...] = jnp.where(first, left, right)
    send_ref[...] = jnp.where(first, right, left)


def packed_gram(periods, counts, factor, slabs):
    n, m = slabs[0].shape[1], slabs[2].shape[1]
    rows = len(PAIRS) * (n // BLOCKS) + len(PAIRS) // 2 * (m // BLOCKS)
    cols = n // BLOCKS
    return pl.pallas_call(
        functools.partial(gram_kernel, periods),
        in_specs=[pl.BlockSpec(memory_space=pltpu.SMEM)] * 2
        + [pl.BlockSpec(memory_space=pltpu.VMEM)] * 4,
        out_shape=[jax.ShapeDtypeStruct((rows, cols // 2), F32)] * 2,
        scratch_shapes=[pltpu.VMEM((rows, cols), F32)],
        compiler_params=pltpu.CompilerParams(vmem_limit_bytes=VMEM_LIMIT),
        cost_estimate=COST,
    )(counts, factor, *slabs)


class Square:
    def __init__(self, refs, blocks):
        self.full, self.gram, self.poly, self.prod, self.temp = refs
        self.blocks = blocks

def put(ref, rows, cols, value):
    high, rest = split(value)
    ref[0, rows, cols] = high
    ref[1, rows, cols] = rest

def product(left, right, blocks, store):
    n = left.shape[1]
    size = n // blocks
    for j in range(blocks):
        rows, cols = slice(0, (j + 1) * size), slice(j * size, (j + 1) * size)
        tile = dot_nn(left[0, rows, :], right[0, :, cols]) + (
            dot_nn(left[0, rows, :], right[1, :, cols]) + dot_nn(left[1, rows, :], right[0, :, cols])
        )
        for i in range(j + 1):
            a = slice(i * size, (i + 1) * size)
            block = tile[a]
            store(a, cols, block)
            if i != j:
                store(cols, a, block.T)

def make_poly(sq):
    n = sq.full.shape[0]
    def store(rows, cols, block):
        value = NS_C * block + NS_B * sq.full[rows, cols]
        if rows == cols:
            r = lax.broadcasted_iota(jnp.int32, block.shape, 0); c = lax.broadcasted_iota(jnp.int32, block.shape, 1)
            value = value + jnp.where(r == c, NS_A, 0.0)
        put(sq.poly, rows, cols, value)
    product(sq.gram, sq.gram, sq.blocks, store)

def next_gram(sq):
    product(sq.poly, sq.gram, sq.blocks, lambda r, c, b: put(sq.temp, r, c, b))
    def store(r, c, b):
        sq.full[r, c] = b
        put(sq.gram, r, c, b)
    product(sq.temp, sq.poly, sq.blocks, store)

def next_product(sq):
    product(sq.poly, sq.prod, sq.blocks, lambda r, c, b: put(sq.temp, r, c, b))
    sq.prod[...] = sq.temp[...]

def ortho_kernel(
    periods, counts_ref, factor_ref, mine_ref, other_ref, big_grad, big_mom, small_grad, small_mom,
    big_out, small_out, packed_ref, *refs,
):
    squares = [Square(refs[:5], BLOCKS), Square(refs[5:], 1)]
    cols = mine_ref.shape[1]
    first = counts_ref[2] == 0
    packed_ref[:, :cols] = jnp.where(first, mine_ref[...], other_ref[...])
    packed_ref[:, cols:] = jnp.where(first, other_ref[...], mine_ref[...])
    scales = []
    for sq, other in zip(squares, (0, big_grad.shape[1] // BLOCKS)):
        size = sq.full.shape[0] // BLOCKS
        r = lax.broadcasted_iota(jnp.int32, (size, size), 0)
        c = lax.broadcasted_iota(jnp.int32, (size, size), 1)
        diag = jnp.zeros((size, size), F32)
        for index, (i, j) in enumerate(PAIRS):
            if i == j:
                diag = diag + jnp.where(r == c, packed_ref[tile_rows(size, other, index)], 0.0)
        trace = jnp.sum(jnp.sum(diag, 0, keepdims=True), 1, keepdims=True)
        scale = 1.0 / (jnp.sqrt(trace) + 1e-07)
        scales.append(scale)
        for index, (i, j) in enumerate(PAIRS):
            tile = packed_ref[tile_rows(size, other, index)] * (scale * scale)
            a, b = slice(i * size, (i + 1) * size), slice(j * size, (j + 1) * size)
            sq.full[a, b] = tile
            put(sq.gram, a, b, tile)
            if i != j:
                sq.full[b, a] = tile.T
                put(sq.gram, b, a, tile.T)
    for sq in squares:
        make_poly(sq)
    for sq in squares:
        sq.prod[...] = sq.poly[...]
        next_gram(sq)
    def step(_, carry):
        for sq in squares: make_poly(sq)
        for sq in squares: next_product(sq)
        for sq in squares: next_gram(sq)
        return carry
    lax.fori_loop(1, NS_STEPS - 1, step, 0)
    for sq in squares: make_poly(sq)
    for sq in squares: next_product(sq)
    slabs = ((big_grad, big_mom, big_out), (small_grad, small_mom, small_out))
    for k, (sq, scale, (grad, mom, out)) in enumerate(zip(squares, scales, slabs)):
        rows = slab_rows(grad[...], mom[...], factor_ref[0], periods[k], counts_ref[k])
        high, rest = split(rows * scale)
        out[...] = (
            dot_nn(high, sq.prod[0]) + (dot_nn(high, sq.prod[1]) + dot_nn(rest, sq.prod[0]))
        ).astype(BF)


def orthogonal(periods, counts, factor, mine, other, slabs):
    def scratch(n):
        return [pltpu.VMEM((n, n), F32)] + [pltpu.VMEM((2, n, n), BF)] * 4

    big, small = slabs[0], slabs[2]
    return pl.pallas_call(
        functools.partial(ortho_kernel, periods),
        in_specs=[pl.BlockSpec(memory_space=pltpu.SMEM)] * 2
        + [pl.BlockSpec(memory_space=pltpu.VMEM)] * 6,
        out_shape=[jax.ShapeDtypeStruct(big.shape, BF), jax.ShapeDtypeStruct(small.shape, BF)],
        scratch_shapes=[pltpu.VMEM((mine.shape[0], 2 * mine.shape[1]), F32)]
        + scratch(big.shape[1])
        + scratch(small.shape[1]),
        compiler_params=pltpu.CompilerParams(vmem_limit_bytes=VMEM_LIMIT),
        cost_estimate=COST,
    )(counts, factor, mine, other, *slabs)


def call(kernel, outs, args, flops, smem=0):
    return pl.pallas_call(
        kernel,
        in_specs=[pl.BlockSpec(memory_space=pltpu.SMEM)] * smem
        + [pl.BlockSpec(memory_space=pltpu.VMEM)] * (len(args) - smem),
        out_specs=[pl.BlockSpec(memory_space=pltpu.VMEM)] * len(outs),
        out_shape=[jax.ShapeDtypeStruct(shape, kind) for shape, kind in outs],
        compiler_params=pltpu.CompilerParams(vmem_limit_bytes=VMEM_LIMIT),
        cost_estimate=COST,
    )(*args)


def vec_at(vec_ref, name):
    offset, extent = vector_layout()[name]
    return vec_ref[:, offset : offset + extent]


def head_masks(value):
    lane = lax.broadcasted_iota(jnp.int32, value.shape, 1) // HD
    return [jnp.where(lane == h, value, jnp.zeros_like(value)) for h in range(value.shape[1] // HD)]


def small_probs(queries, keys, vis):
    scores = dot_nt(queries, keys) * HD**-0.5
    column = lax.broadcasted_iota(jnp.int32, scores.shape, 1)
    scores = jnp.where(column < vis, scores, -jnp.inf)
    exp_scores = jnp.exp(scores - jnp.max(scores, -1, keepdims=True))
    return exp_scores / jnp.sum(exp_scores, -1, keepdims=True)


def enc_attention_kernel(
    vis, clips, start_ref, pos_ref, vec_ref, w_ref, qb_ref, vb_ref, wout_ref,
    stream_ref, hid_ref, qkv_ref, attn_ref, part_ref,
):
    stream = start_ref[...] + vec_at(vec_ref, "emb_b") + pos_ref[...]
    stream_ref[...] = stream
    hid = low(layer_norm(stream, vec_at(vec_ref, "eln1_g"), vec_at(vec_ref, "eln1_b"))[0])
    hid_ref[...] = hid
    qkv_ref[0] = low(dot_nt(hid, w_ref[0]) + qb_ref[...])
    qkv_ref[1] = low(dot_nt(hid, w_ref[1]))
    qkv_ref[2] = low(dot_nt(hid, w_ref[2]) + vb_ref[...])
    rows = stream.shape[0] // clips
    for clip in range(clips):
        at = slice(clip * rows, (clip + 1) * rows)
        keys = qkv_ref[1, at, :]
        mixed = 0.0
        for queries, values in zip(head_masks(qkv_ref[0, at, :]), head_masks(qkv_ref[2, at, :])):
            mixed = mixed + dot_nn(low(small_probs(queries, keys, vis)), values)
        attn_ref[at, :] = low(mixed)
    part_ref[...] = low(dot_nn(attn_ref[...], wout_ref[...]))


def enc_units_kernel(
    stream_ref, total_ref, more_ref, vec_ref, wup_ref, upb_ref, wdown_ref,
    middle_ref, hid_ref, upper_ref, active_ref, part_ref,
):
    middle = stream_ref[...] + (total_ref[...].astype(F32) + more_ref[...].astype(F32)) + vec_at(vec_ref, "eout_b")
    middle_ref[...] = middle
    hid = low(layer_norm(middle, vec_at(vec_ref, "eln2_g"), vec_at(vec_ref, "eln2_b"))[0])
    hid_ref[...] = hid
    upper = dot_nt(hid, wup_ref[...]) + upb_ref[...]
    upper_ref[...] = upper
    active = low(gelu_value(upper))
    active_ref[...] = active
    part_ref[...] = low(dot_nn(active, wdown_ref[...]))


def pick_matrix(own, padded, first, shown_ref):
    row = lax.broadcasted_iota(jnp.int32, (own, padded), 0) + first
    return (row == shown_ref[...]).astype(F32)


def bridge_kernel(
    own, where_ref, middle_ref, total_ref, more_ref, vec_ref, link_ref, w_ref, shown_ref, pos_ref,
    result_ref, dstream_ref, hid_ref, q_ref, kv_ref,
):
    result_ref[...] = middle_ref[...] + (total_ref[...].astype(F32) + more_ref[...].astype(F32)) + vec_at(vec_ref, "edown_b")
    padded = shown_ref.shape[1]
    mine = result_ref[pl.ds(pl.multiple_of(where_ref[0] * padded, padded), padded), :]
    final = low(layer_norm(mine, vec_at(vec_ref, "elnf_g"), vec_at(vec_ref, "elnf_b"))[0])
    latent = dot_nn(final, link_ref[...]) + vec_at(vec_ref, "in_b")
    parts = []
    for _ in range(3):
        parts.append(low(latent))
        latent = latent - parts[-1].astype(F32)
    tile = pos_ref.shape[0] // 7

    def step(t, carry):
        first = pl.multiple_of(t * tile, tile)
        at = pl.ds(first, tile)
        pick = pick_matrix(tile, padded, where_ref[1] * own + first, shown_ref)
        chosen = low(pick)
        value = (dot_nn(chosen, parts[0]) + dot_nn(chosen, parts[1])) + dot_nn(chosen, parts[2])
        hidden = 1.0 - jnp.sum(pick, -1, keepdims=True)
        value = value + hidden * vec_at(vec_ref, "mask") + pos_ref[at, :]
        dstream_ref[at, :] = value
        hid_ref[at, :] = low(
            layer_norm(value, vec_at(vec_ref, "dln1_g"), vec_at(vec_ref, "dln1_b"))[0]
        )
        return carry

    lax.fori_loop(0, 7, step, 0)
    hid = hid_ref[...]
    width = hid.shape[1]
    q_ref[...] = low(dot_nt(hid, w_ref[:width, :]) + vec_at(vec_ref, "dq_b"))
    kv_ref[0] = low(dot_nt(hid, w_ref[width : 2 * width, :]))
    kv_ref[1] = low(dot_nt(hid, w_ref[2 * width :, :]) + vec_at(vec_ref, "dv_b"))


def bridge_back_kernel(
    own, where_ref, gq_ref, gkv_ref, got_ref, hid_ref, w_ref, dstream_ref, mid_ref, vec_ref, shown_ref,
    gw_ref, latent_ref, sums_ref, hgrad_ref,
):
    width = gq_ref.shape[1]
    gk = low(gkv_ref[0].astype(F32) + got_ref[0].astype(F32))
    gv = low(gkv_ref[1].astype(F32) + got_ref[1].astype(F32))
    hid = hid_ref[...]
    hgrad = 0.0
    for k, grad in enumerate((gq_ref[...], gk, gv)):
        at = slice(k * width, (k + 1) * width)
        gw_ref[at, :] = low(dot_tn(grad, hid))
        hgrad = hgrad + dot_nn(grad, w_ref[at, :])
    sums_ref[...] = jnp.zeros_like(sums_ref)
    hgrad_ref[...] = hgrad
    sums_ref[0:1, :] = col_sum(gq_ref[...].astype(F32))
    sums_ref[1:2, :] = col_sum(gv.astype(F32))
    latent_ref[...] = jnp.zeros_like(latent_ref)
    padded = shown_ref.shape[1]
    tile = own // 7
    gain = vec_at(vec_ref, "dln1_g")

    def step(t, carry):
        first = pl.multiple_of(t * tile, tile)
        at = pl.ds(first, tile)
        saved = layer_norm(dstream_ref[at, :], gain, gain)[1]
        sgrad, gain_grad, bias_grad = norm_back(hgrad_ref[at, :], saved, gain)
        din = sgrad + mid_ref[at, :]
        pick = pick_matrix(tile, padded, where_ref[1] * own + first, shown_ref)
        hidden = 1.0 - jnp.sum(pick, -1, keepdims=True)
        sums_ref[2:3, :] += gain_grad
        sums_ref[3:4, :] += bias_grad
        sums_ref[4:5, :] += col_sum(hidden * din)
        chosen = low(pick)
        high = low(din)
        rest = low(din - high.astype(F32))
        latent_ref[...] += dot_tn(chosen, high) + dot_tn(chosen, rest)
        return carry

    lax.fori_loop(0, 7, step, 0)


def enc_units_back_kernel(
    latent_ref, result_ref, vec_ref, link_ref, wdown_ref, wup_ref, upper_ref, active_ref, hid_ref,
    glink_ref, grad_ref, gdown_ref, gup_ref, part_ref, sums_ref,
):
    sums_ref[...] = jnp.zeros_like(sums_ref)
    latent = latent_ref[...]
    gain = vec_at(vec_ref, "elnf_g")
    final, saved = layer_norm(result_ref[...], gain, vec_at(vec_ref, "elnf_b"))
    glink_ref[...] = low(dot_tn(low(final), latent))
    grad, gain_grad, bias_grad = norm_back(dot_nt(latent, link_ref[...]), saved, gain)
    grad_ref[...] = grad
    sums_ref[0:1, : latent.shape[1]] = col_sum(latent.astype(F32))
    sums_ref[1:2, :] = gain_grad
    sums_ref[2:3, :] = bias_grad
    sums_ref[3:4, :] = col_sum(grad)
    down = low(grad)
    gdown_ref[...] = low(dot_tn(active_ref[...], down))
    upper = low(dot_nt(down, wdown_ref[...]) * gelu_slope(upper_ref[...]))
    sums_ref[4:5, :] = col_sum(upper.astype(F32))
    part_ref[...] = low(dot_nn(upper, wup_ref[...]))
    gup_ref[...] = low(dot_tn(upper, hid_ref[...]))


def enc_attention_back_kernel(
    vis, clips, total_ref, more_ref, grad_ref, middle_ref, vec_ref, attn_ref, wout_ref, qkv_ref, w_ref, hid_ref,
    mid_ref, gout_ref, gqkv_ref, part_ref, sums_ref, dqkv_ref,
):
    sums_ref[...] = jnp.zeros_like(sums_ref)
    gain = vec_at(vec_ref, "eln2_g")
    saved = layer_norm(middle_ref[...], gain, gain)[1]
    mid, gain_grad, bias_grad = norm_back((total_ref[...].astype(F32) + more_ref[...].astype(F32)), saved, gain)
    mid = mid + grad_ref[...]
    mid_ref[...] = mid
    sums_ref[0:1, :] = gain_grad
    sums_ref[1:2, :] = bias_grad
    sums_ref[2:3, :] = col_sum(mid)
    out = low(mid)
    gout_ref[...] = low(dot_tn(attn_ref[...], out))
    attn_grad = low(dot_nt(out, wout_ref[...]))
    rows = mid.shape[0] // clips
    for clip in range(clips):
        at = slice(clip * rows, (clip + 1) * rows)
        queries, keys, values = (head_masks(qkv_ref[k, at, :]) for k in range(3))
        all_keys, all_values = qkv_ref[1, at, :], qkv_ref[2, at, :]
        grads = head_masks(attn_grad[at, :])
        dq = dk = dv = 0.0
        for query, key, grad in zip(queries, keys, grads):
            prob = small_probs(query, all_keys, vis)
            dprob = dot_nt(grad, all_values)
            product = prob * dprob
            dscore = low(product - prob * jnp.sum(product, -1, keepdims=True))
            dv = dv + dot_tn(low(prob), grad)
            dq = dq + dot_nn(dscore, key)
            dk = dk + dot_tn(dscore, query)
        dqkv_ref[0, at, :] = low(dq * HD**-0.5)
        dqkv_ref[1, at, :] = low(dk * HD**-0.5)
        dqkv_ref[2, at, :] = low(dv)
    width = attn_ref.shape[1]
    sums_ref[3:4, :width] = col_sum(dqkv_ref[0].astype(F32))
    sums_ref[4:5, :width] = col_sum(dqkv_ref[2].astype(F32))
    part = 0.0
    for k in range(3):
        part = part + dot_nn(dqkv_ref[k], w_ref[k])
        gqkv_ref[k] = low(dot_tn(dqkv_ref[k], hid_ref[...]))
    part_ref[...] = low(part)


def enc_start_back_kernel(total_ref, more_ref, mid_ref, stream_ref, vec_ref, pix_ref, gembed_ref, sums_ref):
    sums_ref[...] = jnp.zeros_like(sums_ref)
    gain = vec_at(vec_ref, "eln1_g")
    saved = layer_norm(stream_ref[...], gain, gain)[1]
    grad, gain_grad, bias_grad = norm_back((total_ref[...].astype(F32) + more_ref[...].astype(F32)), saved, gain)
    grad = grad + mid_ref[...]
    sums_ref[0:1, :] = gain_grad
    sums_ref[1:2, :] = bias_grad
    sums_ref[2:3, :] = col_sum(grad)
    gembed_ref[...] = low(dot_tn(pix_ref[...], low(grad)))


def group_total(keep, send):
    mine = keep + narrow_flip(send, 1)
    rows = mine.shape[0] // 2
    one, two = mine[:rows], mine[rows:]
    bits = []
    bit = 1
    while bit < wide_digits(lax.axis_size(WD))[-1][0]:
        bits.append(bit)
        bit *= 2
    for bit in bits:
        one = one + wide_flip(one, bit)
    two = two + narrow_flip(two, 2)
    one = one + narrow_flip(one, 2)
    for bit in bits:
        two = two + wide_flip(two, bit)
    mine = jnp.concatenate([one, two], 0)
    return mine, narrow_flip(mine, 1)


def adam_update(weight, first, second, gradient, rate, decay):
    first_new = BETA_ONE * first + (1.0 - BETA_ONE) * gradient
    second_new = BETA_TWO * second + (1.0 - BETA_TWO) * gradient * gradient
    direction = (
        first_new
        / (1.0 - BETA_ONE**STEP)
        / (jnp.sqrt(second_new / (1.0 - BETA_TWO**STEP)) + EPS_ADAM)
    )
    return (first_new, second_new, weight - rate * (direction + decay * weight))


def pad_rows(value, rows, axis):
    if value.shape[axis] == rows:
        return value
    widths = [(0, 0)] * value.ndim
    widths[axis] = (0, rows - value.shape[axis])
    return jnp.pad(value, widths)


def per_device(
    pixels,
    visible,
    masked,
    groups,
    enc_qkv,
    enc_qkv_mom,
    enc_out,
    enc_out_mom,
    enc_up,
    enc_up_mom,
    enc_down,
    enc_down_mom,
    dec_qkv,
    dec_qkv_mom,
    dec_out,
    dec_out_mom,
    dec_up,
    dec_up_mom,
    dec_down,
    dec_down_mom,
    embed,
    embed_m,
    embed_v,
    enc_to_dec,
    enc_to_dec_m,
    enc_to_dec_v,
    head,
    head_m,
    head_v,
    vectors,
    vectors_m,
    vectors_v,
):
    wide = lax.axis_size(WD)
    me = lax.axis_index(NR)
    half, clip = me % 2, me // 2
    slow = wide_digits(wide)[-1]
    fast = slow[0]
    plane = place_in(slow)
    clips, vis = visible.shape
    tubs = pixels.shape[1]
    own = tubs // 2

    n_up = enc_up.shape[1]
    n_q = enc_qkv.shape[2]
    n_out = enc_out.shape[0]
    n_emb = embed.shape[0] // QN
    n_link = enc_to_dec.shape[0] * DD // D // QN
    m_up = dec_up.shape[1]
    m_qkv = dec_qkv.shape[1]
    m_out = dec_out.shape[0]
    m_head = head.shape[0] * (PIX // DD)

    up_rows, down_rows = enc_up.T, enc_down
    qkv_rows = jnp.swapaxes(enc_qkv, 1, 2).reshape(3 * n_q, D)
    dqkv_rows, dup_rows = dec_qkv.T, dec_up.T
    head_rows = head.reshape(m_head, DD)
    emb_cols = lax.dynamic_slice_in_dim(embed, me * (D // QN), D // QN, 1)
    m_link = enc_to_dec.shape[0] // QN
    link_rows = lax.dynamic_slice_in_dim(enc_to_dec, me * m_link, m_link, 0)
    pack_b = jnp.concatenate([low(emb_cols).reshape(n_emb, D), low(qkv_rows), low(enc_out)], 0)
    pack_c = low(jnp.concatenate([up_rows, down_rows], 0))
    pack_d = low(
        jnp.concatenate([dup_rows, dqkv_rows, dec_out, dec_down, head_rows, link_rows], 0)
    )
    pack_d = narrow_pair(pack_d, 2)
    line_b = slow_pieces(pack_b)
    pieces_b = all_pieces(line_b)
    came = tuple(line_b.values())
    pack_c, pack_d, vis_now, _ = lax.optimization_barrier((pack_c, pack_d, visible, came))
    line_c = slow_pieces(pack_c)
    full_b = assemble(pieces_b)
    pieces_c = all_pieces(tied(line_c, full_b))
    full_c = assemble(pieces_c)
    line_d = slow_pieces(after(pack_d, tuple(pieces_c.values())))
    embed_w = full_b[:, :n_emb].reshape(PIX, D // QN)
    w_qkv = full_b[:, n_emb : n_emb + 3 * n_q].reshape(wide, 3, n_q, D)
    w_qkv = jnp.swapaxes(w_qkv, 0, 1).reshape(3, wide * n_q, D)
    w_out = full_b[:, n_emb + 3 * n_q :].reshape(wide * n_out, D)
    w_up = full_c[:, :n_up].reshape(wide * n_up, D)
    w_down = full_c[:, n_up:].reshape(wide * n_up, D)
    table = vector_layout()

    def vec_of(name):
        offset, extent = table[name]
        return vectors[offset : offset + extent]

    def share_of(name):
        offset, extent = table[name]
        share = extent // QN
        return lax.dynamic_slice_in_dim(vectors, offset + me * share, share)[None, :]

    grads = {}

    padded = -(-vis // 16) * 16
    rows = clips * padded
    shown = jnp.pad(visible, ((0, 0), (0, padded - vis)), constant_values=-1)
    vis_rows = shown.reshape(rows)
    tube_ids = jnp.arange(tubs, dtype=jnp.int32)
    vis_pix = mm(low(vis_rows[:, None] == tube_ids[None, :]), pixels[0]).astype(BF)
    vec_row = vectors[None, :]
    now_rows = jnp.pad(vis_now, ((0, 0), (0, padded - vis)), constant_values=-1).reshape(rows)
    vis_table = sinusoid(now_rows, D)
    start = mm(vis_pix, embed_w)
    start = both(start, narrow_flip(start, 2), clip, 1)
    start = both(start, narrow_flip(start, 1), half, 2).reshape(rows, D)
    units = D // QN * 4
    stream, hid1, eqkv, eattn, part = call(
        functools.partial(enc_attention_kernel, vis, clips),
        [((rows, D), F32), ((rows, D), BF), ((3, rows, D // QN), BF), ((rows, D // QN), BF), ((rows, D), BF)],
        [start, vis_table, vec_row, w_qkv, share_of("eq_b"), share_of("ev_b"), w_out],
        2 * rows * D * D,
    )
    own_pix = after(lax.dynamic_slice_in_dim(pixels[0], half * own, own, 0), part)
    targets = group_targets(own_pix, groups)
    own_pos = after(half * own + jnp.arange(own, dtype=jnp.int32), part)
    own_table = sinusoid(own_pos, DD)
    parts = narrow_parts(part)
    pieces_d = all_pieces(tied(line_d, parts[1]))
    middle, hid2, upper, active, part = call(
        enc_units_kernel,
        [((rows, D), F32), ((rows, D), BF), ((rows, units), F32), ((rows, units), BF), ((rows, D), BF)],
        [stream, *parts, vec_row, w_up, share_of("eup_b"), w_down],
        4 * rows * D * units,
    )

    parts = narrow_parts(part)
    full_d = narrow_pair(assemble(tied(pieces_d, parts[1])), 1, 2)
    at, taken = 0, []
    for extent in (m_up, m_qkv, m_out, m_up, m_head, m_link):
        taken.append(full_d[:, :, :, at : at + extent].reshape(wide * QN * extent, DD))
        at += extent
    d_up, d_qkv, d_out, d_down, d_head, link_w = taken
    d_head = d_head.reshape(DD, PIX)

    where = jnp.stack([clip, half])
    clip_shown = lax.dynamic_slice_in_dim(shown, clip, 1, 0)
    enc_result, dstream, dh1, dq, dkv = call(
        functools.partial(bridge_kernel, own),
        [((rows, D), F32), ((own, DD), F32), ((own, DD), BF), ((own, DD), BF), ((2, own, DD), BF)],
        [where, middle, *parts, vec_row, link_w, d_qkv, clip_shown, own_table],
        6 * own * DD * DD,
        1,
    )
    pick = own_pos[:, None] == clip_shown
    hidden_row = 1.0 - jnp.sum(pick.astype(F32), -1, keepdims=True)
    all_kv = both(dkv, narrow_flip(dkv, 1), half, 1).reshape(2, tubs, DD)
    def plane_rows(parts):
        return jnp.stack([pad_rows(low(part), parts[0].shape[0], 0) for part in parts], 0)

    late = lax.optimization_barrier(
        (
            (enc_up_mom, enc_qkv_mom, enc_out_mom, enc_down_mom),
            (dec_up_mom, dec_qkv_mom, dec_out_mom, dec_down_mom),
            all_kv,
        )
    )
    (up_mom, qkv_mom, out_mom, down_mom), (dup_mom, dqkv_mom, dout_mom, ddown_mom), all_kv = late
    qkv_mom = jnp.swapaxes(qkv_mom, 1, 2).reshape(3 * n_q, D)
    enc_mom, dec_mom = joined_exchange(
        plane_rows([up_mom.T, qkv_mom, out_mom, down_mom]),
        plane_rows([dup_mom.T, dqkv_mom.T, dout_mom, ddown_mom]),
        slow,
    )

    tile = next(t for t in (224, 112, 16) if tubs % t == 0)
    dattn, mixed, dlog = attention_fwd(dq, all_kv, tile)
    dattn, enc_mom, dec_mom = lax.optimization_barrier((dattn, enc_mom, dec_mom))

    dmiddle = dstream + mm(dattn, d_out) + vec_of("dout_b")
    dh2, dsaved2 = layer_norm(dmiddle, vec_of("dln2_g"), vec_of("dln2_b"))
    dh2 = low(dh2)
    dupper = mm_nt(dh2, d_up) + vec_of("dup_b")
    dactive = low(gelu_value(dupper))
    dresult = dmiddle + mm(dactive, d_down) + vec_of("ddown_b")
    hf, hsaved = layer_norm(dresult, vec_of("dlnf_g"), vec_of("dlnf_b"))
    hf = low(hf)
    predicted = mm(hf, d_head) + vec_of("head_b")
    error = (predicted - targets) * hidden_row
    loss_part = jnp.sum(error * error)
    pred_grad = error * (2.0 / (clips * wide * (tubs - vis) * PIX))

    pred_low = low(pred_grad)
    g_head = mm_tn(hf, pred_low)
    grads["head_b"] = col_sum(pred_grad)
    dgrad, grads["dlnf_g"], grads["dlnf_b"] = norm_back(
        mm_nt(pred_low, d_head), hsaved, vec_of("dlnf_g")
    )
    down_low = low(dgrad)
    g_ddown = mm_tn(dactive, down_low)
    grads["ddown_b"] = col_sum(dgrad)
    upper_low = low(mm_nt(down_low, d_down) * gelu_slope(dupper))
    g_dup = mm_tn(upper_low, dh2)
    grads["dup_b"] = col_sum(upper_low.astype(F32))
    mid_grad, grads["dln2_g"], grads["dln2_b"] = norm_back(
        mm(upper_low, d_up), dsaved2, vec_of("dln2_g")
    )
    mid_grad = mid_grad + dgrad
    out_low = low(mid_grad)
    g_dout = mm_tn(dattn, out_low)
    grads["dout_b"] = col_sum(mid_grad)
    attn_grad = low(mm_nt(out_low, d_out))
    def dec_parts(value, extent):
        return low(value).reshape(4, fast, 2, 2, extent, DD)

    def fast_scatter(value, axis):
        digits = wide_digits(wide)[:-1]
        shape = value.shape
        value = value.reshape(
            shape[:axis] + tuple(radix for _, radix in digits[::-1]) + shape[axis + 1 :]
        )
        for count, digit in enumerate(digits):
            value = line_scatter(value, digit, axis + len(digits) - 1 - count)
        return value

    def half_sum(value, place, axis, bit):
        sent = low(pick_half(value, 1 - place, axis))
        return pick_half(value, place, axis).astype(F32) + narrow_flip(sent, bit).astype(F32)

    cut = m_up - m_qkv
    p_head = dec_parts(g_head.reshape(-1, DD), m_head)
    early = jnp.stack(
        [
            dec_parts(g_dup, m_up),
            jnp.concatenate([dec_parts(g_dout, m_out), p_head[:, :, :, :, cut:]], 4),
            dec_parts(g_ddown, m_up),
        ],
        0,
    )
    early = half_sum(early, half, 4, 1)
    attn_grad, early = lax.optimization_barrier((attn_grad, early))
    early = half_sum(early, clip, 3, 2)
    gq, gkv = attention_bwd(dq, all_kv, attn_grad, mixed, dlog, tile)
    gkv, early = lax.optimization_barrier((gkv, early))
    gkv = gkv.reshape(2, 2, own, DD)
    got = narrow_flip(pick_half(gkv, 1 - half, 1), 1)
    g_dqkv, latent_part, sums, _ = call(
        functools.partial(bridge_back_kernel, own),
        [((3 * DD, DD), BF), ((padded, DD), F32), ((8, DD), F32), ((own, DD), F32)],
        [where, gq, pick_half(gkv, half, 1), got, dh1, d_qkv, dstream, mid_grad, vec_row, clip_shown],
        12 * own * DD * DD,
        1,
    )
    for row, name in enumerate(("dq_b", "dv_b", "dln1_g", "dln1_b", "mask")):
        grads[name] = sums[row]

    late = jnp.concatenate([dec_parts(g_dqkv, m_qkv), p_head[:, :, :, :, :cut]], 4)[None]
    early = fast_scatter(after(early, latent_part), 2)

    latent_pair = low(pair_sum(latent_part))
    latent_low = both(latent_pair, narrow_flip(latent_pair, 2), clip, 0).reshape(rows, DD)
    g_link, egrad, g_down, g_up, part, sums = call(
        enc_units_back_kernel,
        [((D, DD), BF), ((rows, D), F32), ((units, D), BF), ((units, D), BF), ((rows, D), BF), ((8, D), F32)],
        [latent_low, enc_result, vec_row, link_w, w_down, w_up, upper, active, hid2],
        8 * rows * D * units,
    )
    parts = narrow_parts(part)
    g_link, sums, _ = lax.optimization_barrier((g_link, sums, parts[1]))
    grads["in_b"] = sums[0, :DD]
    for row, name in enumerate(("elnf_g", "elnf_b", "edown_b", "eup_b")):
        grads[name] = sums[row + 1]

    def enc_parts(value, extent):
        return low(value).reshape(4, fast, extent, D).transpose(1, 0, 2, 3)

    g_up, g_down, late, _ = lax.optimization_barrier((g_up, g_down, late, parts[0]))
    late = half_sum(late, half, 4, 1)
    sum_up = fast_scatter(enc_parts(g_up, n_up), 0)
    sum_down = fast_scatter(enc_parts(g_down, n_up), 0)
    mid_grad, g_out, g_qkv, part, sums, _ = call(
        functools.partial(enc_attention_back_kernel, vis, clips),
        [((rows, D), F32), ((D // QN, D), BF), ((3, D // QN, D), BF), ((rows, D), BF), ((8, D), F32), ((3, rows, D // QN), BF)],
        [*parts, egrad, middle, vec_row, eattn, w_out, eqkv, w_qkv, hid1],
        4 * rows * D * D,
    )
    for row, name in enumerate(("eln2_g", "eln2_b", "eout_b")):
        grads[name] = sums[row]
    grads["eq_b"], grads["ev_b"] = sums[3, : D // QN], sums[4, : D // QN]
    parts = narrow_parts(part)
    ends_sum = ends_total(joined(sum_up, early[0]), joined(sum_down, early[2]), slow, (0, 3))
    g_embed, sums = call(
        enc_start_back_kernel,
        [((PIX, D), BF), ((8, D), F32)],
        [*parts, mid_grad, stream, vec_row, vis_pix],
        2 * rows * D * PIX,
    )
    for row, name in enumerate(("eln1_g", "eln1_b", "emb_b")):
        grads[name] = sums[row]
    g_embed = pick_half(g_embed.reshape(wide, QN, n_emb, D), me, 1)
    g_link = pick_half(g_link.reshape(wide, QN, n_link, D), me, 1)
    part_qkv = jnp.concatenate([enc_parts(g, n_q) for g in g_qkv], 2)
    part_rest = jnp.concatenate(
        [enc_parts(g_out, n_out), enc_parts(g_embed, n_emb), enc_parts(g_link, n_link)], 2
    )
    longer = max(part_qkv.shape[2], part_rest.shape[2])
    sum_qkv = fast_scatter(pad_rows(part_qkv, longer, 2), 0)
    sum_rest = fast_scatter(pad_rows(part_rest, longer, 2), 0)
    late = fast_scatter(half_sum(after(late, parts[1]), clip, 3, 2), 2)
    middle_sum = ends_total(joined(sum_qkv, late[0]), joined(sum_rest, early[1]), slow, (1, 2))
    enc_ends, dec_ends = parted(ends_sum, n_up)
    enc_middle, dec_middle = parted(middle_sum, longer)
    middle = (plane == 1) | (plane == 2)
    enc_sum = jnp.where(middle, pad_rows(enc_middle, n_up, 1), enc_ends)
    dec_sum = jnp.where(middle, dec_middle, dec_ends)

    leading = jnp.where(me == 0, 1.0, 0.0)

    def spread(share):
        full = jnp.zeros((share.shape[0] * QN,), F32)
        return lax.dynamic_update_slice_in_dim(full, share, me * share.shape[0], 0)

    pieces = []
    for name in table:
        piece = grads[name].reshape(-1)
        if name in ("eq_b", "ev_b", "eup_b"):
            piece = spread(piece)
        elif name[0] == "e" or name == "in_b":
            piece = leading * piece
        pieces.append(piece)
    vec_total = sum_all(jnp.concatenate(pieces + [loss_part[None]]).reshape(1, -1))[0]
    loss_sum = vec_total[-1]
    vec_total = vec_total[:-1]
    squares = jnp.sum(dec_sum * dec_sum) + jnp.sum(enc_sum * enc_sum)
    square_total = sum_tiny(jnp.broadcast_to(squares, (8, 128)))[0, 0]
    grad_norm = jnp.sqrt(square_total + jnp.sum(vec_total * vec_total))
    factor = jnp.minimum(1.0, CLIP_AT / grad_norm)

    counts = jnp.asarray(
        [[n_up, m_up], [3 * n_q, m_qkv], [n_out, m_out], [n_up, m_up]], jnp.int32
    )[plane]
    counts = jnp.concatenate([counts, half[None]])
    slabs = [
        enc_sum.reshape(4 * n_up, D),
        enc_mom.reshape(4 * n_up, D),
        dec_sum.reshape(4 * m_up, DD),
        dec_mom.reshape(4 * m_up, DD),
    ]
    periods = (n_up, m_up)
    mine, other = group_total(*packed_gram(periods, counts, factor[None], slabs))
    enc_back, dec_back, _ = lax.optimization_barrier((enc_sum, dec_sum, grad_norm))
    enc_grad, dec_grad = joined_exchange(low(enc_back), low(dec_back), slow)
    enc_grad, dec_grad = enc_grad.astype(F32) * factor, dec_grad.astype(F32) * factor

    def turned(value):
        return value.T

    def same(value):
        return value

    def unqkv(value):
        return jnp.swapaxes(value.reshape(3, n_q, D), 1, 2)

    rest = enc_grad[2, n_out : n_out + n_emb + n_link]
    rest = narrow_gather(rest)
    embed_grad = rest[:, :n_emb].reshape(embed.shape)
    link_grad = rest[:, n_emb:].reshape(enc_to_dec.shape)
    head_grad = jnp.concatenate([dec_grad[1, m_qkv:], dec_grad[2, m_out:]], 0).reshape(head.shape)
    adam = []
    for weight, first, second, grad, rate, decay in [
        (embed, embed_m, embed_v, embed_grad, RATE_ADAM, DECAY),
        (enc_to_dec, enc_to_dec_m, enc_to_dec_v, link_grad, RATE_ADAM, DECAY),
        (head, head_m, head_v, head_grad, RATE_ADAM, DECAY),
        (vectors, vectors_m, vectors_v, factor * vec_total, RATE_VECTOR, 0.0),
    ]:
        adam += adam_update(weight, first, second, grad, rate, decay)
    entries = [
        (enc_qkv, enc_qkv_mom, enc_grad[1, : 3 * n_q], unqkv, 3 * D),
        (enc_out, enc_out_mom, enc_grad[2, :n_out], same, D),
        (enc_up, enc_up_mom, enc_grad[0], turned, FE),
        (enc_down, enc_down_mom, enc_grad[3], same, FE),
        (dec_qkv, dec_qkv_mom, dec_grad[1, :m_qkv], turned, 3 * DD),
        (dec_out, dec_out_mom, dec_grad[2, :m_out], same, DD),
        (dec_up, dec_up_mom, dec_grad[0], turned, FD),
        (dec_down, dec_down_mom, dec_grad[3], same, FD),
    ]
    moms = [MOMENTUM * mom + side(grad) for _, mom, grad, side, _ in entries]
    mine, moms, adam = lax.optimization_barrier((mine, moms, adam))
    enc_ortho, dec_ortho = orthogonal(periods, counts, factor[None], mine, other, slabs)
    enc_ortho, dec_ortho = joined_exchange(
        enc_ortho.reshape(4, n_up, D), dec_ortho.reshape(4, m_up, DD), slow
    )
    enc_ortho, dec_ortho = enc_ortho.astype(F32), dec_ortho.astype(F32)
    results = [loss_sum, grad_norm]
    orthos = [
        enc_ortho[1, : 3 * n_q],
        enc_ortho[2, :n_out],
        enc_ortho[0],
        enc_ortho[3],
        dec_ortho[1, :m_qkv],
        dec_ortho[2, :m_out],
        dec_ortho[0],
        dec_ortho[3],
    ]
    for (weight, _, _, side, largest), mom, part in zip(entries, moms, orthos):
        step = RATE_MUON * 0.2 * math.sqrt(largest)
        results += [weight * (1.0 - RATE_MUON * DECAY) - step * side(part), mom]
    results += adam
    return tuple(results)


def solution(mesh):
    enc, dec = (NR, WD), (WD, NR)
    muon = [P(None, None, enc), P(enc, None), P(None, enc), P(enc, None)]
    muon += [P(None, dec), P(dec, None), P(None, dec), P(dec, None)]
    pairs = [spec for spec in muon for _ in range(2)]
    adam = [P(WD, None)] * 6 + [P(dec, None)] * 3 + [P()] * 3
    in_specs = [P(WD, None, None), P(WD, None), P(WD, None), P()] + pairs + adam
    out_specs = [P(), P()] + pairs + adam
    return jax.shard_map(
        per_device,
        mesh=mesh,
        in_specs=tuple(in_specs),
        out_specs=tuple(out_specs),
        check_vma=False,
    )
```

```python
import functools
import math

import jax
import jax.numpy as jnp
from jax import lax
from jax.experimental import pallas as pl
from jax.experimental.pallas import tpu as pltpu
from jax.sharding import PartitionSpec as P

WD = "wide"
NR = "narrow"
D = 768
HD = 64
FE = 3072
DD = 384
FD = 1536
PIX = 1536
GROUPS = 3
NS_STEPS = 5
STEP = 10
QN = 4

EPS_NORM = 1e-06
TARGET_EPS = 1.0
CLIP_AT = 0.0002
MOMENTUM = 0.95
RATE_MUON = 0.15
RATE_ADAM = 0.02
RATE_VECTOR = 0.2
DECAY = 0.05
BETA_ONE = 0.9
BETA_TWO = 0.95
EPS_ADAM = 1e-12
NS_A = 3.4445
NS_B = -4.775
NS_C = 2.0315
ROOT_HALF = 0.7071067811865476
INV_ROOT_TWO_PI = 0.3989422804014327
BF = jnp.bfloat16
F32 = jnp.float32
LOG2E = 1.4426950408889634
PAIR = 2 * HD
BLOCKS = 3
PAIRS = [(i, j) for i in range(BLOCKS) for j in range(i, BLOCKS)]
VMEM_LIMIT = 56 * 2**20
COST = pl.CostEstimate(flops=2000000000, bytes_accessed=1000, transcendentals=0)

BLOCK = ("ln1_g", "ln1_b", "q_b", "v_b", "out_b", "ln2_g", "ln2_b", "up_b", "down_b")


def vector_layout():
    entries = []
    for side, width, hidden in (("e", D, FE), ("d", DD, FD)):
        if side == "d":
            entries += [("in_b", DD), ("mask", DD)]
        entries += [(side + name, hidden if name == "up_b" else width) for name in BLOCK]
        entries += [(side + "lnf_g", width), (side + "lnf_b", width)]
        if side == "e":
            entries += [("emb_b", D)]
    entries += [("head_b", PIX)]
    table, offset = {}, 0
    for name, extent in entries:
        table[name] = (offset, extent)
        offset += extent
    return table


def wide_digits(count):
    digits, rest, step = [], count, 1
    while rest > 1:
        radix = 2 if not digits or rest % 4 else 4
        digits.append((step, radix))
        step, rest = step * radix, rest // radix
    return digits


def shift_pairs(count, digit, delta, keep=None):
    step, radix = digit
    pairs = []
    for src in range(count):
        place = src // step % radix
        if 0 <= place + delta < radix and (keep is None or keep(place)):
            pairs.append((src, src + delta * step))
    return pairs


def wide_move(value, digit, delta, keep=None):
    return lax.ppermute(value, WD, shift_pairs(lax.axis_size(WD), digit, delta, keep))


def wide_flip(value, bit):
    count = lax.axis_size(WD)
    return lax.ppermute(value, WD, [(src, src ^ bit) for src in range(count)])


def narrow_flip(value, bit):
    return lax.ppermute(value, NR, [(src, src ^ bit) for src in range(QN)])


def place_in(digit):
    return lax.axis_index(WD) // digit[0] % digit[1]


def pick_half(value, which, axis):
    return lax.dynamic_index_in_dim(value, which, axis, keepdims=False)


def both(mine, theirs, place, axis):
    first = jnp.where(place == 0, mine, theirs)
    second = jnp.where(place == 0, theirs, mine)
    return jnp.stack([first, second], axis)


def in_order(got, place):
    odd, high = place % 2 == 1, place // 2 == 1
    got = [jnp.where(odd, got[k ^ 1], got[k]) for k in range(4)]
    return [jnp.where(high, got[k ^ 2], got[k]) for k in range(4)]


def after(value, *earlier):
    return lax.optimization_barrier((value,) + earlier)[0]


def slow_pieces(block):
    step, radix = wide_digits(lax.axis_size(WD))[-1]
    return {mask * step: wide_flip(block, mask * step) if mask else block for mask in range(radix)}


def all_pieces(pieces):
    pieces = dict(pieces)
    for step, radix in wide_digits(lax.axis_size(WD))[-2::-1]:
        others = [held for held in pieces if held]
        joined = jnp.stack([pieces[held] for held in others], 0)
        for mask in range(1, radix):
            pieces[mask * step] = wide_flip(pieces[0], mask * step)
            moved = wide_flip(joined, mask * step)
            for k, held in enumerate(others):
                pieces[held ^ mask * step] = moved[k]
    return pieces


def assemble(pieces):
    count = lax.axis_size(WD)
    shape = pieces[0].shape
    for digit in wide_digits(count):
        step, radix = digit
        place = place_in(digit)
        joined = {}
        for held in pieces:
            if held // step % radix == 0:
                group = [pieces[held ^ mask * step] for mask in range(radix)]
                if radix == 2:
                    joined[held] = both(group[0], group[1], place, 0)
                else:
                    joined[held] = jnp.stack(in_order(group, place), 0)
        pieces = joined
    return pieces[0].reshape((count,) + shape)


def tied(pieces, *earlier):
    return dict(zip(pieces, lax.optimization_barrier((tuple(pieces.values()),) + earlier)[0]))


def narrow_pair(value, bit, axis=0):
    return both(value, narrow_flip(value, bit), lax.axis_index(NR) // bit % 2, axis)


def narrow_gather(block):
    return narrow_pair(narrow_pair(block, 2), 1, 1).reshape((QN,) + block.shape)


def line_scatter(value, digit, axis):
    place = place_in(digit)
    total = pick_half(value, place, axis).astype(F32)
    for mask in range(1, digit[1]):
        sent = pick_half(value, place ^ mask, axis).astype(BF)
        total = total + wide_flip(sent, mask * digit[0]).astype(F32)
    return total


def slow_exchange(value, digit):
    place = place_in(digit)
    got = [pick_half(value, place, 0)]
    for mask in range(1, digit[1]):
        got.append(wide_flip(pick_half(value, place ^ mask, 0), mask * digit[0]))
    return jnp.stack(in_order(got, place), 0)


def ends_total(one, two, digit, targets):
    place = place_in(digit)
    total = jnp.where(place == targets[0], one, two)
    one, two = low(one), low(two)
    count = lax.axis_size(WD)
    for mask in range(1, 4):
        pairs = [
            (src, src ^ mask * digit[0])
            for src in range(count)
            if (src // digit[0] % digit[1]) ^ mask in targets
        ]
        sent = jnp.where(place ^ mask == targets[0], one, two)
        total = total + lax.ppermute(sent, WD, pairs).astype(F32)
    return total


def joined(big, small):
    rows = small.shape[1] // 2
    return jnp.concatenate([big, jnp.concatenate([small[:, :rows], small[:, rows:]], 2)], 1)


def parted(value, rows):
    small = value[:, rows:]
    width = small.shape[2] // 2
    return value[:, :rows], jnp.concatenate([small[..., :width], small[..., width:]], 1)


def joined_exchange(big, small, digit):
    return parted(slow_exchange(joined(big, small), digit), big.shape[1])


def pair_sum(value):
    return value + narrow_flip(value, 1)


def sum_all(value):
    value = pair_sum(value)
    value = value + narrow_flip(value, 2)
    bit = 1
    while bit < lax.axis_size(WD):
        value = value + wide_flip(value, bit)
        bit *= 2
    return value


def sum_tiny(value):
    me = lax.axis_index(NR)
    parts = in_order([value] + [narrow_flip(value, mask) for mask in range(1, QN)], me)
    value = (parts[0] + parts[1]) + (parts[2] + parts[3])
    for digit in wide_digits(lax.axis_size(WD)):
        if digit[1] == 2:
            value = value + wide_flip(value, digit[0])
        else:
            flips = [wide_flip(value, mask * digit[0]) for mask in range(1, 4)]
            parts = in_order([value] + flips, place_in(digit))
            value = (parts[0] + parts[1]) + (parts[2] + parts[3])
    return value


def narrow_parts(part):
    part = low(part.astype(F32) + narrow_flip(part, 1).astype(F32))
    return [part, narrow_flip(part, 2)]


def sinusoid(positions, extent):
    half_extent = extent // 2
    frequency = jnp.exp(
        jnp.arange(half_extent, dtype=F32) * (-2.0 * math.log(10000.0) / extent)
    )
    angles = positions.astype(F32)[:, None] * frequency[None, :]
    return jnp.concatenate([jnp.sin(angles), jnp.cos(angles)], axis=1)


def low(value):
    return value.astype(BF)


def mm(left, right):
    return jnp.dot(left, right, preferred_element_type=F32)


def mm_tn(left, right):
    return lax.dot_general(left, right, (((0,), (0,)), ((), ())), preferred_element_type=F32)


def mm_nt(left, right):
    return lax.dot_general(left, right, (((1,), (1,)), ((), ())), preferred_element_type=F32)


def col_sum(value):
    return jnp.sum(value, 0, keepdims=True)


def layer_norm(value, gain, bias):
    center = value - jnp.mean(value, -1, keepdims=True)
    inv = lax.rsqrt(jnp.mean(center * center, -1, keepdims=True) + EPS_NORM)
    normed = center * inv
    return (normed * gain + bias, (normed, inv))


def norm_back(grad, saved, gain):
    normed, inv = saved
    grad_n = grad * gain
    grad_in = inv * (
        grad_n
        - jnp.mean(grad_n, -1, keepdims=True)
        - normed * jnp.mean(grad_n * normed, -1, keepdims=True)
    )
    return (grad_in, col_sum(grad * normed), col_sum(grad))


def gelu_value(upper):
    return 0.5 * upper * (1.0 + lax.erf(upper * ROOT_HALF))


def gelu_slope(upper):
    return (
        0.5 * (1.0 + lax.erf(upper * ROOT_HALF))
        + upper * jnp.exp(-0.5 * upper * upper) * INV_ROOT_TWO_PI
    )


def group_targets(pix, groups):
    rows = pix.astype(F32)
    masks = [(groups == g).astype(F32)[None, :] for g in range(GROUPS)]
    per_group = pix.shape[-1] // GROUPS

    def spread(parts):
        return sum(part * mask for part, mask in zip(parts, masks))

    means = [jnp.sum(rows * mask, -1, keepdims=True) / per_group for mask in masks]
    center = rows - spread(means)
    squares = center * center
    scale = [
        lax.rsqrt(jnp.sum(squares * mask, -1, keepdims=True) / per_group + TARGET_EPS)
        for mask in masks
    ]
    return center * spread(scale)


def dot_nn(left, right):
    return jnp.dot(left, right, preferred_element_type=F32)


def dot_tn(left, right):
    return mm_tn(left, right)


def dot_nt(left, right):
    return mm_nt(left, right)


def lane_masked(value):
    lane = lax.broadcasted_iota(jnp.int32, value.shape, 1)
    zero = jnp.zeros_like(value)
    return [jnp.where(lane < HD, value, zero), jnp.where(lane < HD, zero, value)]

def attn_fwd_kernel(tile, q_ref, kv_ref, o_ref, of_ref, lse_ref, s_ref):
    queries = q_ref.shape[0]; keys = kv_ref.shape[1]
    qs = lane_masked(q_ref[...])
    scale = HD ** -0.5 * LOG2E
    def first(t, peaks):
        at = pl.ds(pl.multiple_of(t * tile, tile), tile)
        k_t = kv_ref[0, at, :]
        out = []
        for h in range(2):
            s = dot_nt(k_t, qs[h])
            s_ref[h, at, :] = s
            out.append(jnp.maximum(peaks[h], jnp.max(s, 0, keepdims=True)))
        return tuple(out)
    start = jnp.full((1, queries), -jnp.inf, F32)
    peaks = lax.fori_loop(0, keys // tile, first, (start, start))
    peaks = [p * scale for p in peaks]
    def second(t, carry):
        at = pl.ds(pl.multiple_of(t * tile, tile), tile)
        v_t = kv_ref[1, at, :]
        out = []
        for h in range(2):
            total, mixed = carry[h]
            p = jnp.exp2(s_ref[h, at, :] * scale - peaks[h])
            out.append((total + jnp.sum(p, 0, keepdims=True), mixed + dot_tn(v_t, p.astype(BF))))
        return tuple(out)
    zero = (jnp.zeros((1, queries), F32), jnp.zeros((PAIR, queries), F32))
    done = lax.fori_loop(0, keys // tile, second, (zero, zero))
    row = lax.broadcasted_iota(jnp.int32, (PAIR, queries), 0)
    mixed = jnp.where(row < HD, done[0][1] / done[0][0], done[1][1] / done[1][0]).T
    of_ref[...] = mixed
    o_ref[...] = mixed.astype(BF)
    for h in range(2):
        lse_ref[0, h : h + 1, :] = peaks[h] + jnp.log2(done[h][0])

def attention_fwd(q, kv, tile):
    queries, width = q.shape; keys = kv.shape[1]
    pairs = width // PAIR
    return pl.pallas_call(
        functools.partial(attn_fwd_kernel, tile),
        grid=(pairs,),
        in_specs=[pl.BlockSpec((queries, PAIR), lambda i: (0, i)), pl.BlockSpec((2, keys, PAIR), lambda i: (0, 0, i))],
        out_specs=[pl.BlockSpec((queries, PAIR), lambda i: (0, i)), pl.BlockSpec((queries, PAIR), lambda i: (0, i)), pl.BlockSpec((1, 2, queries), lambda i: (i, 0, 0))],
        out_shape=[jax.ShapeDtypeStruct((queries, width), BF), jax.ShapeDtypeStruct((queries, width), F32), jax.ShapeDtypeStruct((pairs, 2, queries), F32)],
        scratch_shapes=[pltpu.VMEM((2, keys, queries), F32)],
        compiler_params=pltpu.CompilerParams(vmem_limit_bytes=VMEM_LIMIT),
        cost_estimate=COST,
    )(q, kv)

def attn_bwd_kernel(tile, q_ref, kv_ref, g_ref, of_ref, lse_ref, dq_ref, dkv_ref, dqt_ref):
    queries = q_ref.shape[0]; keys = kv_ref.shape[1]
    scale = HD ** -0.5
    qs = lane_masked(q_ref[...]); gs = lane_masked(g_ref[...])
    prod = g_ref[...].astype(F32) * of_ref[...]
    which = lax.broadcasted_iota(jnp.int32, (8, PAIR), 0); lane = lax.broadcasted_iota(jnp.int32, (8, PAIR), 1)
    picks = jnp.where(lane // HD == which, 1.0, 0.0)
    deltas = lax.dot_general(picks, prod, (((1,), (1,)), ((), ())), precision=lax.Precision.HIGHEST, preferred_element_type=F32)
    dqt_ref[...] = jnp.zeros_like(dqt_ref)
    def step(t, carry):
        at = pl.ds(pl.multiple_of(t * tile, tile), tile)
        k_t = kv_ref[0, at, :]; v_t = kv_ref[1, at, :]
        dk = jnp.zeros((tile, PAIR), F32); dv = jnp.zeros((tile, PAIR), F32)
        for h in range(2):
            p = jnp.exp2(dot_nt(k_t, qs[h]) * (scale * LOG2E) - lse_ref[0, h : h + 1, :])
            dp = dot_nt(v_t, gs[h])
            ds = (p * (dp - deltas[h : h + 1, :])).astype(BF)
            dv = dv + dot_nn(p.astype(BF), gs[h])
            dk = dk + dot_nn(ds, qs[h])
            dqt_ref[h] += dot_tn(k_t, ds)
        dkv_ref[0, at, :] = (dk * scale).astype(BF)
        dkv_ref[1, at, :] = dv.astype(BF)
        return carry
    lax.fori_loop(0, keys // tile, step, 0)
    row = lax.broadcasted_iota(jnp.int32, (PAIR, queries), 0)
    dq_ref[...] = (jnp.where(row < HD, dqt_ref[0], dqt_ref[1]).T * scale).astype(BF)

def attention_bwd(q, kv, grad, mixed, lse, tile):
    queries, width = q.shape; keys = kv.shape[1]
    pairs = width // PAIR
    qspec = pl.BlockSpec((queries, PAIR), lambda i: (0, i)); kspec = pl.BlockSpec((2, keys, PAIR), lambda i: (0, 0, i))
    return pl.pallas_call(
        functools.partial(attn_bwd_kernel, tile),
        grid=(pairs,),
        in_specs=[qspec, kspec, qspec, qspec, pl.BlockSpec((1, 2, queries), lambda i: (i, 0, 0))],
        out_specs=[qspec, kspec],
        out_shape=[jax.ShapeDtypeStruct((queries, width), BF), jax.ShapeDtypeStruct((2, keys, width), BF)],
        scratch_shapes=[pltpu.VMEM((2, PAIR, queries), F32)],
        compiler_params=pltpu.CompilerParams(vmem_limit_bytes=VMEM_LIMIT),
        cost_estimate=COST,
    )(q, kv, grad, mixed, lse)


def split(value):
    high = value.astype(BF)
    return high, (value - high.astype(F32)).astype(BF)

def tile_rows(size, other, index):
    if not other:
        return slice(index * size, (index + 1) * size), slice(0, size)
    half = len(PAIRS) // 2
    at = len(PAIRS) * other + index % half * size
    return slice(at, at + size), slice(index // half * size, (index // half + 1) * size)


def slab_rows(grad, mom, factor, period, count):
    row = lax.rem(lax.broadcasted_iota(jnp.int32, (grad.shape[0], 1), 0), period)
    scale = jnp.where(row < count, factor, 0.0)
    return MOMENTUM * mom.astype(F32) + scale * grad


def gram_kernel(
    periods, counts_ref, factor_ref, big_grad, big_mom, small_grad, small_mom, keep_ref, send_ref, out_ref
):
    for k, (grad, mom) in enumerate(((big_grad, big_mom), (small_grad, small_mom))):
        rows = slab_rows(grad[...], mom[...], factor_ref[0], periods[k], counts_ref[k])
        size = rows.shape[1] // BLOCKS
        high, rest = split(rows)
        for index, (i, j) in enumerate(PAIRS):
            a, b = slice(i * size, (i + 1) * size), slice(j * size, (j + 1) * size)
            tile = dot_tn(high[:, a], high[:, b]) + (
                dot_tn(high[:, a], rest[:, b]) + dot_tn(rest[:, a], high[:, b])
            )
            at, cols = tile_rows(size, k * big_grad.shape[1] // BLOCKS, index)
            out_ref[at, cols] = tile
    cols = keep_ref.shape[1]
    first = counts_ref[2] == 0
    left, right = out_ref[:, :cols], out_ref[:, cols:]
    keep_ref[...] = jnp.where(first, left, right)
    send_ref[...] = jnp.where(first, right, left)


def packed_gram(periods, counts, factor, slabs):
    n, m = slabs[0].shape[1], slabs[2].shape[1]
    rows = len(PAIRS) * (n // BLOCKS) + len(PAIRS) // 2 * (m // BLOCKS)
    cols = n // BLOCKS
    return pl.pallas_call(
        functools.partial(gram_kernel, periods),
        in_specs=[pl.BlockSpec(memory_space=pltpu.SMEM)] * 2
        + [pl.BlockSpec(memory_space=pltpu.VMEM)] * 4,
        out_shape=[jax.ShapeDtypeStruct((rows, cols // 2), F32)] * 2,
        scratch_shapes=[pltpu.VMEM((rows, cols), F32)],
        compiler_params=pltpu.CompilerParams(vmem_limit_bytes=VMEM_LIMIT),
        cost_estimate=COST,
    )(counts, factor, *slabs)


class Square:
    def __init__(self, refs, blocks):
        self.full, self.gram, self.poly, self.prod, self.temp = refs
        self.blocks = blocks

def put(ref, rows, cols, value):
    high, rest = split(value)
    ref[0, rows, cols] = high
    ref[1, rows, cols] = rest

def product(left, right, blocks, store):
    n = left.shape[1]
    size = n // blocks
    for j in range(blocks):
        rows, cols = slice(0, (j + 1) * size), slice(j * size, (j + 1) * size)
        tile = dot_nn(left[0, rows, :], right[0, :, cols]) + (
            dot_nn(left[0, rows, :], right[1, :, cols]) + dot_nn(left[1, rows, :], right[0, :, cols])
        )
        for i in range(j + 1):
            a = slice(i * size, (i + 1) * size)
            block = tile[a]
            store(a, cols, block)
            if i != j:
                store(cols, a, block.T)

def make_poly(sq):
    n = sq.full.shape[0]
    def store(rows, cols, block):
        value = NS_C * block + NS_B * sq.full[rows, cols]
        if rows == cols:
            r = lax.broadcasted_iota(jnp.int32, block.shape, 0); c = lax.broadcasted_iota(jnp.int32, block.shape, 1)
            value = value + jnp.where(r == c, NS_A, 0.0)
        put(sq.poly, rows, cols, value)
    product(sq.gram, sq.gram, sq.blocks, store)

def next_gram(sq):
    product(sq.poly, sq.gram, sq.blocks, lambda r, c, b: put(sq.temp, r, c, b))
    def store(r, c, b):
        sq.full[r, c] = b
        put(sq.gram, r, c, b)
    product(sq.temp, sq.poly, sq.blocks, store)

def next_product(sq):
    product(sq.poly, sq.prod, sq.blocks, lambda r, c, b: put(sq.temp, r, c, b))
    sq.prod[...] = sq.temp[...]

def ortho_kernel(
    periods, counts_ref, factor_ref, mine_ref, other_ref, big_grad, big_mom, small_grad, small_mom,
    big_out, small_out, packed_ref, *refs,
):
    squares = [Square(refs[:5], BLOCKS), Square(refs[5:], BLOCKS)]
    cols = mine_ref.shape[1]
    first = counts_ref[2] == 0
    packed_ref[:, :cols] = jnp.where(first, mine_ref[...], other_ref[...])
    packed_ref[:, cols:] = jnp.where(first, other_ref[...], mine_ref[...])
    scales = []
    for sq, other in zip(squares, (0, big_grad.shape[1] // BLOCKS)):
        size = sq.full.shape[0] // BLOCKS
        r = lax.broadcasted_iota(jnp.int32, (size, size), 0)
        c = lax.broadcasted_iota(jnp.int32, (size, size), 1)
        diag = jnp.zeros((size, size), F32)
        for index, (i, j) in enumerate(PAIRS):
            if i == j:
                diag = diag + jnp.where(r == c, packed_ref[tile_rows(size, other, index)], 0.0)
        trace = jnp.sum(jnp.sum(diag, 0, keepdims=True), 1, keepdims=True)
        scale = 1.0 / (jnp.sqrt(trace) + 1e-07)
        scales.append(scale)
        for index, (i, j) in enumerate(PAIRS):
            tile = packed_ref[tile_rows(size, other, index)] * (scale * scale)
            a, b = slice(i * size, (i + 1) * size), slice(j * size, (j + 1) * size)
            sq.full[a, b] = tile
            put(sq.gram, a, b, tile)
            if i != j:
                sq.full[b, a] = tile.T
                put(sq.gram, b, a, tile.T)
    for sq in squares:
        make_poly(sq)
    for sq in squares:
        sq.prod[...] = sq.poly[...]
        next_gram(sq)
    def step(_, carry):
        for sq in squares: make_poly(sq)
        for sq in squares: next_product(sq)
        for sq in squares: next_gram(sq)
        return carry
    lax.fori_loop(1, NS_STEPS - 1, step, 0)
    for sq in squares: make_poly(sq)
    for sq in squares: next_product(sq)
    slabs = ((big_grad, big_mom, big_out), (small_grad, small_mom, small_out))
    for k, (sq, scale, (grad, mom, out)) in enumerate(zip(squares, scales, slabs)):
        rows = slab_rows(grad[...], mom[...], factor_ref[0], periods[k], counts_ref[k])
        high, rest = split(rows * scale)
        out[...] = (
            dot_nn(high, sq.prod[0]) + (dot_nn(high, sq.prod[1]) + dot_nn(rest, sq.prod[0]))
        ).astype(BF)


def orthogonal(periods, counts, factor, mine, other, slabs):
    def scratch(n):
        return [pltpu.VMEM((n, n), F32)] + [pltpu.VMEM((2, n, n), BF)] * 4

    big, small = slabs[0], slabs[2]
    return pl.pallas_call(
        functools.partial(ortho_kernel, periods),
        in_specs=[pl.BlockSpec(memory_space=pltpu.SMEM)] * 2
        + [pl.BlockSpec(memory_space=pltpu.VMEM)] * 6,
        out_shape=[jax.ShapeDtypeStruct(big.shape, BF), jax.ShapeDtypeStruct(small.shape, BF)],
        scratch_shapes=[pltpu.VMEM((mine.shape[0], 2 * mine.shape[1]), F32)]
        + scratch(big.shape[1])
        + scratch(small.shape[1]),
        compiler_params=pltpu.CompilerParams(vmem_limit_bytes=VMEM_LIMIT),
        cost_estimate=COST,
    )(counts, factor, mine, other, *slabs)


def call(kernel, outs, args, flops, smem=0):
    return pl.pallas_call(
        kernel,
        in_specs=[pl.BlockSpec(memory_space=pltpu.SMEM)] * smem
        + [pl.BlockSpec(memory_space=pltpu.VMEM)] * (len(args) - smem),
        out_specs=[pl.BlockSpec(memory_space=pltpu.VMEM)] * len(outs),
        out_shape=[jax.ShapeDtypeStruct(shape, kind) for shape, kind in outs],
        compiler_params=pltpu.CompilerParams(vmem_limit_bytes=VMEM_LIMIT),
        cost_estimate=COST,
    )(*args)


def vec_at(vec_ref, name):
    offset, extent = vector_layout()[name]
    return vec_ref[:, offset : offset + extent]


def head_masks(value):
    lane = lax.broadcasted_iota(jnp.int32, value.shape, 1) // HD
    return [jnp.where(lane == h, value, jnp.zeros_like(value)) for h in range(value.shape[1] // HD)]


def small_probs(queries, keys, vis):
    scores = dot_nt(queries, keys) * HD**-0.5
    column = lax.broadcasted_iota(jnp.int32, scores.shape, 1)
    scores = jnp.where(column < vis, scores, -jnp.inf)
    exp_scores = jnp.exp(scores - jnp.max(scores, -1, keepdims=True))
    return exp_scores / jnp.sum(exp_scores, -1, keepdims=True)


def enc_attention_kernel(
    vis, clips, start_ref, pos_ref, vec_ref, w_ref, qb_ref, vb_ref, wout_ref,
    stream_ref, hid_ref, qkv_ref, attn_ref, part_ref,
):
    stream = start_ref[...] + vec_at(vec_ref, "emb_b") + pos_ref[...]
    stream_ref[...] = stream
    hid = low(layer_norm(stream, vec_at(vec_ref, "eln1_g"), vec_at(vec_ref, "eln1_b"))[0])
    hid_ref[...] = hid
    qkv_ref[0] = low(dot_nt(hid, w_ref[0]) + qb_ref[...])
    qkv_ref[1] = low(dot_nt(hid, w_ref[1]))
    qkv_ref[2] = low(dot_nt(hid, w_ref[2]) + vb_ref[...])
    rows = stream.shape[0] // clips
    for clip in range(clips):
        at = slice(clip * rows, (clip + 1) * rows)
        keys = qkv_ref[1, at, :]
        mixed = 0.0
        for queries, values in zip(head_masks(qkv_ref[0, at, :]), head_masks(qkv_ref[2, at, :])):
            mixed = mixed + dot_nn(low(small_probs(queries, keys, vis)), values)
        attn_ref[at, :] = low(mixed)
    part_ref[...] = low(dot_nn(attn_ref[...], wout_ref[...]))


def enc_units_kernel(
    stream_ref, total_ref, more_ref, vec_ref, wup_ref, upb_ref, wdown_ref,
    middle_ref, hid_ref, upper_ref, active_ref, part_ref,
):
    middle = stream_ref[...] + (total_ref[...].astype(F32) + more_ref[...].astype(F32)) + vec_at(vec_ref, "eout_b")
    middle_ref[...] = middle
    hid = low(layer_norm(middle, vec_at(vec_ref, "eln2_g"), vec_at(vec_ref, "eln2_b"))[0])
    hid_ref[...] = hid
    upper = dot_nt(hid, wup_ref[...]) + upb_ref[...]
    upper_ref[...] = upper
    active = low(gelu_value(upper))
    active_ref[...] = active
    part_ref[...] = low(dot_nn(active, wdown_ref[...]))


def pick_matrix(own, padded, first, shown_ref):
    row = lax.broadcasted_iota(jnp.int32, (own, padded), 0) + first
    return (row == shown_ref[...]).astype(F32)


def bridge_kernel(
    own, where_ref, middle_ref, total_ref, more_ref, vec_ref, link_ref, w_ref, shown_ref, pos_ref,
    result_ref, dstream_ref, hid_ref, q_ref, kv_ref,
):
    result_ref[...] = middle_ref[...] + (total_ref[...].astype(F32) + more_ref[...].astype(F32)) + vec_at(vec_ref, "edown_b")
    padded = shown_ref.shape[1]
    mine = result_ref[pl.ds(pl.multiple_of(where_ref[0] * padded, padded), padded), :]
    final = low(layer_norm(mine, vec_at(vec_ref, "elnf_g"), vec_at(vec_ref, "elnf_b"))[0])
    latent = dot_nn(final, link_ref[...]) + vec_at(vec_ref, "in_b")
    parts = []
    for _ in range(3):
        parts.append(low(latent))
        latent = latent - parts[-1].astype(F32)
    tile = pos_ref.shape[0] // 7

    def step(t, carry):
        first = pl.multiple_of(t * tile, tile)
        at = pl.ds(first, tile)
        pick = pick_matrix(tile, padded, where_ref[1] * own + first, shown_ref)
        chosen = low(pick)
        value = (dot_nn(chosen, parts[0]) + dot_nn(chosen, parts[1])) + dot_nn(chosen, parts[2])
        hidden = 1.0 - jnp.sum(pick, -1, keepdims=True)
        value = value + hidden * vec_at(vec_ref, "mask") + pos_ref[at, :]
        dstream_ref[at, :] = value
        hid_ref[at, :] = low(
            layer_norm(value, vec_at(vec_ref, "dln1_g"), vec_at(vec_ref, "dln1_b"))[0]
        )
        return carry

    lax.fori_loop(0, 7, step, 0)
    hid = hid_ref[...]
    width = hid.shape[1]
    q_ref[...] = low(dot_nt(hid, w_ref[:width, :]) + vec_at(vec_ref, "dq_b"))
    kv_ref[0] = low(dot_nt(hid, w_ref[width : 2 * width, :]))
    kv_ref[1] = low(dot_nt(hid, w_ref[2 * width :, :]) + vec_at(vec_ref, "dv_b"))


def bridge_back_kernel(
    own, where_ref, gq_ref, gkv_ref, got_ref, hid_ref, w_ref, dstream_ref, mid_ref, vec_ref, shown_ref,
    gw_ref, latent_ref, sums_ref, hgrad_ref,
):
    width = gq_ref.shape[1]
    gk = low(gkv_ref[0].astype(F32) + got_ref[0].astype(F32))
    gv = low(gkv_ref[1].astype(F32) + got_ref[1].astype(F32))
    hid = hid_ref[...]
    hgrad = 0.0
    for k, grad in enumerate((gq_ref[...], gk, gv)):
        at = slice(k * width, (k + 1) * width)
        gw_ref[at, :] = low(dot_tn(grad, hid))
        hgrad = hgrad + dot_nn(grad, w_ref[at, :])
    sums_ref[...] = jnp.zeros_like(sums_ref)
    hgrad_ref[...] = hgrad
    sums_ref[0:1, :] = col_sum(gq_ref[...].astype(F32))
    sums_ref[1:2, :] = col_sum(gv.astype(F32))
    latent_ref[...] = jnp.zeros_like(latent_ref)
    padded = shown_ref.shape[1]
    tile = own // 7
    gain = vec_at(vec_ref, "dln1_g")

    def step(t, carry):
        first = pl.multiple_of(t * tile, tile)
        at = pl.ds(first, tile)
        saved = layer_norm(dstream_ref[at, :], gain, gain)[1]
        sgrad, gain_grad, bias_grad = norm_back(hgrad_ref[at, :], saved, gain)
        din = sgrad + mid_ref[at, :]
        pick = pick_matrix(tile, padded, where_ref[1] * own + first, shown_ref)
        hidden = 1.0 - jnp.sum(pick, -1, keepdims=True)
        sums_ref[2:3, :] += gain_grad
        sums_ref[3:4, :] += bias_grad
        sums_ref[4:5, :] += col_sum(hidden * din)
        chosen = low(pick)
        high = low(din)
        rest = low(din - high.astype(F32))
        latent_ref[...] += dot_tn(chosen, high) + dot_tn(chosen, rest)
        return carry

    lax.fori_loop(0, 7, step, 0)


def enc_units_back_kernel(
    latent_ref, result_ref, vec_ref, link_ref, wdown_ref, wup_ref, upper_ref, active_ref, hid_ref,
    glink_ref, grad_ref, gdown_ref, gup_ref, part_ref, sums_ref,
):
    sums_ref[...] = jnp.zeros_like(sums_ref)
    latent = latent_ref[...]
    gain = vec_at(vec_ref, "elnf_g")
    final, saved = layer_norm(result_ref[...], gain, vec_at(vec_ref, "elnf_b"))
    glink_ref[...] = low(dot_tn(low(final), latent))
    grad, gain_grad, bias_grad = norm_back(dot_nt(latent, link_ref[...]), saved, gain)
    grad_ref[...] = grad
    sums_ref[0:1, : latent.shape[1]] = col_sum(latent.astype(F32))
    sums_ref[1:2, :] = gain_grad
    sums_ref[2:3, :] = bias_grad
    sums_ref[3:4, :] = col_sum(grad)
    down = low(grad)
    gdown_ref[...] = low(dot_tn(active_ref[...], down))
    upper = low(dot_nt(down, wdown_ref[...]) * gelu_slope(upper_ref[...]))
    sums_ref[4:5, :] = col_sum(upper.astype(F32))
    part_ref[...] = low(dot_nn(upper, wup_ref[...]))
    gup_ref[...] = low(dot_tn(upper, hid_ref[...]))


def enc_attention_back_kernel(
    vis, clips, total_ref, more_ref, grad_ref, middle_ref, vec_ref, attn_ref, wout_ref, qkv_ref, w_ref, hid_ref,
    mid_ref, gout_ref, gqkv_ref, part_ref, sums_ref, dqkv_ref,
):
    sums_ref[...] = jnp.zeros_like(sums_ref)
    gain = vec_at(vec_ref, "eln2_g")
    saved = layer_norm(middle_ref[...], gain, gain)[1]
    mid, gain_grad, bias_grad = norm_back((total_ref[...].astype(F32) + more_ref[...].astype(F32)), saved, gain)
    mid = mid + grad_ref[...]
    mid_ref[...] = mid
    sums_ref[0:1, :] = gain_grad
    sums_ref[1:2, :] = bias_grad
    sums_ref[2:3, :] = col_sum(mid)
    out = low(mid)
    gout_ref[...] = low(dot_tn(attn_ref[...], out))
    attn_grad = low(dot_nt(out, wout_ref[...]))
    rows = mid.shape[0] // clips
    for clip in range(clips):
        at = slice(clip * rows, (clip + 1) * rows)
        queries, keys, values = (head_masks(qkv_ref[k, at, :]) for k in range(3))
        all_keys, all_values = qkv_ref[1, at, :], qkv_ref[2, at, :]
        grads = head_masks(attn_grad[at, :])
        dq = dk = dv = 0.0
        for query, key, grad in zip(queries, keys, grads):
            prob = small_probs(query, all_keys, vis)
            dprob = dot_nt(grad, all_values)
            product = prob * dprob
            dscore = low(product - prob * jnp.sum(product, -1, keepdims=True))
            dv = dv + dot_tn(low(prob), grad)
            dq = dq + dot_nn(dscore, key)
            dk = dk + dot_tn(dscore, query)
        dqkv_ref[0, at, :] = low(dq * HD**-0.5)
        dqkv_ref[1, at, :] = low(dk * HD**-0.5)
        dqkv_ref[2, at, :] = low(dv)
    width = attn_ref.shape[1]
    sums_ref[3:4, :width] = col_sum(dqkv_ref[0].astype(F32))
    sums_ref[4:5, :width] = col_sum(dqkv_ref[2].astype(F32))
    part = 0.0
    for k in range(3):
        part = part + dot_nn(dqkv_ref[k], w_ref[k])
        gqkv_ref[k] = low(dot_tn(dqkv_ref[k], hid_ref[...]))
    part_ref[...] = low(part)


def enc_start_back_kernel(total_ref, more_ref, mid_ref, stream_ref, vec_ref, pix_ref, gembed_ref, sums_ref):
    sums_ref[...] = jnp.zeros_like(sums_ref)
    gain = vec_at(vec_ref, "eln1_g")
    saved = layer_norm(stream_ref[...], gain, gain)[1]
    grad, gain_grad, bias_grad = norm_back((total_ref[...].astype(F32) + more_ref[...].astype(F32)), saved, gain)
    grad = grad + mid_ref[...]
    sums_ref[0:1, :] = gain_grad
    sums_ref[1:2, :] = bias_grad
    sums_ref[2:3, :] = col_sum(grad)
    gembed_ref[...] = low(dot_tn(pix_ref[...], low(grad)))


def group_total(keep, send):
    mine = keep + narrow_flip(send, 1)
    rows = mine.shape[0] // 2
    one, two = mine[:rows], mine[rows:]
    bits = []
    bit = 1
    while bit < wide_digits(lax.axis_size(WD))[-1][0]:
        bits.append(bit)
        bit *= 2
    for bit in bits:
        one = one + wide_flip(one, bit)
    two = two + narrow_flip(two, 2)
    one = one + narrow_flip(one, 2)
    for bit in bits:
        two = two + wide_flip(two, bit)
    mine = jnp.concatenate([one, two], 0)
    return mine, narrow_flip(mine, 1)


def adam_update(weight, first, second, gradient, rate, decay):
    first_new = BETA_ONE * first + (1.0 - BETA_ONE) * gradient
    second_new = BETA_TWO * second + (1.0 - BETA_TWO) * gradient * gradient
    direction = (
        first_new
        / (1.0 - BETA_ONE**STEP)
        / (jnp.sqrt(second_new / (1.0 - BETA_TWO**STEP)) + EPS_ADAM)
    )
    return (first_new, second_new, weight - rate * (direction + decay * weight))


def pad_rows(value, rows, axis):
    if value.shape[axis] == rows:
        return value
    widths = [(0, 0)] * value.ndim
    widths[axis] = (0, rows - value.shape[axis])
    return jnp.pad(value, widths)


def per_device(
    pixels,
    visible,
    masked,
    groups,
    enc_qkv,
    enc_qkv_mom,
    enc_out,
    enc_out_mom,
    enc_up,
    enc_up_mom,
    enc_down,
    enc_down_mom,
    dec_qkv,
    dec_qkv_mom,
    dec_out,
    dec_out_mom,
    dec_up,
    dec_up_mom,
    dec_down,
    dec_down_mom,
    embed,
    embed_m,
    embed_v,
    enc_to_dec,
    enc_to_dec_m,
    enc_to_dec_v,
    head,
    head_m,
    head_v,
    vectors,
    vectors_m,
    vectors_v,
):
    wide = lax.axis_size(WD)
    me = lax.axis_index(NR)
    half, clip = me % 2, me // 2
    slow = wide_digits(wide)[-1]
    fast = slow[0]
    plane = place_in(slow)
    clips, vis = visible.shape
    tubs = pixels.shape[1]
    own = tubs // 2

    n_up = enc_up.shape[1]
    n_q = enc_qkv.shape[2]
    n_out = enc_out.shape[0]
    n_emb = embed.shape[0] // QN
    n_link = enc_to_dec.shape[0] * DD // D // QN
    m_up = dec_up.shape[1]
    m_qkv = dec_qkv.shape[1]
    m_out = dec_out.shape[0]
    m_head = head.shape[0] * (PIX // DD)

    up_rows, down_rows = enc_up.T, enc_down
    qkv_rows = jnp.swapaxes(enc_qkv, 1, 2).reshape(3 * n_q, D)
    dqkv_rows, dup_rows = dec_qkv.T, dec_up.T
    head_rows = head.reshape(m_head, DD)
    emb_cols = lax.dynamic_slice_in_dim(embed, me * (D // QN), D // QN, 1)
    m_link = enc_to_dec.shape[0] // QN
    link_rows = lax.dynamic_slice_in_dim(enc_to_dec, me * m_link, m_link, 0)
    pack_b = jnp.concatenate([low(emb_cols).reshape(n_emb, D), low(qkv_rows), low(enc_out)], 0)
    pack_c = low(jnp.concatenate([up_rows, down_rows], 0))
    pack_d = low(
        jnp.concatenate([dup_rows, dqkv_rows, dec_out, dec_down, head_rows, link_rows], 0)
    )
    pack_d = narrow_pair(pack_d, 2)
    line_b = slow_pieces(pack_b)
    pieces_b = all_pieces(line_b)
    came = tuple(line_b.values())
    pack_c, pack_d, vis_now, _ = lax.optimization_barrier((pack_c, pack_d, visible, came))
    line_c = slow_pieces(pack_c)
    full_b = assemble(pieces_b)
    pieces_c = all_pieces(tied(line_c, full_b))
    full_c = assemble(pieces_c)
    line_d = slow_pieces(after(pack_d, tuple(pieces_c.values())))
    embed_w = full_b[:, :n_emb].reshape(PIX, D // QN)
    w_qkv = full_b[:, n_emb : n_emb + 3 * n_q].reshape(wide, 3, n_q, D)
    w_qkv = jnp.swapaxes(w_qkv, 0, 1).reshape(3, wide * n_q, D)
    w_out = full_b[:, n_emb + 3 * n_q :].reshape(wide * n_out, D)
    w_up = full_c[:, :n_up].reshape(wide * n_up, D)
    w_down = full_c[:, n_up:].reshape(wide * n_up, D)
    table = vector_layout()

    def vec_of(name):
        offset, extent = table[name]
        return vectors[offset : offset + extent]

    def share_of(name):
        offset, extent = table[name]
        share = extent // QN
        return lax.dynamic_slice_in_dim(vectors, offset + me * share, share)[None, :]

    grads = {}

    padded = -(-vis // 16) * 16
    rows = clips * padded
    shown = jnp.pad(visible, ((0, 0), (0, padded - vis)), constant_values=-1)
    vis_rows = shown.reshape(rows)
    tube_ids = jnp.arange(tubs, dtype=jnp.int32)
    vis_pix = mm(low(vis_rows[:, None] == tube_ids[None, :]), pixels[0]).astype(BF)
    vec_row = vectors[None, :]
    now_rows = jnp.pad(vis_now, ((0, 0), (0, padded - vis)), constant_values=-1).reshape(rows)
    vis_table = sinusoid(now_rows, D)
    start = mm(vis_pix, embed_w)
    start = both(start, narrow_flip(start, 2), clip, 1)
    start = both(start, narrow_flip(start, 1), half, 2).reshape(rows, D)
    units = D // QN * 4
    stream, hid1, eqkv, eattn, part = call(
        functools.partial(enc_attention_kernel, vis, clips),
        [((rows, D), F32), ((rows, D), BF), ((3, rows, D // QN), BF), ((rows, D // QN), BF), ((rows, D), BF)],
        [start, vis_table, vec_row, w_qkv, share_of("eq_b"), share_of("ev_b"), w_out],
        2 * rows * D * D,
    )
    own_pix = after(lax.dynamic_slice_in_dim(pixels[0], half * own, own, 0), part)
    targets = group_targets(own_pix, groups)
    own_pos = after(half * own + jnp.arange(own, dtype=jnp.int32), part)
    own_table = sinusoid(own_pos, DD)
    parts = narrow_parts(part)
    pieces_d = all_pieces(tied(line_d, parts[1]))
    middle, hid2, upper, active, part = call(
        enc_units_kernel,
        [((rows, D), F32), ((rows, D), BF), ((rows, units), F32), ((rows, units), BF), ((rows, D), BF)],
        [stream, *parts, vec_row, w_up, share_of("eup_b"), w_down],
        4 * rows * D * units,
    )

    parts = narrow_parts(part)
    full_d = narrow_pair(assemble(tied(pieces_d, parts[1])), 1, 2)
    at, taken = 0, []
    for extent in (m_up, m_qkv, m_out, m_up, m_head, m_link):
        taken.append(full_d[:, :, :, at : at + extent].reshape(wide * QN * extent, DD))
        at += extent
    d_up, d_qkv, d_out, d_down, d_head, link_w = taken
    d_head = d_head.reshape(DD, PIX)

    where = jnp.stack([clip, half])
    clip_shown = lax.dynamic_slice_in_dim(shown, clip, 1, 0)
    enc_result, dstream, dh1, dq, dkv = call(
        functools.partial(bridge_kernel, own),
        [((rows, D), F32), ((own, DD), F32), ((own, DD), BF), ((own, DD), BF), ((2, own, DD), BF)],
        [where, middle, *parts, vec_row, link_w, d_qkv, clip_shown, own_table],
        6 * own * DD * DD,
        1,
    )
    pick = own_pos[:, None] == clip_shown
    hidden_row = 1.0 - jnp.sum(pick.astype(F32), -1, keepdims=True)
    all_kv = both(dkv, narrow_flip(dkv, 1), half, 1).reshape(2, tubs, DD)
    def plane_rows(parts):
        return jnp.stack([pad_rows(low(part), parts[0].shape[0], 0) for part in parts], 0)

    late = lax.optimization_barrier(
        (
            (enc_up_mom, enc_qkv_mom, enc_out_mom, enc_down_mom),
            (dec_up_mom, dec_qkv_mom, dec_out_mom, dec_down_mom),
            all_kv,
        )
    )
    (up_mom, qkv_mom, out_mom, down_mom), (dup_mom, dqkv_mom, dout_mom, ddown_mom), all_kv = late
    qkv_mom = jnp.swapaxes(qkv_mom, 1, 2).reshape(3 * n_q, D)
    enc_mom, dec_mom = joined_exchange(
        plane_rows([up_mom.T, qkv_mom, out_mom, down_mom]),
        plane_rows([dup_mom.T, dqkv_mom.T, dout_mom, ddown_mom]),
        slow,
    )

    tile = next(t for t in (784, 224, 112, 16) if tubs % t == 0)
    dattn, mixed, dlog = attention_fwd(dq, all_kv, tile)
    dattn, enc_mom, dec_mom = lax.optimization_barrier((dattn, enc_mom, dec_mom))

    dmiddle = dstream + mm(dattn, d_out) + vec_of("dout_b")
    dh2, dsaved2 = layer_norm(dmiddle, vec_of("dln2_g"), vec_of("dln2_b"))
    dh2 = low(dh2)
    dupper = mm_nt(dh2, d_up) + vec_of("dup_b")
    dactive = low(gelu_value(dupper))
    dresult = dmiddle + mm(dactive, d_down) + vec_of("ddown_b")
    hf, hsaved = layer_norm(dresult, vec_of("dlnf_g"), vec_of("dlnf_b"))
    hf = low(hf)
    predicted = mm(hf, d_head) + vec_of("head_b")
    error = (predicted - targets) * hidden_row
    loss_part = jnp.sum(error * error)
    pred_grad = error * (2.0 / (clips * wide * (tubs - vis) * PIX))

    pred_low = low(pred_grad)
    g_head = mm_tn(hf, pred_low)
    grads["head_b"] = col_sum(pred_grad)
    dgrad, grads["dlnf_g"], grads["dlnf_b"] = norm_back(
        mm_nt(pred_low, d_head), hsaved, vec_of("dlnf_g")
    )
    down_low = low(dgrad)
    g_ddown = mm_tn(dactive, down_low)
    grads["ddown_b"] = col_sum(dgrad)
    upper_low = low(mm_nt(down_low, d_down) * gelu_slope(dupper))
    g_dup = mm_tn(upper_low, dh2)
    grads["dup_b"] = col_sum(upper_low.astype(F32))
    mid_grad, grads["dln2_g"], grads["dln2_b"] = norm_back(
        mm(upper_low, d_up), dsaved2, vec_of("dln2_g")
    )
    mid_grad = mid_grad + dgrad
    out_low = low(mid_grad)
    g_dout = mm_tn(dattn, out_low)
    grads["dout_b"] = col_sum(mid_grad)
    attn_grad = low(mm_nt(out_low, d_out))
    def dec_parts(value, extent):
        return low(value).reshape(4, fast, 2, 2, extent, DD)

    def fast_scatter(value, axis):
        digits = wide_digits(wide)[:-1]
        shape = value.shape
        value = value.reshape(
            shape[:axis] + tuple(radix for _, radix in digits[::-1]) + shape[axis + 1 :]
        )
        for count, digit in enumerate(digits):
            value = line_scatter(value, digit, axis + len(digits) - 1 - count)
        return value

    def half_sum(value, place, axis, bit):
        sent = low(pick_half(value, 1 - place, axis))
        return pick_half(value, place, axis).astype(F32) + narrow_flip(sent, bit).astype(F32)

    cut = m_up - m_qkv
    p_head = dec_parts(g_head.reshape(-1, DD), m_head)
    early = jnp.stack(
        [
            dec_parts(g_dup, m_up),
            jnp.concatenate([dec_parts(g_dout, m_out), p_head[:, :, :, :, cut:]], 4),
            dec_parts(g_ddown, m_up),
        ],
        0,
    )
    early = half_sum(early, half, 4, 1)
    attn_grad, early = lax.optimization_barrier((attn_grad, early))
    early = half_sum(early, clip, 3, 2)
    gq, gkv = attention_bwd(dq, all_kv, attn_grad, mixed, dlog, tile)
    gkv, early = lax.optimization_barrier((gkv, early))
    gkv = gkv.reshape(2, 2, own, DD)
    got = narrow_flip(pick_half(gkv, 1 - half, 1), 1)
    g_dqkv, latent_part, sums, _ = call(
        functools.partial(bridge_back_kernel, own),
        [((3 * DD, DD), BF), ((padded, DD), F32), ((8, DD), F32), ((own, DD), F32)],
        [where, gq, pick_half(gkv, half, 1), got, dh1, d_qkv, dstream, mid_grad, vec_row, clip_shown],
        12 * own * DD * DD,
        1,
    )
    for row, name in enumerate(("dq_b", "dv_b", "dln1_g", "dln1_b", "mask")):
        grads[name] = sums[row]

    late = jnp.concatenate([dec_parts(g_dqkv, m_qkv), p_head[:, :, :, :, :cut]], 4)[None]
    early = fast_scatter(after(early, latent_part), 2)

    latent_pair = low(pair_sum(latent_part))
    latent_low = both(latent_pair, narrow_flip(latent_pair, 2), clip, 0).reshape(rows, DD)
    g_link, egrad, g_down, g_up, part, sums = call(
        enc_units_back_kernel,
        [((D, DD), BF), ((rows, D), F32), ((units, D), BF), ((units, D), BF), ((rows, D), BF), ((8, D), F32)],
        [latent_low, enc_result, vec_row, link_w, w_down, w_up, upper, active, hid2],
        8 * rows * D * units,
    )
    parts = narrow_parts(part)
    g_link, sums, _ = lax.optimization_barrier((g_link, sums, parts[1]))
    grads["in_b"] = sums[0, :DD]
    for row, name in enumerate(("elnf_g", "elnf_b", "edown_b", "eup_b")):
        grads[name] = sums[row + 1]

    def enc_parts(value, extent):
        return low(value).reshape(4, fast, extent, D).transpose(1, 0, 2, 3)

    g_up, g_down, late, _ = lax.optimization_barrier((g_up, g_down, late, parts[0]))
    late = half_sum(late, half, 4, 1)
    sum_up = fast_scatter(enc_parts(g_up, n_up), 0)
    sum_down = fast_scatter(enc_parts(g_down, n_up), 0)
    mid_grad, g_out, g_qkv, part, sums, _ = call(
        functools.partial(enc_attention_back_kernel, vis, clips),
        [((rows, D), F32), ((D // QN, D), BF), ((3, D // QN, D), BF), ((rows, D), BF), ((8, D), F32), ((3, rows, D // QN), BF)],
        [*parts, egrad, middle, vec_row, eattn, w_out, eqkv, w_qkv, hid1],
        4 * rows * D * D,
    )
    for row, name in enumerate(("eln2_g", "eln2_b", "eout_b")):
        grads[name] = sums[row]
    grads["eq_b"], grads["ev_b"] = sums[3, : D // QN], sums[4, : D // QN]
    parts = narrow_parts(part)
    ends_sum = ends_total(joined(sum_up, early[0]), joined(sum_down, early[2]), slow, (0, 3))
    g_embed, sums = call(
        enc_start_back_kernel,
        [((PIX, D), BF), ((8, D), F32)],
        [*parts, mid_grad, stream, vec_row, vis_pix],
        2 * rows * D * PIX,
    )
    for row, name in enumerate(("eln1_g", "eln1_b", "emb_b")):
        grads[name] = sums[row]
    g_embed = pick_half(g_embed.reshape(wide, QN, n_emb, D), me, 1)
    g_link = pick_half(g_link.reshape(wide, QN, n_link, D), me, 1)
    part_qkv = jnp.concatenate([enc_parts(g, n_q) for g in g_qkv], 2)
    part_rest = jnp.concatenate(
        [enc_parts(g_out, n_out), enc_parts(g_embed, n_emb), enc_parts(g_link, n_link)], 2
    )
    longer = max(part_qkv.shape[2], part_rest.shape[2])
    sum_qkv = fast_scatter(pad_rows(part_qkv, longer, 2), 0)
    sum_rest = fast_scatter(pad_rows(part_rest, longer, 2), 0)
    late = fast_scatter(half_sum(after(late, parts[1]), clip, 3, 2), 2)
    middle_sum = ends_total(joined(sum_qkv, late[0]), joined(sum_rest, early[1]), slow, (1, 2))
    enc_ends, dec_ends = parted(ends_sum, n_up)
    enc_middle, dec_middle = parted(middle_sum, longer)
    middle = (plane == 1) | (plane == 2)
    enc_sum = jnp.where(middle, pad_rows(enc_middle, n_up, 1), enc_ends)
    dec_sum = jnp.where(middle, dec_middle, dec_ends)

    leading = jnp.where(me == 0, 1.0, 0.0)

    def spread(share):
        full = jnp.zeros((share.shape[0] * QN,), F32)
        return lax.dynamic_update_slice_in_dim(full, share, me * share.shape[0], 0)

    pieces = []
    for name in table:
        piece = grads[name].reshape(-1)
        if name in ("eq_b", "ev_b", "eup_b"):
            piece = spread(piece)
        elif name[0] == "e" or name == "in_b":
            piece = leading * piece
        pieces.append(piece)
    vec_total = sum_all(jnp.concatenate(pieces + [loss_part[None]]).reshape(1, -1))[0]
    loss_sum = vec_total[-1]
    vec_total = vec_total[:-1]
    squares = jnp.sum(dec_sum * dec_sum) + jnp.sum(enc_sum * enc_sum)
    square_total = sum_tiny(jnp.broadcast_to(squares, (8, 128)))[0, 0]
    grad_norm = jnp.sqrt(square_total + jnp.sum(vec_total * vec_total))
    factor = jnp.minimum(1.0, CLIP_AT / grad_norm)

    counts = jnp.asarray(
        [[n_up, m_up], [3 * n_q, m_qkv], [n_out, m_out], [n_up, m_up]], jnp.int32
    )[plane]
    counts = jnp.concatenate([counts, half[None]])
    slabs = [
        enc_sum.reshape(4 * n_up, D),
        enc_mom.reshape(4 * n_up, D),
        dec_sum.reshape(4 * m_up, DD),
        dec_mom.reshape(4 * m_up, DD),
    ]
    periods = (n_up, m_up)
    mine, other = group_total(*packed_gram(periods, counts, factor[None], slabs))
    enc_back, dec_back, _ = lax.optimization_barrier((enc_sum, dec_sum, grad_norm))
    enc_grad, dec_grad = joined_exchange(low(enc_back), low(dec_back), slow)
    enc_grad, dec_grad = enc_grad.astype(F32) * factor, dec_grad.astype(F32) * factor

    def turned(value):
        return value.T

    def same(value):
        return value

    def unqkv(value):
        return jnp.swapaxes(value.reshape(3, n_q, D), 1, 2)

    rest = enc_grad[2, n_out : n_out + n_emb + n_link]
    rest = narrow_gather(rest)
    embed_grad = rest[:, :n_emb].reshape(embed.shape)
    link_grad = rest[:, n_emb:].reshape(enc_to_dec.shape)
    head_grad = jnp.concatenate([dec_grad[1, m_qkv:], dec_grad[2, m_out:]], 0).reshape(head.shape)
    adam = []
    for weight, first, second, grad, rate, decay in [
        (embed, embed_m, embed_v, embed_grad, RATE_ADAM, DECAY),
        (enc_to_dec, enc_to_dec_m, enc_to_dec_v, link_grad, RATE_ADAM, DECAY),
        (head, head_m, head_v, head_grad, RATE_ADAM, DECAY),
        (vectors, vectors_m, vectors_v, factor * vec_total, RATE_VECTOR, 0.0),
    ]:
        adam += adam_update(weight, first, second, grad, rate, decay)
    entries = [
        (enc_qkv, enc_qkv_mom, enc_grad[1, : 3 * n_q], unqkv, 3 * D),
        (enc_out, enc_out_mom, enc_grad[2, :n_out], same, D),
        (enc_up, enc_up_mom, enc_grad[0], turned, FE),
        (enc_down, enc_down_mom, enc_grad[3], same, FE),
        (dec_qkv, dec_qkv_mom, dec_grad[1, :m_qkv], turned, 3 * DD),
        (dec_out, dec_out_mom, dec_grad[2, :m_out], same, DD),
        (dec_up, dec_up_mom, dec_grad[0], turned, FD),
        (dec_down, dec_down_mom, dec_grad[3], same, FD),
    ]
    moms = [MOMENTUM * mom + side(grad) for _, mom, grad, side, _ in entries]
    mine, moms, adam = lax.optimization_barrier((mine, moms, adam))
    enc_ortho, dec_ortho = orthogonal(periods, counts, factor[None], mine, other, slabs)
    enc_ortho, dec_ortho = joined_exchange(
        enc_ortho.reshape(4, n_up, D), dec_ortho.reshape(4, m_up, DD), slow
    )
    enc_ortho, dec_ortho = enc_ortho.astype(F32), dec_ortho.astype(F32)
    results = [loss_sum, grad_norm]
    orthos = [
        enc_ortho[1, : 3 * n_q],
        enc_ortho[2, :n_out],
        enc_ortho[0],
        enc_ortho[3],
        dec_ortho[1, :m_qkv],
        dec_ortho[2, :m_out],
        dec_ortho[0],
        dec_ortho[3],
    ]
    for (weight, _, _, side, largest), mom, part in zip(entries, moms, orthos):
        step = RATE_MUON * 0.2 * math.sqrt(largest)
        results += [weight * (1.0 - RATE_MUON * DECAY) - step * side(part), mom]
    results += adam
    return tuple(results)


def solution(mesh):
    enc, dec = (NR, WD), (WD, NR)
    muon = [P(None, None, enc), P(enc, None), P(None, enc), P(enc, None)]
    muon += [P(None, dec), P(dec, None), P(None, dec), P(dec, None)]
    pairs = [spec for spec in muon for _ in range(2)]
    adam = [P(WD, None)] * 6 + [P(dec, None)] * 3 + [P()] * 3
    in_specs = [P(WD, None, None), P(WD, None), P(WD, None), P()] + pairs + adam
    out_specs = [P(), P()] + pairs + adam
    return jax.shard_map(
        per_device,
        mesh=mesh,
        in_specs=tuple(in_specs),
        out_specs=tuple(out_specs),
        check_vma=False,
    )
```
